128 devices in a mesh: dp: 8 (over x, core), tensor: 16 (over z, y).
Axes of the slice: x: 4, y: 4, z: 4, core: 2. Of those that a mesh axis runs over, the one named last changes fastest.
Arguments:
- block_input: bfloat16 [16384, 2048], P(('dp', 'tensor')), may hold values from -6 to 6
- out_grad: bfloat16 [16384, 2048], P(('dp', 'tensor')), may hold values from -6 to 6
- segments: int32 [8, 2048], P('dp'), may hold values from 0 to 7, never falling along the last dimension, each value on 1 to 1024 neighbouring positions
- w_query: float32 [2048, 2048], P('dp', 'tensor'), may hold values from -0.125 to 0.125
- keyvalue_weights: float32 [2, 2048, 256], P(None, ('dp', 'tensor')), may hold values from -0.125 to 0.125
- w_output: float32 [2048, 2048], P('tensor', 'dp'), may hold values from -1 to 1
- w_gateup: float32 [2, 2048, 5632], P(None, 'dp', 'tensor'), may hold values from -0.125 to 0.125
- w_down: float32 [5632, 2048], P('tensor', 'dp'), may hold values from -0.078125 to 0.078125
- norm_gains: float32 [2, 2048], P(None, ('dp', 'tensor')), may hold values from 0.5 to 1.5
- query_first: float32 [2048, 2048], P('dp', 'tensor'), may hold values from -256 to 256
- keyval_moment_one: float32 [2, 2048, 256], P(None, ('dp', 'tensor')), may hold values from -256 to 256
- output_first: float32 [2048, 2048], P('tensor', 'dp'), may hold values from -12 to 12
- gateup_first: float32 [2, 2048, 5632], P(None, 'dp', 'tensor'), may hold values from -32 to 32
- down_first: float32 [5632, 2048], P('tensor', 'dp'), may hold values from -48 to 48
- gains_first: float32 [2, 2048], P(None, ('dp', 'tensor')), may hold values from -80 to 80
- query_second: float32 [2048, 2048], P('dp', 'tensor'), may hold values from 7372.8 to 58982.4
- keyval_moment_two: float32 [2, 2048, 256], P(None, ('dp', 'tensor')), may hold values from 7372.8 to 58982.4
- output_second: float32 [2048, 2048], P('tensor', 'dp'), may hold values from 18.0224 to 147.456
- gateup_second: float32 [2, 2048, 5632], P(None, 'dp', 'tensor'), may hold values from 98.304 to 802.816
- down_second: float32 [5632, 2048], P('tensor', 'dp'), may hold values from 294.912 to 2359.296
- gains_second: float32 [2, 2048], P(None, ('dp', 'tensor')), may hold values from 819.2 to 6553.6
Outputs:
- block_output: bfloat16 [16384, 2048], P(('dp', 'tensor'))
- input_grad: bfloat16 [16384, 2048], P(('dp', 'tensor'))
- new_query: float32 [2048, 2048], P('dp', 'tensor')
- new_keyval: float32 [2, 2048, 256], P(None, ('dp', 'tensor'))
- new_output: float32 [2048, 2048], P('tensor', 'dp')
- new_gateup: float32 [2, 2048, 5632], P(None, 'dp', 'tensor')
- new_down: float32 [5632, 2048], P('tensor', 'dp')
- new_gains: float32 [2, 2048], P(None, ('dp', 'tensor'))
- query_mean: float32 [2048, 2048], P('dp', 'tensor')
- keyval_mean: float32 [2, 2048, 256], P(None, ('dp', 'tensor'))
- output_mean: float32 [2048, 2048], P('tensor', 'dp')
- gateup_mean: float32 [2, 2048, 5632], P(None, 'dp', 'tensor')
- down_mean: float32 [5632, 2048], P('tensor', 'dp')
- gains_mean: float32 [2, 2048], P(None, ('dp', 'tensor'))
- query_square: float32 [2048, 2048], P('dp', 'tensor')
- keyval_square: float32 [2, 2048, 256], P(None, ('dp', 'tensor'))
- output_square: float32 [2048, 2048], P('tensor', 'dp')
- gateup_square: float32 [2, 2048, 5632], P(None, 'dp', 'tensor')
- down_square: float32 [5632, 2048], P('tensor', 'dp')
- gains_square: float32 [2, 2048], P(None, ('dp', 'tensor'))
The draws below stay inside these ranges and needn't reach their ends.
Inputs may be any that keep to these rules, and one draw needn't show every extreme that they name: `segments`: in each sequence the document numbers never fall, every one of the 8 documents has 1 to 1024 tokens and one has exactly 1024.
All inputs are finite; a program needn't handle non-finite values.
Results may differ from the reference program's by a relative error of at most 0.035.
Values may be sent and summed in bfloat16 or wider, within the bound.
No kernel may reach another device: no remote copies, remote signals or barrier semaphores. Data moves between devices by JAX's collectives and lax.ppermute only.
A program may use at most 192 MiB of HBM per device.

```python
import math
import jax
import jax.numpy as jnp
import numpy as np
from jax import lax

MODEL_WIDTH = 2048
QUERY_HEADS = 32
KEYVALUE_HEADS = 4
HEAD_SIZE = 64
FF = 5632
STEP = 10
LEN = 2048
SEQS = 8
TOKEN_TOTAL = 16384
SUMMED_HEADS = 2
DOCS = 8


def shard_levels(key, dims, cuts, low, top_value):
    loudness, own = 1.0, jax.random.fold_in(key, 6)
    for position, parts in cuts:
        draws = jnp.exp(jax.random.uniform(jax.random.fold_in(own, position), (parts,), jnp.float32, low / len(cuts), top_value / len(cuts)))
        loudness = loudness * jnp.repeat(draws, dims[position] // parts).reshape([-1 if axis == position else 1 for axis in range(len(dims))])
    return loudness


def profile(count, total, most, lean):
    loads = [(1 << 20) // math.isqrt(grade ** lean) + 1 for grade in range(2, count + 1)]
    spare, given = total - most - (count - 1), [1] * (count - 1)
    while spare > 0:
        free = [i for i in range(count - 1) if given[i] < most]
        whole, left = sum([loads[i] for i in free]), spare
        for i in free:
            extra = min(most - given[i], max(1, left * loads[i] // whole), spare)
            given[i] = given[i] + extra
            spare = spare - extra
    return np.array([most] + given)


def ragged(own_key, number_of, total, bound, lean):
    if number_of == 2:
        one = jax.random.randint(own_key, (), max(1, total - bound), min(bound, total - 1) + 1)
        return jnp.stack([one, total - one])
    lengths = jnp.asarray(profile(number_of, total, bound, lean), jnp.int32)
    twos = (number_of - 1) // 2
    source_of, receiver = lengths[1:1 + 2 * twos:2], lengths[2:2 + 2 * twos:2]
    slack = jnp.minimum(source_of - 1, bound - receiver)
    passed = jax.random.randint(jax.random.fold_in(own_key, 1), (twos,), 0, 1 << 20) % (slack + 1)
    lengths = lengths.at[1:1 + 2 * twos:2].set(source_of - passed).at[2:2 + 2 * twos:2].set(receiver + passed)
    return lengths[jax.random.permutation(jax.random.fold_in(own_key, 2), number_of)]


def bell_draw(stream_key, shape, scale, reach, split=(), kind=jnp.bfloat16):
    level = shard_levels(stream_key, shape, split, -0.22, 0.18) if split else 1.0
    values = jax.random.normal(stream_key, shape, jnp.float32) * scale * level
    return jnp.minimum(jnp.maximum(values, -reach), reach).astype(kind)


def setup_inputs(seed: int = 0) -> dict:
    arg_keys = jax.random.split(jax.random.key(seed), 22)
    return {
        "block_input": bell_draw(arg_keys[0], (TOKEN_TOTAL, MODEL_WIDTH), 1.0, 6.0, ((0, 128),)),
        "out_grad": bell_draw(arg_keys[1], (TOKEN_TOTAL, MODEL_WIDTH), 1.0, 6.0, ((0, 128),)),
        "segments": jax.vmap(lambda own: jnp.searchsorted(jnp.cumsum(ragged(own, DOCS, LEN, LEN // 2, 2)), jnp.arange(LEN), side="right"))(jax.random.split(arg_keys[2], SEQS)).reshape((SEQS, LEN)).astype(jnp.int32),
        "w_query": bell_draw(arg_keys[3], (MODEL_WIDTH, QUERY_HEADS * HEAD_SIZE), MODEL_WIDTH ** -0.5, 0.125, ((0, 8), (1, 16)), jnp.float32),
        "keyvalue_weights": bell_draw(arg_keys[4], (2, MODEL_WIDTH, KEYVALUE_HEADS * HEAD_SIZE), MODEL_WIDTH ** -0.5, 0.125, ((1, 128),), jnp.float32),
        "w_output": bell_draw(arg_keys[5], (QUERY_HEADS * HEAD_SIZE, MODEL_WIDTH), (MODEL_WIDTH // 64) ** -0.5, 1.0, ((0, 16), (1, 8)), jnp.float32),
        "w_gateup": bell_draw(arg_keys[6], (2, MODEL_WIDTH, FF), MODEL_WIDTH ** -0.5, 0.125, ((1, 8), (2, 16)), jnp.float32),
        "w_down": bell_draw(arg_keys[7], (FF, MODEL_WIDTH), FF ** -0.5, 0.078125, ((0, 16), (1, 8)), jnp.float32),
        "norm_gains": jnp.clip(1.0 + 0.1 * jax.random.normal(arg_keys[8], (2, MODEL_WIDTH), jnp.float32), 0.5, 1.5),
        "query_first": bell_draw(arg_keys[9], (MODEL_WIDTH, QUERY_HEADS * HEAD_SIZE), (0.33 * TOKEN_TOTAL ** 0.5), 256.0, ((0, 8), (1, 16)), jnp.float32),
        "keyval_moment_one": bell_draw(arg_keys[10], (2, MODEL_WIDTH, KEYVALUE_HEADS * HEAD_SIZE), (0.33 * TOKEN_TOTAL ** 0.5), 256.0, ((1, 128),), jnp.float32),
        "output_first": bell_draw(arg_keys[11], (QUERY_HEADS * HEAD_SIZE, MODEL_WIDTH), (0.0165 * TOKEN_TOTAL ** 0.5), 12.0, ((0, 16), (1, 8)), jnp.float32),
        "gateup_first": bell_draw(arg_keys[12], (2, MODEL_WIDTH, FF), (0.039 * TOKEN_TOTAL ** 0.5), 32.0, ((1, 8), (2, 16)), jnp.float32),
        "down_first": bell_draw(arg_keys[13], (FF, MODEL_WIDTH), (0.066 * TOKEN_TOTAL ** 0.5), 48.0, ((0, 16), (1, 8)), jnp.float32),
        "gains_first": bell_draw(arg_keys[14], (2, MODEL_WIDTH), (0.11 * TOKEN_TOTAL ** 0.5), 80.0, ((1, 128),), jnp.float32),
        "query_second": jnp.clip(jnp.exp(math.log(58982.4) - 2.0794415 * jax.random.uniform(arg_keys[15], (MODEL_WIDTH, QUERY_HEADS * HEAD_SIZE), jnp.float32) ** shard_levels(arg_keys[15], (MODEL_WIDTH, QUERY_HEADS * HEAD_SIZE), ((0, 8), (1, 16)), -0.2, 0.2)), 7372.8, 58982.4),
        "keyval_moment_two": jnp.clip(jnp.exp(math.log(58982.4) - 2.0794415 * jax.random.uniform(arg_keys[16], (2, MODEL_WIDTH, KEYVALUE_HEADS * HEAD_SIZE), jnp.float32) ** shard_levels(arg_keys[16], (2, MODEL_WIDTH, KEYVALUE_HEADS * HEAD_SIZE), ((1, 128),), -0.2, 0.2)), 7372.8, 58982.4),
        "output_second": jnp.clip(jnp.exp(math.log(147.456) - 2.1019144 * jax.random.uniform(arg_keys[17], (QUERY_HEADS * HEAD_SIZE, MODEL_WIDTH), jnp.float32) ** shard_levels(arg_keys[17], (QUERY_HEADS * HEAD_SIZE, MODEL_WIDTH), ((0, 16), (1, 8)), -0.2, 0.2)), 18.0224, 147.456),
        "gateup_second": jnp.clip(jnp.exp(math.log(802.816) - 2.1000608 * jax.random.uniform(arg_keys[18], (2, MODEL_WIDTH, FF), jnp.float32) ** shard_levels(arg_keys[18], (2, MODEL_WIDTH, FF), ((1, 8), (2, 16)), -0.2, 0.2)), 98.304, 802.816),
        "down_second": jnp.clip(jnp.exp(math.log(2359.296) - 2.0794415 * jax.random.uniform(arg_keys[19], (FF, MODEL_WIDTH), jnp.float32) ** shard_levels(arg_keys[19], (FF, MODEL_WIDTH), ((0, 16), (1, 8)), -0.2, 0.2)), 294.912, 2359.296),
        "gains_second": jnp.clip(jnp.exp(math.log(6553.6) - 2.0794415 * jax.random.uniform(arg_keys[20], (2, MODEL_WIDTH), jnp.float32) ** shard_levels(arg_keys[20], (2, MODEL_WIDTH), ((1, 128),), -0.2, 0.2)), 819.2, 6553.6),
    }


HIGH_PRECISION = lax.Precision.HIGHEST
BETA_ONE = 0.9
BETA_TWO = 0.95
ADAM_EPS = 1e-08
DECAY = 0.1
GAIN_RATE = 0.8
NORM_EPS = 1e-05

@jax.custom_vjp
def low(v):
    return lax.optimization_barrier(v.astype(jnp.bfloat16)).astype(jnp.float32)

@jax.custom_vjp
def low_back(v):
    return v

def low_keep(v):
    return (low(v), None)

def low_pass(kept, grad):
    return (grad,)

def back_keep(v):
    return (v, None)

def back_low(kept, grad):
    return (low(grad),)
low.defvjp(low_keep, low_pass)
low_back.defvjp(back_keep, back_low)

def doc_positions(segment):
    index = jnp.arange(segment.shape[0], dtype=jnp.int32)
    starts = jnp.concatenate([jnp.ones((1,), dtype=bool), segment[1:] != segment[:-1]])
    first = lax.cummax(jnp.where(starts, index, 0).astype(jnp.int32))
    return index - first

def rotate(values, positions):
    half = values.shape[-1] // 2
    freqs = 10000.0 ** (-jnp.arange(half, dtype=jnp.float32) * 2.0 / values.shape[-1])
    angles = positions.astype(jnp.float32)[:, None] * freqs[None, :]
    cosine = jnp.cos(angles)[:, None, :]
    sine = jnp.sin(angles)[:, None, :]
    first, second = (values[..., :half], values[..., half:])
    return jnp.concatenate([first * cosine - second * sine, first * sine + second * cosine], -1)

def norm(values, gain):
    scale = lax.rsqrt(lax.optimization_barrier(jnp.mean(values * values, axis=-1, keepdims=True)) + NORM_EPS)
    return values * scale * gain

def layer(inputs, segment, p_query, p_keyval, p_output, p_gateup, p_down, p_gains):
    segment_length = inputs.shape[0]
    positions = doc_positions(segment)
    gains_low = low(p_gains)
    normalized_input = low(norm(inputs, gains_low[0]))
    query = low_back(jnp.dot(normalized_input, low(p_query), precision=HIGH_PRECISION)).reshape(segment_length, QUERY_HEADS, HEAD_SIZE)
    query = low(rotate(query, positions))
    keyvalue_weight = low(p_keyval)
    key_rows = jnp.dot(normalized_input, keyvalue_weight[0], precision=HIGH_PRECISION).reshape(segment_length, KEYVALUE_HEADS, HEAD_SIZE)
    value_rows = jnp.dot(normalized_input, keyvalue_weight[1], precision=HIGH_PRECISION).reshape(segment_length, KEYVALUE_HEADS, HEAD_SIZE)
    repeat_factor = QUERY_HEADS // KEYVALUE_HEADS // SUMMED_HEADS
    key_rows = jnp.repeat(key_rows, repeat_factor, axis=1)
    value_rows = jnp.repeat(value_rows, repeat_factor, axis=1)
    key_rows = low(rotate(low_back(key_rows), positions))
    value_rows = low(low_back(value_rows))
    keys_all = jnp.repeat(key_rows, SUMMED_HEADS, axis=1)
    vals_all = jnp.repeat(value_rows, SUMMED_HEADS, axis=1)
    scale = HEAD_SIZE ** (-0.5)
    block = min(512, segment_length)
    count = segment_length // block
    key_index = jnp.arange(segment_length, dtype=jnp.int32)

    def one(start):
        qblock = lax.dynamic_slice_in_dim(query, start, block, 0)
        sblock = lax.dynamic_slice_in_dim(segment, start, block, 0)
        scores = jnp.einsum('qhd,khd->hqk', qblock, keys_all, precision=HIGH_PRECISION)
        scores = low_back(scores) * scale
        rows = start + jnp.arange(block, dtype=jnp.int32)
        allowed = (sblock[:, None] == segment[None, :]) & (rows[:, None] >= key_index[None, :])
        scores = jnp.where(allowed[None], scores, -1e+30)
        top = lax.optimization_barrier(jnp.max(scores, axis=-1, keepdims=True))
        weights = jnp.exp(scores - top)
        probs = weights / lax.optimization_barrier(jnp.sum(weights, axis=-1, keepdims=True))
        return jnp.einsum('hqk,khd->qhd', low(probs), vals_all, precision=HIGH_PRECISION)
    starts = (jnp.arange(count, dtype=jnp.int32) * block).astype(jnp.int32)
    attended = lax.map(jax.checkpoint(one), starts).reshape(segment_length, QUERY_HEADS * HEAD_SIZE)
    attended = low(low_back(attended))
    hidden_in = inputs + low_back(jnp.dot(attended, low(p_output), precision=HIGH_PRECISION))
    normed_two = low(norm(hidden_in, gains_low[1]))
    guw = low(p_gateup)
    gate = low_back(jnp.dot(normed_two, guw[0], precision=HIGH_PRECISION))
    upper = low_back(jnp.dot(normed_two, guw[1], precision=HIGH_PRECISION))
    hidden = low(jax.nn.silu(gate) * upper)
    return hidden_in + low_back(jnp.dot(hidden, low(p_down), precision=HIGH_PRECISION))

def adamw(weight, first, second, grad, rate, decay):
    first_new = BETA_ONE * first + (1.0 - BETA_ONE) * grad
    second_new = BETA_TWO * second + (1.0 - BETA_TWO) * grad * grad
    fix_one = 1.0 - BETA_ONE ** STEP
    fix_two = 1.0 - BETA_TWO ** STEP
    update = first_new / fix_one / (jnp.sqrt(second_new / fix_two) + ADAM_EPS)
    return (weight - rate * (update + decay * weight), first_new, second_new)

def reference(block_input, out_grad, segments, w_query, keyvalue_weights, w_output, w_gateup, w_down, norm_gains, query_first, keyval_moment_one, output_first, gateup_first, down_first, gains_first, query_second, keyval_moment_two, output_second, gateup_second, down_second, gains_second):
    weights = (w_query, keyvalue_weights, w_output, w_gateup, w_down, norm_gains)
    inputs_all = block_input.astype(jnp.float32).reshape(SEQS, LEN, MODEL_WIDTH)
    grads_all = out_grad.astype(jnp.float32).reshape(SEQS, LEN, MODEL_WIDTH)

    def per_sequence(totals, item):
        inputs, grad_seq, segment = item

        def forward(inp, p_query, p_keyval, p_output, p_gateup, p_down, p_gains):
            return layer(inp, segment, p_query, p_keyval, p_output, p_gateup, p_down, p_gains)
        result, pull = jax.vjp(forward, inputs, *weights)
        grads = pull(grad_seq)
        totals = tuple((a + b for a, b in zip(totals, grads[1:])))
        return (totals, (result.astype(jnp.bfloat16), grads[0].astype(jnp.bfloat16)))
    zeros = tuple((jnp.zeros_like(w) for w in weights))
    totals, (results, grads_in) = lax.scan(per_sequence, zeros, (inputs_all, grads_all, segments))
    g_query, g_keyval, g_output, g_gateup, g_down, g_gains = totals
    q_new, q_first, q_second = adamw(w_query, query_first, query_second, g_query, MODEL_WIDTH ** (-0.5), DECAY)
    kv_new, kv_first, kv_second = adamw(keyvalue_weights, keyval_moment_one, keyval_moment_two, g_keyval, MODEL_WIDTH ** (-0.5), DECAY)
    o_new, o_first, o_second = adamw(w_output, output_first, output_second, g_output, (MODEL_WIDTH // 64) ** (-0.5), DECAY)
    gu_new, gu_first, gu_second = adamw(w_gateup, gateup_first, gateup_second, g_gateup, MODEL_WIDTH ** (-0.5), DECAY)
    down_new, down_mom, down_sq = adamw(w_down, down_first, down_second, g_down, FF ** (-0.5), DECAY)
    gain_new, gain_first, gain_second = adamw(norm_gains, gains_first, gains_second, g_gains, GAIN_RATE, 0.0)
    return (results.reshape(TOKEN_TOTAL, MODEL_WIDTH), grads_in.reshape(TOKEN_TOTAL, MODEL_WIDTH), q_new, kv_new, o_new, gu_new, down_new, gain_new, q_first, kv_first, o_first, gu_first, down_mom, gain_first, q_second, kv_second, o_second, gu_second, down_sq, gain_second)
```

```python
import jax
import jax.numpy as jnp
from jax import lax
from jax.experimental import pallas as pl
from jax.experimental.pallas import tpu as pltpu
from jax.sharding import Mesh
from jax.sharding import PartitionSpec as P

MODEL_WIDTH = 2048
QUERY_HEADS = 32
KEYVALUE_HEADS = 4
HEAD_SIZE = 64
FF = 5632
STEP = 10

BETA_ONE = 0.9
BETA_TWO = 0.95
ADAM_EPS = 1e-08
DECAY = 0.1
GAIN_RATE = 0.8
NORM_EPS = 1e-05

RING = 4
SHARE = ("x", "core", "y")
ROWS = 128
TOKENS = RING * ROWS
HEADS = QUERY_HEADS // RING
WIDE = HEADS * ROWS
BLOCKS = 16
MASKED = -1e30
CHUNKS, CHUNK = 8, 256
PACK = ROWS + 48


def doc_starts(segment):
    index = jnp.arange(segment.shape[0], dtype=jnp.int32)
    starts = jnp.concatenate([jnp.ones((1,), dtype=bool), segment[1:] != segment[:-1]])
    return lax.cummax(jnp.where(starts, index, 0))


def shift(value, axis, step):
    return lax.ppermute(value, axis, [(i, (i + step) % RING) for i in range(RING)])


def gather_ring(value, axis):
    far = shift(value, axis, 2)
    return [value, shift(value, axis, 1), far, shift(value, axis, 3)]


def scatter_ring(parts, axis):
    far = shift(parts[2], axis, 2)
    return [parts[0], shift(parts[1], axis, 3), far, shift(parts[3], axis, 1)]


def absolute(slots, own):
    turned = jnp.stack([slots[0], slots[3], slots[2], slots[1]])
    return lax.dynamic_slice_in_dim(jnp.concatenate([turned, turned]), RING - own, RING, 0)


def relative(stacked, own):
    turned = jnp.concatenate([stacked, stacked])
    return [
        lax.dynamic_index_in_dim(turned, own + RING - s if s else own, 0, keepdims=False)
        for s in range(RING)
    ]


def dot(left, right, left_dim, right_dim):
    return lax.dot_general(
        left, right, (((left_dim,), (right_dim,)), ((), ())), preferred_element_type=jnp.float32
    )


def rms_scale(values):
    return lax.rsqrt(jnp.mean(values * values, axis=-1, keepdims=True) + NORM_EPS)


def norm_back(unit, scale, gain, grad):
    scaled = grad * gain
    return scale * (scaled - unit * jnp.mean(scaled * unit, axis=-1, keepdims=True))


def part(ref, index, size):
    return ref[index * size : (index + 1) * size, :]


def heads_side_by_side(value):
    return jnp.concatenate([part(value, h, HEAD_SIZE) for h in range(HEADS)], axis=1)


def mask_parts(info, starts, step):
    z, y = info[0], info[1]
    place = (z + RING - step) % RING
    begin = place * (RING * ROWS) + y * ROWS
    row = begin + lax.broadcasted_iota(jnp.int32, (1, ROWS), 1)
    rows = jnp.concatenate([row] * HEADS, axis=1)
    start = jnp.concatenate([starts] * HEADS, axis=1)
    return z, y, place * RING + y, rows, start


def block_slot(block, z, y):
    return ((y + RING - block % RING) % RING) * RING + (z + RING - block // RING) % RING


def rope(values, cosine, sine):
    half = HEAD_SIZE // 2
    out = []
    for h in range(values.shape[0] // HEAD_SIZE):
        first = values[h * HEAD_SIZE : h * HEAD_SIZE + half]
        second = values[h * HEAD_SIZE + half : (h + 1) * HEAD_SIZE]
        out += [first * cosine - second * sine, first * sine + second * cosine]
    return jnp.concatenate(out, axis=0)


def qkv_kernel(x0, x1, x2, x3, wq_ref, wkv_ref, gain_ref, cos_ref, sin_ref, n_ref, q_ref, kv_ref, w_ref):
    for s, ref in enumerate((x0, x1, x2, x3)):
        value = ref[...].astype(jnp.float32)
        n_ref[s * ROWS : (s + 1) * ROWS, :] = (
            value * rms_scale(value) * gain_ref[...]
        ).astype(jnp.bfloat16)
    for xc in range(CHUNKS):
        columns = slice(xc * CHUNK, (xc + 1) * CHUNK)
        for y in range(RING):
            w_ref[y * ROWS : (y + 1) * ROWS, columns] = wq_ref[xc * RING + y]
        rows = [
            wkv_ref[
                xc * RING + y, (z % 2) * 16 : (z % 2 + 1) * 16, (z // 2) * 128 : (z // 2 + 1) * 128
            ]
            for z in range(RING)
            for y in range(RING)
        ]
        w_ref[4 * ROWS : 5 * ROWS, columns] = jnp.concatenate(rows, axis=0).T
    qkv = dot(w_ref[...], n_ref[...], 1, 1)
    query = rope(qkv[: 4 * ROWS], cos_ref[...], sin_ref[...]).astype(jnp.bfloat16)
    q_ref[...] = query * jnp.bfloat16(HEAD_SIZE**-0.5)
    key = rope(qkv[4 * ROWS : 4 * ROWS + HEAD_SIZE], cos_ref[...], sin_ref[...])
    key_value = jnp.concatenate([key, qkv[4 * ROWS + HEAD_SIZE :]], axis=0)
    kv_ref[...] = key_value.T.astype(jnp.bfloat16)


def attend_kernel(
    info, q_ref, kv_ref, start_ref, wo_ref, o_ref, lse_ref, p0, p1, p2, p3, wall_ref, kvt_ref
):
    step = pl.program_id(0)

    @pl.when(step == 0)
    def _():
        for b in range(BLOCKS):
            kvt_ref[b] = kv_ref[b].T
        for xc in range(CHUNKS):
            for y in range(RING):
                wall_ref[y * ROWS : (y + 1) * ROWS, xc * CHUNK : (xc + 1) * CHUNK] = wo_ref[
                    xc * RING + y
                ]

    z, y, last, rows, start = mask_parts(info, start_ref[0], step)
    query = heads_side_by_side(q_ref[...])
    query = jnp.concatenate([query, jnp.zeros_like(query)], axis=0)

    def one(block, carry):
        top, total, acc = carry
        slot = block_slot(block, z, y)
        scores = dot(kv_ref[slot], query, 1, 0)
        key = block * ROWS + lax.broadcasted_iota(jnp.int32, (ROWS, 1), 0)
        scores = jnp.where((key >= start) & (key <= rows), scores, MASKED)
        new_top = jnp.maximum(top, jnp.max(scores, axis=0, keepdims=True))
        weights = jnp.exp(scores - new_top)
        fade = jnp.exp(top - new_top)
        total = total * fade + jnp.sum(weights, axis=0, keepdims=True)
        acc = acc * fade + dot(kvt_ref[slot, HEAD_SIZE:], weights.astype(jnp.bfloat16), 1, 0)
        return new_top, total, acc

    top, total, acc = lax.fori_loop(
        info[2 + step],
        last + 1,
        one,
        (
            jnp.full((1, WIDE), MASKED, jnp.float32),
            jnp.zeros((1, WIDE), jnp.float32),
            jnp.zeros((HEAD_SIZE, WIDE), jnp.float32),
        ),
    )
    out = acc / total
    out = jnp.concatenate([out[:, h * ROWS : (h + 1) * ROWS] for h in range(HEADS)], axis=0)
    o_ref[...] = out.astype(jnp.bfloat16)
    lse_ref[0] = top + jnp.log(total)
    product = dot(out.T.astype(jnp.bfloat16), wall_ref[...], 1, 0).astype(jnp.bfloat16)
    for s, ref in enumerate((p0, p1, p2, p3)):

        @pl.when(step == s)
        def _(ref=ref):
            ref[...] = product


def attend_back_kernel(
    info,
    q_ref,
    d0,
    d1,
    d2,
    d3,
    wall_ref,
    o_ref,
    lse_ref,
    kv_ref,
    start_ref,
    cos_ref,
    sin_ref,
    gq_ref,
    g0,
    g1,
    g2,
    g3,
    kvt_ref,
    gkv_ref,
    dh_ref,
):
    step = pl.program_id(0)

    @pl.when(step == 0)
    def _():
        for b in range(BLOCKS):
            kvt_ref[b] = kv_ref[b].T
        gkv_ref[...] = jnp.zeros_like(gkv_ref)
        for s, ref in enumerate((d0, d1, d2, d3)):
            dh_ref[s] = ref[...]

    z, y, last, rows, start = mask_parts(info, start_ref[0], step)
    query = heads_side_by_side(q_ref[...])
    grad = dot(wall_ref[...], dh_ref[step], 1, 1).astype(jnp.bfloat16)
    grad = heads_side_by_side(grad)
    out = heads_side_by_side(o_ref[...])
    rowdot = jnp.sum(grad.astype(jnp.float32) * out.astype(jnp.float32), axis=0, keepdims=True)
    query = jnp.concatenate([query, jnp.zeros_like(query)], axis=0)
    grad = jnp.concatenate([jnp.zeros_like(grad), grad], axis=0)
    lse = lse_ref[0]

    def one(block, acc):
        slot = block_slot(block, z, y)
        kv = kv_ref[slot]
        scores = dot(kv, query, 1, 0)
        key = block * ROWS + lax.broadcasted_iota(jnp.int32, (ROWS, 1), 0)
        probs = jnp.where((key >= start) & (key <= rows), jnp.exp(scores - lse), 0.0)
        grad_probs = dot(kv, grad, 1, 0)
        grad_scores = (probs * (grad_probs - rowdot)).astype(jnp.bfloat16)
        gkv_ref[slot] += dot(grad_scores, query, 1, 1) + dot(
            probs.astype(jnp.bfloat16), grad, 1, 1
        )
        return acc + dot(kvt_ref[slot, :HEAD_SIZE], grad_scores, 1, 0)

    acc = lax.fori_loop(
        info[2 + step], last + 1, one, jnp.zeros((HEAD_SIZE, WIDE), jnp.float32)
    )
    acc = acc * HEAD_SIZE**-0.5
    acc = jnp.concatenate([acc[:, h * ROWS : (h + 1) * ROWS] for h in range(HEADS)], axis=0)
    gq_ref[...] = rope(acc, cos_ref[...], -sin_ref[...]).astype(jnp.bfloat16)

    @pl.when(step == RING - 1)
    def _():
        for t, ref in enumerate((g0, g1, g2, g3)):
            for s in range(RING):
                ref[s * ROWS : (s + 1) * ROWS, :] = gkv_ref[t * RING + s].astype(jnp.bfloat16)


def input_back_kernel(
    gq_ref, k0, k1, k2, k3, w_ref, x0, x1, x2, x3, cos_ref, sin_ref, gqkv_ref, p0, p1, p2, p3, gain_ref, row_ref
):
    total = sum(ref[...].astype(jnp.float32) for ref in (k0, k1, k2, k3)).T
    key = rope(total[:HEAD_SIZE], cos_ref[...], -sin_ref[...])
    gqkv_ref[: 4 * ROWS] = gq_ref[...]
    gqkv_ref[4 * ROWS :] = jnp.concatenate([key, total[HEAD_SIZE:]], axis=0).astype(jnp.bfloat16)
    row_ref[...] = gqkv_ref[...].T
    scales = [rms_scale(ref[...].astype(jnp.float32)) for ref in (x0, x1, x2, x3)]
    for xc in range(CHUNKS):
        columns = slice(xc * CHUNK, (xc + 1) * CHUNK)
        product = dot(row_ref[...], w_ref[:, columns], 1, 0)
        gain = jnp.zeros((1, CHUNK), jnp.float32)
        for s, (ref, x, scale) in enumerate(
            zip((p0, p1, p2, p3), (x0, x1, x2, x3), scales)
        ):
            piece = product[s * ROWS : (s + 1) * ROWS]
            ref[:, columns] = piece.astype(jnp.bfloat16)
            unit = x[:, columns].astype(jnp.float32) * scale
            gain += jnp.sum(piece * unit, axis=0, keepdims=True)
        gain_ref[:, columns] = gain


def grad_qkv_kernel(info, gqkv_ref, n_ref, gains_ref, keep_ref, send_ref):
    y, core = info[1], info[7]
    for c, out in ((core, keep_ref), (1 - core, send_ref)):
        columns = pl.ds(pl.multiple_of(c * CHUNK, CHUNK), CHUNK)
        grad = dot(gqkv_ref[...], n_ref[:, columns], 1, 0)
        kv = grad[4 * ROWS :].T
        for home in range(RING):
            slot = (y + RING - home) % RING
            out[0, slot, :ROWS] = part(grad, home, ROWS).astype(jnp.bfloat16)
            halves = [
                jnp.concatenate(
                    [
                        kv[z * 64 + home * 16 : z * 64 + home * 16 + 16]
                        for z in (2 * side, 2 * side + 1)
                    ],
                    axis=0,
                )
                for side in range(2)
            ]
            out[0, slot, ROWS : ROWS + 32] = jnp.concatenate(halves, axis=1).astype(jnp.bfloat16)
            gains = jnp.broadcast_to(gains_ref[0, c, home], (16, 128))
            out[0, slot, ROWS + 32 :] = jnp.concatenate([gains, gains], axis=1).astype(jnp.bfloat16)


def grad_output_kernel(info, o_ref, d0, d1, d2, d3, keep_ref, send_ref):
    y, core = info[1], info[7]
    for c, out in ((core, keep_ref), (1 - core, send_ref)):
        columns = pl.ds(pl.multiple_of(c * CHUNK, CHUNK), CHUNK)
        rows = jnp.concatenate([ref[:, columns] for ref in (d0, d1, d2, d3)], axis=0)
        grad = dot(o_ref[...], rows, 1, 0)
        for home in range(RING):
            slot = (y + RING - home) % RING
            out[0, slot] = part(grad, home, ROWS).astype(jnp.bfloat16)


def feed_kernel(
    n0, n1, n2, n3, d0, d1, d2, d3, w_hbm, hg_ref, p0, p1, p2, p3, w_ref, n_ref, d_ref, row_ref, sems
):
    units = w_ref.shape[2]
    copies = [
        [
            pltpu.make_async_copy(
                w_hbm.at[xc, y], w_ref.at[y, :, :, pl.ds(xc * CHUNK, CHUNK)], sems.at[y, xc]
            )
            for xc in range(CHUNKS)
        ]
        for y in range(RING)
    ]
    for group in copies:
        for copy in group:
            copy.start()
    for s in range(RING):
        n_ref[s * ROWS : (s + 1) * ROWS, :] = (n0, n1, n2, n3)[s][...]
        d_ref[s * ROWS : (s + 1) * ROWS, :] = (d0, d1, d2, d3)[s][...]
    for y in range(RING):
        for copy in copies[y]:
            copy.wait()

    def one(y, _):
        gate_up = dot(w_ref[y, :2].reshape(2 * units, MODEL_WIDTH), n_ref[...], 1, 1)
        grad_hidden = dot(w_ref[y, 2], d_ref[...], 1, 1)
        gate, upper = gate_up[:units], gate_up[units:]
        sig = 1.0 / (1.0 + jnp.exp(-gate))
        silu = gate * sig
        grad_gate = grad_hidden * upper * (sig + silu * (1.0 - sig))
        hg_ref[y, 0] = grad_gate.astype(jnp.bfloat16)
        hg_ref[y, 1] = (grad_hidden * silu).astype(jnp.bfloat16)
        hg_ref[y, 2] = (silu * upper).astype(jnp.bfloat16)
        row_ref[y] = hg_ref[y, :2].reshape(2 * units, TOKENS).T
        return 0

    lax.fori_loop(0, RING, one, 0)

    def back(xc, _):
        columns = pl.ds(pl.multiple_of(xc * CHUNK, CHUNK), CHUNK)
        total = sum(
            dot(row_ref[y], w_ref[y, :2, :, columns].reshape(2 * units, CHUNK), 1, 0)
            for y in range(RING)
        ).astype(jnp.bfloat16)
        for s, ref in enumerate((p0, p1, p2, p3)):
            ref[:, columns] = total[s * ROWS : (s + 1) * ROWS]
        return 0

    lax.fori_loop(0, CHUNKS, back, 0)


def feed_grad_kernel(
    hg_ref, n0, n1, n2, n3, d0, d1, d2, d3, w_ref, g_ref, p0, p1, p2, p3, row_ref
):
    units = w_ref.shape[3]

    @pl.when(pl.program_id(0) == 0)
    def _():
        for y in range(RING):
            row_ref[y] = hg_ref[y, 2].T

    normed = jnp.concatenate([ref[...] for ref in (n0, n1, n2, n3)], axis=0)
    grads = jnp.concatenate([ref[...] for ref in (d0, d1, d2, d3)], axis=0)
    for y in range(RING):
        grad = dot(hg_ref[y, :2].reshape(2 * units, TOKENS), normed, 1, 0).astype(jnp.bfloat16)
        g_ref[0, y, :2] = grad.reshape(2, units, CHUNK)
        g_ref[0, y, 2] = dot(hg_ref[y, 2], grads, 1, 0).astype(jnp.bfloat16)
    total = sum(dot(row_ref[y], w_ref[0, y, 0], 1, 0) for y in range(RING)).astype(jnp.bfloat16)
    for s, ref in enumerate((p0, p1, p2, p3)):
        ref[...] = total[s * ROWS : (s + 1) * ROWS]


def whole(shape):
    return pl.BlockSpec(shape, lambda *_: (0,) * len(shape))


def struct(shape, dtype=jnp.bfloat16):
    return jax.ShapeDtypeStruct(shape, dtype)


def cost(flops, moved, exps=0):
    return pl.CostEstimate(flops=flops, bytes_accessed=moved, transcendentals=exps)


def params(mebibytes):
    return pltpu.CompilerParams(vmem_limit_bytes=mebibytes << 20)


SLOT = (ROWS, MODEL_WIDTH)
COLUMNS = pl.BlockSpec((HEADS * HEAD_SIZE, ROWS), lambda s, info: (0, s))
TABLE = pl.BlockSpec((HEAD_SIZE // 2, ROWS), lambda s, info: (0, s))


def row_spec(width):
    return pl.BlockSpec((1, 1, width), lambda s, info: (s, 0, 0))


def project_qkv(x_slots, pack, gain, cosine, sine):
    return pl.pallas_call(
        qkv_kernel,
        grid=(1,),
        in_specs=[whole(SLOT)] * 4
        + [
            pl.BlockSpec((32, 128, CHUNK), lambda i: (0, 1, 0)),
            pl.BlockSpec((32, 32, CHUNK), lambda i: (0, 8, 0)),
            whole((1, MODEL_WIDTH)),
            whole((32, TOKENS)),
            whole((32, TOKENS)),
        ],
        out_specs=[
            whole((TOKENS, MODEL_WIDTH)),
            whole((512, TOKENS)),
            whole((TOKENS, 128)),
            whole((640, MODEL_WIDTH)),
        ],
        out_shape=[
            struct((TOKENS, MODEL_WIDTH)),
            struct((512, TOKENS)),
            struct((TOKENS, 128)),
            struct((640, MODEL_WIDTH)),
        ],
        compiler_params=params(48),
        cost_estimate=cost(2 * 640 * TOKENS * MODEL_WIDTH, 9 << 20),
        name="project_qkv",
    )(*x_slots, pack, pack, gain, cosine, sine)


def attend(info, q_t, kv, starts, pack):
    return pl.pallas_call(
        attend_kernel,
        grid_spec=pltpu.PrefetchScalarGridSpec(
            num_scalar_prefetch=1,
            grid=(RING,),
            in_specs=[
                COLUMNS,
                whole((BLOCKS, ROWS, 128)),
                row_spec(ROWS),
                pl.BlockSpec((32, 128, CHUNK), lambda s, info: (0, 0, 0)),
            ],
            out_specs=[COLUMNS, row_spec(WIDE)] + [whole(SLOT)] * 4 + [whole((512, MODEL_WIDTH))],
            scratch_shapes=[pltpu.VMEM((BLOCKS, 128, ROWS), jnp.bfloat16)],
        ),
        out_shape=[struct((512, TOKENS)), struct((RING, 1, WIDE), jnp.float32)]
        + [struct(SLOT)] * 4
        + [struct((512, MODEL_WIDTH))],
        compiler_params=params(40),
        cost_estimate=cost(
            4 * HEADS * TOKENS * 640 * 128 + 2 * 512 * TOKENS * MODEL_WIDTH, 8 << 20, HEADS * TOKENS * 640
        ),
        name="attend",
    )(info, q_t, kv, starts, pack)


def attend_back(info, q_t, dh_slots, wall, o_t, lse, kv, starts, cosine, sine):
    return pl.pallas_call(
        attend_back_kernel,
        grid_spec=pltpu.PrefetchScalarGridSpec(
            num_scalar_prefetch=1,
            grid=(RING,),
            in_specs=[COLUMNS]
            + [whole(SLOT)] * 4
            + [
                whole((512, MODEL_WIDTH)),
                COLUMNS,
                row_spec(WIDE),
                whole((BLOCKS, ROWS, 128)),
                row_spec(ROWS),
                TABLE,
                TABLE,
            ],
            out_specs=[COLUMNS] + [whole((TOKENS, 128))] * 4,
            scratch_shapes=[
                pltpu.VMEM((BLOCKS, 128, ROWS), jnp.bfloat16),
                pltpu.VMEM((BLOCKS, ROWS, 128), jnp.float32),
                pltpu.VMEM((RING, *SLOT), jnp.bfloat16),
            ],
        ),
        out_shape=[struct((512, TOKENS))] + [struct((TOKENS, 128))] * 4,
        compiler_params=params(40),
        cost_estimate=cost(
            10 * HEADS * TOKENS * 640 * 128 + 2 * 512 * TOKENS * MODEL_WIDTH, 8 << 20, HEADS * TOKENS * 640
        ),
        name="attend_back",
    )(info, q_t, *dh_slots, wall, o_t, lse, kv, starts, cosine, sine)


def input_back(gq_t, gkv_slots, w_qkv, x_slots, cosine, sine):
    return pl.pallas_call(
        input_back_kernel,
        grid=(1,),
        in_specs=[whole((512, TOKENS))]
        + [whole((TOKENS, 128))] * 4
        + [whole((640, MODEL_WIDTH))]
        + [whole(SLOT)] * 4
        + [whole((32, TOKENS))] * 2,
        out_specs=[whole((640, TOKENS))] + [whole(SLOT)] * 4 + [whole((1, MODEL_WIDTH))],
        out_shape=[struct((640, TOKENS))] + [struct(SLOT)] * 4 + [struct((1, MODEL_WIDTH), jnp.float32)],
        scratch_shapes=[pltpu.VMEM((TOKENS, 640), jnp.bfloat16)],
        compiler_params=params(48),
        cost_estimate=cost(2 * 640 * TOKENS * MODEL_WIDTH, 9 << 20),
        name="input_back",
    )(gq_t, *gkv_slots, w_qkv, *x_slots, cosine, sine)


def pack_specs(rows):
    spec = pl.BlockSpec((1, RING, rows, CHUNK), lambda s, info: (s, 0, 0, 0))
    return [spec, spec], [struct((RING, RING, rows, CHUNK))] * 2


def pair_columns(rows):
    return pl.BlockSpec((rows, 2 * CHUNK), lambda s, info: (0, (info[6] + RING - s) % RING))


def grad_qkv(info, gqkv_t, normed, gains):
    out_specs, out_shape = pack_specs(PACK)
    return pl.pallas_call(
        grad_qkv_kernel,
        grid_spec=pltpu.PrefetchScalarGridSpec(
            num_scalar_prefetch=1,
            grid=(RING,),
            in_specs=[
                whole((640, TOKENS)),
                pair_columns(TOKENS),
                pl.BlockSpec(
                    (1, 2, RING, 1, 128), lambda s, info: ((info[6] + RING - s) % RING, 0, 0, 0, 0)
                ),
            ],
            out_specs=out_specs,
        ),
        out_shape=out_shape,
        compiler_params=params(32),
        cost_estimate=cost(2 * 640 * TOKENS * MODEL_WIDTH, 6 << 20),
        name="grad_qkv",
    )(info, gqkv_t, normed, gains)


def grad_output(info, o_t, dh_slots):
    out_specs, out_shape = pack_specs(ROWS)
    return pl.pallas_call(
        grad_output_kernel,
        grid_spec=pltpu.PrefetchScalarGridSpec(
            num_scalar_prefetch=1,
            grid=(RING,),
            in_specs=[whole((512, TOKENS))] + [pair_columns(ROWS)] * 4,
            out_specs=out_specs,
        ),
        out_shape=out_shape,
        compiler_params=params(32),
        cost_estimate=cost(2 * 512 * TOKENS * MODEL_WIDTH, 6 << 20),
        name="grad_output",
    )(info, o_t, *dh_slots)


def feed(n_slots, d_slots, weights):
    units = weights.shape[3]
    return pl.pallas_call(
        feed_kernel,
        in_specs=[pl.BlockSpec(memory_space=pltpu.VMEM)] * 8 + [pl.BlockSpec(memory_space=pl.ANY)],
        out_specs=[pl.BlockSpec(memory_space=pltpu.VMEM)] * 5,
        out_shape=[struct((RING, 3, units, TOKENS))] + [struct(SLOT)] * 4,
        scratch_shapes=[
            pltpu.VMEM((RING, 3, units, MODEL_WIDTH), jnp.bfloat16),
            pltpu.VMEM((TOKENS, MODEL_WIDTH), jnp.bfloat16),
            pltpu.VMEM((TOKENS, MODEL_WIDTH), jnp.bfloat16),
            pltpu.VMEM((RING, TOKENS, 2 * units), jnp.bfloat16),
            pltpu.SemaphoreType.DMA((RING, CHUNKS)),
        ],
        compiler_params=params(58),
        cost_estimate=cost(2 * 5 * RING * units * TOKENS * MODEL_WIDTH, 28 << 20, RING * units * TOKENS),
        name="feed",
    )(*n_slots, *d_slots, weights)


def feed_grad(hg, n_slots, d_slots, weights):
    units = weights.shape[3]
    chunk = pl.BlockSpec((ROWS, CHUNK), lambda i: (0, i))
    return pl.pallas_call(
        feed_grad_kernel,
        grid=(CHUNKS,),
        in_specs=[whole((RING, 3, units, TOKENS))]
        + [chunk] * 8
        + [pl.BlockSpec((1, RING, 1, units, CHUNK), lambda i: (i, 0, 2, 0, 0))],
        out_specs=[pl.BlockSpec((1, RING, 3, units, CHUNK), lambda i: (i, 0, 0, 0, 0))] + [chunk] * 4,
        out_shape=[struct(weights.shape)] + [struct(SLOT)] * 4,
        scratch_shapes=[pltpu.VMEM((RING, TOKENS, units), jnp.bfloat16)],
        compiler_params=params(40),
        cost_estimate=cost(2 * 4 * RING * units * TOKENS * MODEL_WIDTH, 34 << 20),
        name="feed_grad",
    )(hg, *n_slots, *d_slots, weights)


def scatter_share(keep, send):
    f32 = jnp.float32
    other = lax.ppermute(send, "core", [(0, 1), (1, 0)])
    parts = [
        (keep[s].astype(f32) + other[s].astype(f32)).astype(jnp.bfloat16) for s in range(RING)
    ]
    parts = scatter_ring(parts, "x")
    parts = [
        sum(p[s].astype(f32) for p in parts).astype(jnp.bfloat16) for s in range(RING)
    ]
    parts = scatter_ring(parts, "y")
    return sum(p.astype(f32) for p in parts)


def adamw(weight, first, second, grad, rate, decay):
    first_new = BETA_ONE * first + (1.0 - BETA_ONE) * grad
    second_new = BETA_TWO * second + (1.0 - BETA_TWO) * grad * grad
    fix_one = 1.0 - BETA_ONE**STEP
    fix_two = 1.0 - BETA_TWO**STEP
    update = first_new / fix_one / (jnp.sqrt(second_new / fix_two) + ADAM_EPS)
    return (weight - rate * (update + decay * weight), first_new, second_new)


def local(
    block_input,
    out_grad,
    segments,
    w_query,
    keyvalue_weights,
    w_output,
    w_gateup,
    w_down,
    norm_gains,
    query_first,
    keyval_moment_one,
    output_first,
    gateup_first,
    down_first,
    gains_first,
    query_second,
    keyval_moment_two,
    output_second,
    gateup_second,
    down_second,
    gains_second,
):
    bf16, f32 = jnp.bfloat16, jnp.float32
    x, core, z, y = (lax.axis_index(name) for name in ("x", "core", "z", "y"))
    units = w_down.shape[0]

    kv_rows = keyvalue_weights.astype(bf16).reshape(2, 16, RING, HEAD_SIZE).transpose(2, 1, 0, 3)
    message = jnp.concatenate(
        [
            kv_rows.reshape(RING, 16, 128),
            jnp.broadcast_to(
                jnp.pad(norm_gains.astype(bf16).reshape(1, 1, 32), ((0, 0), (0, 15), (0, 96))),
                (RING, 16, 128),
            ),
        ],
        1,
    )
    small = absolute(scatter_ring_from(relative(message, z), "z"), z)
    kv_piece = jnp.concatenate(
        [small[:2, :16].reshape(32, 128), small[2:, :16].reshape(32, 128)], 1
    )
    gain_piece = jnp.pad(small[:, 16, :32].reshape(1, 128), ((0, 15), (0, 128)))
    pack = jnp.concatenate(
        [w_output.astype(bf16), w_query.astype(bf16).T, kv_piece, gain_piece], 0
    )
    pack = lax.all_gather(pack, SHARE, axis=0, tiled=False)
    feed_shard = jnp.concatenate(
        [w_gateup.astype(bf16).transpose(0, 2, 1), w_down.astype(bf16)[None]], 0
    )
    feed_shard, _ = lax.optimization_barrier((feed_shard, pack))
    w_feed = lax.all_gather(feed_shard, SHARE, axis=0, tiled=False)
    w_feed = w_feed.reshape(CHUNKS, RING, 3, units, CHUNK)
    gains = pack[:, 288, :128].reshape(CHUNKS, RING, RING, 2, 16).transpose(3, 0, 2, 1, 4)
    gains = gains.reshape(2, MODEL_WIDTH).astype(f32)

    x_slots = gather_ring(block_input, "z")

    starts = doc_starts(segments[0])
    by_block = lax.dynamic_index_in_dim(starts.reshape(RING, RING, ROWS), y, 1, keepdims=False)
    row_starts = jnp.stack(relative(by_block, z))
    places = (z + RING - jnp.arange(RING, dtype=jnp.int32)) % RING
    begins = places * (RING * ROWS) + y * ROWS
    positions = (begins[:, None] + jnp.arange(ROWS, dtype=jnp.int32) - row_starts).reshape(-1)
    half = HEAD_SIZE // 2
    freqs = 10000.0 ** (-jnp.arange(half, dtype=f32) * 2.0 / HEAD_SIZE)
    angles = freqs[:, None] * positions.astype(f32)[None, :]
    cosine, sine = jnp.cos(angles), jnp.sin(angles)
    info = jnp.concatenate(
        [
            jnp.stack([z, y]).astype(jnp.int32),
            row_starts[:, 0] // ROWS,
            jnp.stack([x, core]).astype(jnp.int32),
        ]
    )
    row_starts = row_starts[:, None, :]

    normed, q_t, kv_own, w_qkv = project_qkv(x_slots, pack, gains[:1], cosine, sine)
    kv = jnp.stack(gather_ring(kv_own, "y")).reshape(BLOCKS, ROWS, 2 * HEAD_SIZE)
    o_t, lse, *o_slots, wo = attend(info, q_t, kv, row_starts, pack)
    o_sum = sum(p.astype(f32) for p in scatter_ring(o_slots, "z"))
    h1 = block_input.astype(f32) + o_sum

    scale_two = rms_scale(h1)
    unit_two = h1 * scale_two
    n_slots = gather_ring((unit_two * gains[1]).astype(bf16), "z")
    d_slots = gather_ring(out_grad, "z")
    hg, *gn2_slots = feed(n_slots, d_slots, w_feed)
    gn2 = sum(p.astype(f32) for p in scatter_ring(gn2_slots, "z"))
    grad_gain_two = jnp.sum(gn2 * unit_two, 0, keepdims=True)
    dh1 = out_grad.astype(f32) + norm_back(unit_two, scale_two, gains[1], gn2)
    grad_feed, *down_slots = feed_grad(hg, n_slots, d_slots, w_feed)
    own_feed = lax.psum_scatter(
        grad_feed.reshape(32, 3, units, CHUNK), SHARE, scatter_dimension=0, tiled=False
    ).astype(f32)

    dh_slots = gather_ring(dh1.astype(bf16), "z")
    gq_t, *gkv_slots = attend_back(info, q_t, dh_slots, wo, o_t, lse, kv, row_starts, cosine, sine)
    gkv_slots = scatter_ring(gkv_slots, "y")
    gqkv_t, *gn1_slots, grad_gain_one = input_back(gq_t, gkv_slots, w_qkv, x_slots, cosine, sine)
    gn1 = sum(p.astype(f32) for p in scatter_ring(gn1_slots, "z"))
    own_o = scatter_share(*grad_output(info, o_t, dh_slots))
    grad_gains = jnp.concatenate([grad_gain_one, grad_gain_two], 0)
    grad_gains = grad_gains.reshape(2, 4, 2, RING, RING, 16).transpose(1, 2, 4, 3, 0, 5)
    own_pack = scatter_share(
        *grad_qkv(info, gqkv_t, normed, grad_gains.reshape(4, 2, RING, 1, 128))
    )
    down_sum = sum(p.astype(f32) for p in scatter_ring(down_slots, "z"))
    result = (h1 + down_sum).astype(bf16)
    own_inputs = block_input.astype(f32)
    scale_one = rms_scale(own_inputs)
    grad_input = (dh1 + norm_back(own_inputs * scale_one, scale_one, gains[0], gn1)).astype(bf16)

    own_q = own_pack[:ROWS].T
    kv_piece = own_pack[ROWS : ROWS + 32]
    kv_piece = jnp.concatenate([kv_piece[:, :128], kv_piece[:, 128:]], 0).reshape(RING, 16, 128)
    gain_piece = own_pack[ROWS + 32, :128].reshape(RING, 1, 32)
    message = jnp.concatenate([kv_piece, jnp.pad(gain_piece, ((0, 0), (0, 15), (0, 96)))], 1)
    small = absolute(scatter_ring_from(relative(message, z), "z"), z)
    own_kv = small[:, :16].reshape(RING, 16, 2, HEAD_SIZE).transpose(2, 1, 0, 3)
    own_kv = own_kv.reshape(2, 16, RING * HEAD_SIZE)
    own_gains = jnp.sum(small[:, 16, :32], 0).reshape(2, 16)

    rate = MODEL_WIDTH ** (-0.5)
    q = adamw(w_query, query_first, query_second, own_q, rate, DECAY)
    kvs = adamw(keyvalue_weights, keyval_moment_one, keyval_moment_two, own_kv, rate, DECAY)
    o = adamw(w_output, output_first, output_second, own_o, (MODEL_WIDTH // 64) ** (-0.5), DECAY)
    own_gu = own_feed[:2].transpose(0, 2, 1)
    gu = adamw(w_gateup, gateup_first, gateup_second, own_gu, rate, DECAY)
    down = adamw(w_down, down_first, down_second, own_feed[2], FF ** (-0.5), DECAY)
    gain = adamw(norm_gains, gains_first, gains_second, own_gains, GAIN_RATE, 0.0)
    updates = (q, kvs, o, gu, down, gain)
    return (result, grad_input, *(u[i] for i in range(3) for u in updates))


def scatter_ring_from(slots, axis):
    own, after, far, before = scatter_ring(slots, axis)
    return [own, before, far, after]


def solution(mesh):
    view = Mesh(mesh.devices.reshape(4, 2, 4, 4), ("x", "core", "z", "y"))
    dp, tensor = ("x", "core"), ("z", "y")
    both = dp + tensor
    tokens = P(both, None)
    weights = (
        P(dp, tensor),
        P(None, both, None),
        P(tensor, dp),
        P(None, dp, tensor),
        P(tensor, dp),
        P(None, both),
    )
    return jax.shard_map(
        local,
        mesh=view,
        in_specs=(tokens, tokens, P(dp, None), *weights * 3),
        out_specs=(tokens, tokens, *weights * 3),
        check_vma=False,
    )
```

```python
import functools

import jax
import jax.numpy as jnp
from jax import lax
from jax.experimental import pallas as pl
from jax.experimental.pallas import tpu as pltpu
from jax.sharding import Mesh
from jax.sharding import PartitionSpec as P

MODEL_WIDTH = 2048
QUERY_HEADS = 32
KEYVALUE_HEADS = 4
HEAD_SIZE = 64
FF = 5632
STEP = 10

BETA_ONE = 0.9
BETA_TWO = 0.95
ADAM_EPS = 1e-08
DECAY = 0.1
GAIN_RATE = 0.8
NORM_EPS = 1e-05

RING = 4
SHARE = ("x", "core", "y")
ROWS = 128
TOKENS = RING * ROWS
HEADS = QUERY_HEADS // RING
WIDE = HEADS * ROWS
BLOCKS = 16
MASKED = -1e30
HALVES = (1, 3, 0, 2)
CHUNKS, CHUNK = 8, 256
PACK = 2 * ROWS + 48


def doc_starts(segment):
    index = jnp.arange(segment.shape[0], dtype=jnp.int32)
    starts = jnp.concatenate([jnp.ones((1,), dtype=bool), segment[1:] != segment[:-1]])
    return lax.cummax(jnp.where(starts, index, 0))


def shift(value, axis, step):
    return lax.ppermute(value, axis, [(i, (i + step) % RING) for i in range(RING)])


def gather_ring(value, axis):
    far = shift(value, axis, 2)
    return [value, shift(value, axis, 1), far, shift(value, axis, 3)]


def gather_far_last(value, axis, *others):
    near = shift(value, axis, 1), shift(value, axis, 3)
    (value_late,) = after([value], *near, *others)
    return [value, near[0], shift(value_late, axis, 2), near[1]]


def scatter_far_last(own, part_one, part_three, part_two, axis):
    near = shift(part_one, axis, 3), shift(part_three, axis, 1)
    (part_two,) = after([part_two], *near)
    return [own, near[0], shift(part_two, axis, 2), near[1]]


def scatter_ring(parts, axis):
    far = shift(parts[2], axis, 2)
    return [parts[0], shift(parts[1], axis, 3), far, shift(parts[3], axis, 1)]


def absolute(slots, own):
    turned = jnp.stack([slots[0], slots[3], slots[2], slots[1]])
    return lax.dynamic_slice_in_dim(jnp.concatenate([turned, turned]), RING - own, RING, 0)


def relative(stacked, own):
    turned = jnp.concatenate([stacked, stacked])
    return [
        lax.dynamic_index_in_dim(turned, own + RING - s if s else own, 0, keepdims=False)
        for s in range(RING)
    ]


def dot(left, right, left_dim, right_dim):
    return lax.dot_general(
        left, right, (((left_dim,), (right_dim,)), ((), ())), preferred_element_type=jnp.float32
    )


def rms_scale(values):
    return lax.rsqrt(jnp.mean(values * values, axis=-1, keepdims=True) + NORM_EPS)


def norm_back(unit, scale, gain, grad):
    scaled = grad * gain
    return scale * (scaled - unit * jnp.mean(scaled * unit, axis=-1, keepdims=True))


def part(ref, index, size):
    return ref[index * size : (index + 1) * size, :]


def heads_side_by_side(value):
    return jnp.concatenate([part(value, h, HEAD_SIZE) for h in range(HEADS)], axis=1)


def mask_parts(info, starts, step):
    z, y = info[0], info[1]
    place = (z + RING - step) % RING
    begin = place * (RING * ROWS) + y * ROWS
    row = begin + lax.broadcasted_iota(jnp.int32, (1, ROWS), 1)
    rows = jnp.concatenate([row] * HEADS, axis=1)
    start = jnp.concatenate([starts] * HEADS, axis=1)
    return z, y, place * RING + y, rows, start


def block_slot(block, z, y):
    return ((y + RING - block % RING) % RING) * RING + (z + RING - block // RING) % RING


def rope(values, cosine, sine):
    half = HEAD_SIZE // 2
    out = []
    for h in range(values.shape[0] // HEAD_SIZE):
        first = values[h * HEAD_SIZE : h * HEAD_SIZE + half]
        second = values[h * HEAD_SIZE + half : (h + 1) * HEAD_SIZE]
        out += [first * cosine - second * sine, first * sine + second * cosine]
    return jnp.concatenate(out, axis=0)


def turned(place, step):
    return (place + RING - step) % RING


def weight_slots(info, own_refs, other_ref):
    y, x, core = info[1], info[6], info[7]
    for cs in range(2):
        for ys in range(RING):
            for xs in range(RING):
                ref = other_ref.at[ys, xs] if cs else own_refs[ys].at[xs]
                yield turned(x, xs) * 2 + (1 - core if cs else core), turned(y, ys), ref


def place_of(index, size):
    return pl.ds(pl.multiple_of(index * size, size), size)


def gain_spread(which, transposed):
    shape = (CHUNK, 512) if transposed else (512, CHUNK)
    lane = lax.broadcasted_iota(jnp.int32, shape, 1 if transposed else 0)
    column = lax.broadcasted_iota(jnp.int32, shape, 0 if transposed else 1)
    y, z, gain, row = lane // 128, lane // 32 % 4, lane // 16 % 2, lane % 16
    same = (column // 64 == z) & (column // 16 % 4 == y) & (column % 16 == row) & (gain == which)
    return jnp.where(same, 1.0, 0.0).astype(jnp.bfloat16)


def fetch_pack(pack_hbm, which, out_ref, sems):
    return [
        pltpu.make_async_copy(
            pack_hbm.at[xc * RING + y, pl.ds(which * ROWS, ROWS)],
            out_ref.at[pl.ds(y * ROWS, ROWS), pl.ds(xc * CHUNK, CHUNK)],
            sems.at[xc, y],
        )
        for xc in range(CHUNKS)
        for y in range(RING)
    ]


def qkv_kernel(
    info, x0, x1, x2, x3, pack_hbm, k0, k1, k2, k3, k_other, cos_ref, sin_ref,
    n_ref, q_ref, kv_ref, w_ref, gain_ref, scale_ref, wkv_ref, piece_ref, sems,
):
    copies = fetch_pack(pack_hbm, 1, w_ref, sems)
    for copy in copies:
        copy.start()
    for chunk, y, ref in weight_slots(info, (k0, k1, k2, k3), k_other):
        for z in range(RING):
            wkv_ref[chunk, pl.ds(pl.multiple_of(z * 64 + y * 16, 16), 16), :] = ref[
                (z % 2) * 16 : (z % 2 + 1) * 16, (z // 2) * 128 : (z // 2 + 1) * 128
            ]
        piece_ref[chunk, y] = ref[32:48, :128].astype(jnp.float32)
    pieces = [
        jnp.concatenate([piece_ref[xc, y, :1] for y in range(RING)], axis=1) for xc in range(CHUNKS)
    ]
    pieces = jnp.concatenate(pieces, axis=0).astype(jnp.bfloat16)
    gains = [dot(pieces, gain_spread(which, False), 1, 0) for which in range(2)]
    for xc in range(CHUNKS):
        columns = slice(xc * CHUNK, (xc + 1) * CHUNK)
        w_ref[4 * ROWS : 5 * ROWS, columns] = wkv_ref[xc].T
        for which in range(2):
            gain_ref[which : which + 1, columns] = gains[which][xc : xc + 1]
    for s, ref in enumerate((x0, x1, x2, x3)):
        value = ref[...].astype(jnp.float32)
        scale = rms_scale(value)
        scale_ref[s * ROWS : (s + 1) * ROWS] = jnp.broadcast_to(scale, (ROWS, 128))
        n_ref[s * ROWS : (s + 1) * ROWS, :] = (value * scale * gain_ref[:1]).astype(jnp.bfloat16)
    for copy in copies:
        copy.wait()
    qkv = dot(w_ref[...], n_ref[...], 1, 1)
    query = rope(qkv[: 4 * ROWS], cos_ref[...], sin_ref[...]).astype(jnp.bfloat16)
    q_ref[...] = query * jnp.bfloat16(HEAD_SIZE**-0.5)
    key = rope(qkv[4 * ROWS : 4 * ROWS + HEAD_SIZE], cos_ref[...], sin_ref[...])
    key_value = jnp.concatenate([key, qkv[4 * ROWS + HEAD_SIZE :]], axis=0)
    kv_ref[...] = key_value.T.astype(jnp.bfloat16)


def slot_of(slots, step):
    out = slots[0]
    for index in range(1, len(slots)):
        out = out + (slots[index] - slots[index - 1]) * ((step + len(slots) - index) // len(slots))
    return out


def attend_kernel(
    slots, info, q_ref, kv_ref, start_ref, *refs
):
    step = pl.program_id(0)
    first_call = 2 not in slots
    if first_call:
        pack_hbm, o_ref, lse_ref, *outs, wall_ref, kvt_ref, sems = refs
        copies = fetch_pack(pack_hbm, 0, wall_ref, sems)

        @pl.when(step == 0)
        def _():
            for copy in copies:
                copy.start()
            for b in range(BLOCKS):
                kvt_ref[b] = kv_ref[b].T
    else:
        wall_ref, kvt_ref, o_ref, lse_ref, *outs = refs

    slot_now = slot_of(slots, step)
    z, y, last, rows, start = mask_parts(info, start_ref[0], slot_now)
    query = heads_side_by_side(q_ref[...])
    query = jnp.concatenate([query, jnp.zeros_like(query)], axis=0)

    def one(block, carry):
        top, total, acc = carry
        slot = block_slot(block, z, y)
        scores = dot(kv_ref[slot], query, 1, 0)
        key = block * ROWS + lax.broadcasted_iota(jnp.int32, (ROWS, 1), 0)
        scores = jnp.where((key >= start) & (key <= rows), scores, MASKED)
        new_top = jnp.maximum(top, jnp.max(scores, axis=0, keepdims=True))
        weights = jnp.exp(scores - new_top)
        fade = jnp.exp(top - new_top)
        total = total * fade + jnp.sum(weights, axis=0, keepdims=True)
        acc = acc * fade + dot(kvt_ref[slot, HEAD_SIZE:], weights.astype(jnp.bfloat16), 1, 0)
        return new_top, total, acc

    top, total, acc = lax.fori_loop(
        info[2 + slot_now],
        last + 1,
        one,
        (
            jnp.full((1, WIDE), MASKED, jnp.float32),
            jnp.zeros((1, WIDE), jnp.float32),
            jnp.zeros((HEAD_SIZE, WIDE), jnp.float32),
        ),
    )
    out = acc / total
    out = jnp.concatenate([out[:, h * ROWS : (h + 1) * ROWS] for h in range(HEADS)], axis=0)
    o_ref[...] = out.astype(jnp.bfloat16)
    lse_ref[0] = top + jnp.log(total)
    if first_call:

        @pl.when(step == 0)
        def _():
            for copy in copies:
                copy.wait()

    product = dot(out.T.astype(jnp.bfloat16), wall_ref[...], 1, 0).astype(jnp.bfloat16)
    for s, ref in enumerate(outs):

        @pl.when(step == s)
        def _(ref=ref):
            ref[...] = product


def attend_back_kernel(slots, info, q_ref, *refs):
    count = len(slots)
    d_refs, refs = refs[:count], refs[count:]
    wall_ref, o_ref, lse_ref, kv_ref, kvt_ref, start_ref, cos_ref, sin_ref, *refs = refs
    last_call = slots[-1] == 2
    if last_call:
        before_ref, gq_ref, *g_refs, gkv_ref, dh_ref = refs
    else:
        gq_ref, gkv_ref, dh_ref = refs
    step = pl.program_id(0)

    @pl.when(step == 0)
    def _():
        if last_call:
            gkv_ref[...] = before_ref[...]
        else:
            gkv_ref[...] = jnp.zeros_like(gkv_ref)
        for s, ref in enumerate(d_refs):
            dh_ref[s] = ref[...]

    slot_now = slot_of(slots, step)
    z, y, last, rows, start = mask_parts(info, start_ref[0], slot_now)
    query = heads_side_by_side(q_ref[...])
    grad = dot(wall_ref[...], dh_ref[step], 1, 1).astype(jnp.bfloat16)
    grad = heads_side_by_side(grad)
    out = heads_side_by_side(o_ref[...])
    rowdot = jnp.sum(grad.astype(jnp.float32) * out.astype(jnp.float32), axis=0, keepdims=True)
    query = jnp.concatenate([query, jnp.zeros_like(query)], axis=0)
    grad = jnp.concatenate([jnp.zeros_like(grad), grad], axis=0)
    lse = lse_ref[0]

    def one(block, acc):
        slot = block_slot(block, z, y)
        kv = kv_ref[slot]
        scores = dot(kv, query, 1, 0)
        key = block * ROWS + lax.broadcasted_iota(jnp.int32, (ROWS, 1), 0)
        probs = jnp.where((key >= start) & (key <= rows), jnp.exp(scores - lse), 0.0)
        grad_probs = dot(kv, grad, 1, 0)
        grad_scores = (probs * (grad_probs - rowdot)).astype(jnp.bfloat16)
        gkv_ref[slot] += dot(grad_scores, query, 1, 1) + dot(
            probs.astype(jnp.bfloat16), grad, 1, 1
        )
        return acc + dot(kvt_ref[slot, :HEAD_SIZE], grad_scores, 1, 0)

    acc = lax.fori_loop(
        info[2 + slot_now], last + 1, one, jnp.zeros((HEAD_SIZE, WIDE), jnp.float32)
    )
    acc = acc * HEAD_SIZE**-0.5
    acc = jnp.concatenate([acc[:, h * ROWS : (h + 1) * ROWS] for h in range(HEADS)], axis=0)
    gq_ref[...] = rope(acc, cos_ref[...], -sin_ref[...]).astype(jnp.bfloat16)

    if last_call:

        @pl.when(step == count - 1)
        def _():
            for t, ref in enumerate(g_refs):
                for s in range(RING):
                    ref[s * ROWS : (s + 1) * ROWS, :] = gkv_ref[t * RING + s].astype(jnp.bfloat16)


def input_back_kernel(
    info, gq_ref, k0, k1, k2, k3, w_ref, x0, x1, x2, x3, cos_ref, sin_ref, n_ref, gain_two_ref,
    scale_ref, h0, h1, h2, h3, p0, p1, p2, p3, keep_ref, send_ref, row_ref, gkv_ref,
):
    for out, ref in zip((p0, p1, p2, p3), (h0, h1, h2, h3)):
        out[ROWS:] = ref[...]
    y, x, core = info[1], info[6], info[7]
    total = sum(ref[...].astype(jnp.float32) for ref in (k0, k1, k2, k3)).T
    key = rope(total[:HEAD_SIZE], cos_ref[...], -sin_ref[...])
    gkv_ref[...] = jnp.concatenate([key, total[HEAD_SIZE:]], axis=0).astype(jnp.bfloat16)
    row_ref[:, : 4 * ROWS] = gq_ref[...].T
    row_ref[:, 4 * ROWS :] = gkv_ref[...].T
    gains = []
    for xc in range(CHUNKS):
        columns = slice(xc * CHUNK, (xc + 1) * CHUNK)
        product = dot(row_ref[...], w_ref[:, columns], 1, 0)
        gain = jnp.zeros((1, CHUNK), jnp.float32)
        for s, (ref, inputs) in enumerate(zip((p0, p1, p2, p3), (x0, x1, x2, x3))):
            piece = product[s * ROWS : (s + 1) * ROWS]
            ref[:ROWS, columns] = piece.astype(jnp.bfloat16)
            scale = scale_ref[s * ROWS : (s + 1) * ROWS, :1]
            unit = inputs[:, columns].astype(jnp.float32) * scale
            gain += jnp.sum(piece * unit, axis=0, keepdims=True)
        gains.append(gain)
    gains_two = [gain_two_ref[:, xc * CHUNK : (xc + 1) * CHUNK] for xc in range(CHUNKS)]
    gains = sum(
        dot(jnp.concatenate(rows, axis=0).astype(jnp.bfloat16), gain_spread(which, True), 1, 0)
        for which, rows in enumerate((gains, gains_two))
    )
    kv_all = dot(gkv_ref[...], n_ref[...], 1, 0)
    for xc in range(CHUNKS):
        kv = kv_all[:, xc * CHUNK : (xc + 1) * CHUNK].T
        for home in range(RING):
            halves = [
                jnp.concatenate(
                    [
                        kv[z * 64 + home * 16 : z * 64 + home * 16 + 16]
                        for z in (2 * side, 2 * side + 1)
                    ],
                    axis=0,
                )
                for side in range(2)
            ]
            piece = jnp.broadcast_to(gains[xc : xc + 1, home * 128 : (home + 1) * 128], (16, 128))
            piece = jnp.concatenate(
                [jnp.concatenate(halves, axis=1), jnp.concatenate([piece, piece], axis=1)], axis=0
            ).astype(jnp.bfloat16)
            slots = turned(x, xc // 2), turned(y, home)

            @pl.when(core == xc % 2)
            def _(slots=slots, piece=piece):
                keep_ref[slots[0], slots[1]] = piece

            @pl.when(core != xc % 2)
            def _(slots=slots, piece=piece):
                send_ref[slots[0], slots[1]] = piece


def grad_output_query_kernel(info, o_ref, gq_ref, d0, d1, d2, d3, n_ref, keep_ref, send_ref):
    y, core = info[1], info[7]
    for c, out in ((core, keep_ref), (1 - core, send_ref)):
        columns = place_of(c, CHUNK)
        rows = jnp.concatenate([ref[:, columns] for ref in (d0, d1, d2, d3)], axis=0)
        grad_output = dot(o_ref[...], rows, 1, 0).astype(jnp.bfloat16)
        grad_query = dot(gq_ref[...], n_ref[:, columns], 1, 0).astype(jnp.bfloat16)
        for home in range(RING):
            slot = turned(y, home)
            out[0, slot, :ROWS] = part(grad_output, home, ROWS)
            out[0, slot, ROWS:] = part(grad_query, home, ROWS)


def feed_kernel(
    info, n0, n1, d0, d1, w_hbm, keep_ref, send_ref, h_ref, p0, p1,
    gu_ref, down_ref, n_ref, d_ref, hg_ref, row_ref, slot_ref, sems, slot_sems,
):
    units = gu_ref.shape[2]
    half = units // 2
    first = info[7] == 0

    def fetch(xc, y):
        columns = pl.ds(xc * CHUNK, CHUNK)
        return (
            pltpu.make_async_copy(
                w_hbm.at[xc, y, pl.ds(0, 2)], gu_ref.at[y, :, :, columns], sems.at[0, y, xc]
            ),
            pltpu.make_async_copy(w_hbm.at[xc, y, 2], down_ref.at[y, :, columns], sems.at[1, y, xc]),
        )

    slots = [
        pltpu.make_async_copy(ref, slot_ref.at[i], slot_sems.at[i])
        for i, ref in enumerate((n0, n1, d0, d1))
    ]
    for copy in slots:
        copy.start()
    for y in range(2):
        for xc in range(CHUNKS):
            for copy in fetch(xc, y):
                copy.start()
    for i, copy in enumerate(slots):
        copy.wait()
        out = (n_ref, d_ref)[i // 2]
        out[:, i % 2 * ROWS : (i % 2 + 1) * ROWS] = slot_ref[i].T

    def one(y, _):
        @pl.when(y < RING - 2)
        def _():
            for xc in range(CHUNKS):
                for copy in fetch(xc, y + 2):
                    copy.start()

        for xc in range(CHUNKS):
            for copy in fetch(xc, y):
                copy.wait()
        gate_up = dot(gu_ref[y].reshape(2 * units, MODEL_WIDTH), n_ref[...], 1, 0)
        grad_hidden = dot(down_ref[y], d_ref[...], 1, 0)
        gate, upper = gate_up[:units], gate_up[units:]
        sig = 1.0 / (1.0 + jnp.exp(-gate))
        silu = gate * sig
        grad_gate = grad_hidden * upper * (sig + silu * (1.0 - sig))
        grad_up = grad_hidden * silu
        hidden = silu * upper
        hg_ref[y, 0] = grad_gate.astype(jnp.bfloat16)
        hg_ref[y, 1] = grad_up.astype(jnp.bfloat16)
        h_ref[y] = hidden.astype(jnp.bfloat16)
        for k, value in enumerate((grad_gate, grad_up, hidden)):
            low, high = value[:half], value[half:]
            keep_ref[y, k] = jnp.where(first, low, high).astype(jnp.bfloat16)
            send_ref[y, k] = jnp.where(first, high, low).astype(jnp.bfloat16)
        return 0

    lax.fori_loop(0, RING, one, 0)
    row_ref[...] = hg_ref[...].reshape(RING * 2 * units, 2 * ROWS).T

    def back(i, _):
        columns = place_of(i, 2 * CHUNK)
        weights = gu_ref[:, :, :, columns].reshape(RING * 2 * units, 2 * CHUNK)
        total = dot(row_ref[...], weights, 1, 0).astype(jnp.bfloat16)
        p0[:, columns], p1[:, columns] = total[:ROWS], total[ROWS:]
        return 0

    lax.fori_loop(0, CHUNKS // 2, back, 0)


def half_rows(refs):
    return jnp.concatenate([refs[s][...] for s in HALVES], axis=0)


def feed_grad_kernel(
    keep0, keep1, other0, other1, n0, n1, n2, n3, n_other, d0, d1, d2, d3, d_other, g_hbm, gu_ref, down_ref, g_ref, sems
):
    units = keep0.shape[2]
    step = pl.program_id(0)

    @pl.when(step == 0)
    def _():
        for index, ref in enumerate((keep0, keep1, other0, other1)):
            columns = slice(index * 2 * ROWS, (index + 1) * 2 * ROWS)
            gu_ref[:, columns] = ref[:, :2].reshape(RING * 2 * units, 2 * ROWS)
            down_ref[:, columns] = ref[:, 2].reshape(RING * units, 2 * ROWS)

    rows = jnp.concatenate([half_rows((n0, n1, n2, n3)), n_other[...]], axis=0)
    grad = dot(gu_ref[...], rows, 1, 0).astype(jnp.bfloat16)
    g_ref[step, :, :2] = grad.reshape(RING, 2, units, 2 * CHUNK)
    rows = jnp.concatenate([half_rows((d0, d1, d2, d3)), d_other[...]], axis=0)
    grad = dot(down_ref[...], rows, 1, 0).astype(jnp.bfloat16)
    g_ref[step, :, 2] = grad.reshape(RING, units, 2 * CHUNK)
    pltpu.make_async_copy(g_ref.at[step], g_hbm.at[step], sems.at[step]).start()

    @pl.when(step == RING - 1)
    def _():
        for x in range(RING):
            pltpu.make_async_copy(g_ref.at[x], g_hbm.at[x], sems.at[x]).wait()


def feed_down_kernel(h0_ref, h1_ref, w_hbm, p0, p1, p2, p3, row_ref, w_ref, sems):
    units = h0_ref.shape[1]
    copies = [
        [
            pltpu.make_async_copy(
                w_hbm.at[xc, y, 2],
                w_ref.at[xc // 2, pl.ds(y * units, units), pl.ds(xc % 2 * CHUNK, CHUNK)],
                sems.at[xc, y],
            )
            for xc in (2 * step, 2 * step + 1)
            for y in range(RING)
        ]
        for step in range(CHUNKS // 2)
    ]
    for group in copies:
        for copy in group:
            copy.start()
    for half, ref in enumerate((h0_ref, h1_ref)):
        row_ref[half * 2 * ROWS : (half + 1) * 2 * ROWS] = (
            ref[...].reshape(RING * units, 2 * ROWS).T
        )
    for step, group in enumerate(copies):
        for copy in group:
            copy.wait()
        total = dot(row_ref[...], w_ref[step], 1, 0).astype(jnp.bfloat16)
        for index, ref in enumerate((p1, p3, p0, p2)):
            ref[:, step * 2 * CHUNK : (step + 1) * 2 * CHUNK] = part(total, index, ROWS)


def whole(shape):
    return pl.BlockSpec(shape, lambda *_: (0,) * len(shape))


def struct(shape, dtype=jnp.bfloat16):
    return jax.ShapeDtypeStruct(shape, dtype)


def cost(flops, moved, exps=0):
    return pl.CostEstimate(flops=flops, bytes_accessed=moved, transcendentals=exps)


def params(mebibytes):
    return pltpu.CompilerParams(vmem_limit_bytes=mebibytes << 20)


SLOT = (ROWS, MODEL_WIDTH)
SPLIT = ((1, 3), (0, 2))
SPLIT_BACK = ((0, 1, 3), (2,))


def columns_of(slots, rows):
    return pl.BlockSpec((rows, ROWS), lambda s, info: (0, slot_of(slots, s)))


def row_of(slots, width):
    return pl.BlockSpec((1, 1, width), lambda s, info: (slot_of(slots, s), 0, 0))


def hbm(value):
    return pltpu.with_memory_space_constraint(value, pltpu.HBM)


def project_qkv(info, x_slots, pack, k_slots, k_other, cosine, sine):
    return pl.pallas_call(
        qkv_kernel,
        grid_spec=pltpu.PrefetchScalarGridSpec(
            num_scalar_prefetch=1,
            grid=(1,),
            in_specs=[whole(SLOT)] * 4
            + [pl.BlockSpec(memory_space=pltpu.HBM)]
            + [whole((RING, 48, CHUNK))] * 4
            + [whole((RING, RING, 48, CHUNK))]
            + [whole((32, TOKENS))] * 2,
            out_specs=[
                whole((TOKENS, MODEL_WIDTH)),
                whole((512, TOKENS)),
                whole((TOKENS, 128)),
                whole((640, MODEL_WIDTH)),
                whole((2, MODEL_WIDTH)),
                whole((TOKENS, 128)),
            ],
            scratch_shapes=[
                pltpu.VMEM((CHUNKS, CHUNK, 128), jnp.bfloat16),
                pltpu.VMEM((CHUNKS, RING, 16, 128), jnp.float32),
                pltpu.SemaphoreType.DMA((CHUNKS, RING)),
            ],
        ),
        out_shape=[
            struct((TOKENS, MODEL_WIDTH)),
            struct((512, TOKENS)),
            struct((TOKENS, 128)),
            struct((640, MODEL_WIDTH)),
            struct((2, MODEL_WIDTH), jnp.float32),
            struct((TOKENS, 128), jnp.float32),
        ],
        compiler_params=params(32),
        cost_estimate=cost(2 * 640 * TOKENS * MODEL_WIDTH, 9 << 20),
        name="project_qkv",
    )(info, *map(hbm, x_slots), hbm(pack), *k_slots, k_other, cosine, sine)


def attend(slots, info, q_t, kv, starts, pack=None, shared=()):
    count = len(slots)
    walls = [whole((512, MODEL_WIDTH)), whole((BLOCKS, 128, ROWS))]
    shapes = [struct((512, MODEL_WIDTH)), struct((BLOCKS, 128, ROWS))]
    return pl.pallas_call(
        functools.partial(attend_kernel, slots),
        grid_spec=pltpu.PrefetchScalarGridSpec(
            num_scalar_prefetch=1,
            grid=(count,),
            in_specs=[columns_of(slots, 512), whole((BLOCKS, ROWS, 128)), row_of(slots, ROWS)]
            + (walls if shared else [pl.BlockSpec(memory_space=pltpu.HBM)]),
            out_specs=[
                pl.BlockSpec((512, ROWS), lambda s, info: (0, s)),
                pl.BlockSpec((1, 1, WIDE), lambda s, info: (s, 0, 0)),
            ]
            + [whole(SLOT)] * count
            + ([] if shared else walls),
            scratch_shapes=[] if shared else [pltpu.SemaphoreType.DMA((CHUNKS, RING))],
        ),
        out_shape=[struct((512, count * ROWS)), struct((count, 1, WIDE), jnp.float32)]
        + [struct(SLOT)] * count
        + ([] if shared else shapes),
        compiler_params=params(16),
        cost_estimate=cost(
            count * HEADS * TOKENS * 640 * 128 + count * 512 * ROWS * 2 * MODEL_WIDTH,
            6 << 20,
            count * HEADS * ROWS * 640,
        ),
        name="attend",
    )(info, q_t, kv, starts, *(shared or [hbm(pack)]))


def attend_back(
    slots, info, q_t, dh_slots, wall, o_t, lse, kv, kv_t, starts, cosine, sine, before=None
):
    count = len(slots)
    sums = (BLOCKS, ROWS, 128)
    out_specs = [pl.BlockSpec((512, ROWS), lambda s, info: (0, s))]
    out_shape = [struct((512, count * ROWS))]
    scratch_shapes = []
    if before is None:
        out_specs += [whole(sums)]
        out_shape += [struct(sums, jnp.float32)]
    else:
        out_specs += [whole((TOKENS, 128))] * 4
        out_shape += [struct((TOKENS, 128))] * 4
        scratch_shapes += [pltpu.VMEM(sums, jnp.float32)]
    return pl.pallas_call(
        functools.partial(attend_back_kernel, slots),
        grid_spec=pltpu.PrefetchScalarGridSpec(
            num_scalar_prefetch=1,
            grid=(count,),
            in_specs=[columns_of(slots, 512)]
            + [whole(SLOT)] * count
            + [
                whole((512, MODEL_WIDTH)),
                columns_of(slots, 512),
                row_of(slots, WIDE),
                whole((BLOCKS, ROWS, 128)),
                whole((BLOCKS, 128, ROWS)),
                row_of(slots, ROWS),
                columns_of(slots, HEAD_SIZE // 2),
                columns_of(slots, HEAD_SIZE // 2),
            ]
            + ([] if before is None else [whole(sums)]),
            out_specs=out_specs,
            scratch_shapes=scratch_shapes + [pltpu.VMEM((count, *SLOT), jnp.bfloat16)],
        ),
        out_shape=out_shape,
        compiler_params=params(18),
        cost_estimate=cost(
            3 * count * HEADS * ROWS * 640 * 128 * 4 + count * 512 * ROWS * 2 * MODEL_WIDTH,
            8 << 20,
            count * HEADS * ROWS * 640,
        ),
        name="attend_back",
    )(
        info, q_t, *dh_slots, wall, o_t, lse, kv, kv_t, starts, cosine, sine,
        *([] if before is None else [before]),
    )


def input_back(info, gq_t, gkv_slots, w_qkv, x_slots, cosine, sine, normed, gain_two, scales, down):
    pieces = (RING, RING, 48, CHUNK)
    return pl.pallas_call(
        input_back_kernel,
        grid_spec=pltpu.PrefetchScalarGridSpec(
            num_scalar_prefetch=1,
            grid=(1,),
            in_specs=[whole((512, TOKENS))]
            + [whole((TOKENS, 128))] * 4
            + [whole((640, MODEL_WIDTH))]
            + [whole(SLOT)] * 4
            + [whole((32, TOKENS))] * 2
            + [whole((TOKENS, MODEL_WIDTH)), whole((1, MODEL_WIDTH)), whole((TOKENS, 128))]
            + [whole(SLOT)] * 4,
            out_specs=[whole((2 * ROWS, MODEL_WIDTH))] * 4 + [whole(pieces)] * 2,
            scratch_shapes=[
                pltpu.VMEM((TOKENS, 640), jnp.bfloat16),
                pltpu.VMEM((128, TOKENS), jnp.bfloat16),
            ],
        ),
        out_shape=[pltpu.HBM((2 * ROWS, MODEL_WIDTH), jnp.bfloat16)] * 4 + [struct(pieces)] * 2,
        compiler_params=params(32),
        cost_estimate=cost(2 * 768 * TOKENS * MODEL_WIDTH, 15 << 20),
        name="input_back",
    )(
        info, gq_t, *gkv_slots, w_qkv, *map(hbm, x_slots), cosine, sine, normed, gain_two, scales, *down,
    )


def pack_specs(rows):
    spec = pl.BlockSpec((1, RING, rows, CHUNK), lambda s, info: (s, 0, 0, 0))
    return [spec, spec], [struct((RING, RING, rows, CHUNK))] * 2


def pair_columns(rows):
    return pl.BlockSpec((rows, 2 * CHUNK), lambda s, info: (0, (info[6] + RING - s) % RING))


def grad_output_query(info, o_t, gq_t, dh_slots, normed):
    out_specs, out_shape = pack_specs(2 * ROWS)
    return pl.pallas_call(
        grad_output_query_kernel,
        grid_spec=pltpu.PrefetchScalarGridSpec(
            num_scalar_prefetch=1,
            grid=(RING,),
            in_specs=[whole((512, TOKENS))] * 2
            + [pair_columns(ROWS)] * 4
            + [pair_columns(TOKENS)],
            out_specs=out_specs,
        ),
        out_shape=out_shape,
        compiler_params=params(14),
        cost_estimate=cost(4 * 512 * TOKENS * MODEL_WIDTH, 9 << 20),
        name="grad_output_query",
    )(info, o_t, gq_t, *dh_slots, normed)


def feed(info, n_pair, d_pair, weights):
    units = weights.shape[3]
    pair = (2 * ROWS, MODEL_WIDTH)
    split = (RING, 3, units // 2, 2 * ROWS)
    return pl.pallas_call(
        feed_kernel,
        in_specs=[pl.BlockSpec(memory_space=pltpu.SMEM)]
        + [pl.BlockSpec(memory_space=pl.ANY)] * 4
        + [pl.BlockSpec(memory_space=pltpu.HBM)],
        out_specs=[pl.BlockSpec(memory_space=pltpu.VMEM)] * 5,
        out_shape=[struct(split)] * 2 + [struct((RING, units, 2 * ROWS))] + [struct(SLOT)] * 2,
        scratch_shapes=[
            pltpu.VMEM((RING, 2, units, MODEL_WIDTH), jnp.bfloat16),
            pltpu.VMEM((RING, units, MODEL_WIDTH), jnp.bfloat16),
            pltpu.VMEM(pair[::-1], jnp.bfloat16),
            pltpu.VMEM(pair[::-1], jnp.bfloat16),
            pltpu.VMEM((RING, 2, units, 2 * ROWS), jnp.bfloat16),
            pltpu.VMEM((2 * ROWS, RING * 2 * units), jnp.bfloat16),
            pltpu.VMEM((4, *SLOT), jnp.bfloat16),
            pltpu.SemaphoreType.DMA((2, RING, CHUNKS)),
            pltpu.SemaphoreType.DMA((4,)),
        ],
        compiler_params=params(30),
        cost_estimate=cost(5 * RING * units * TOKENS * MODEL_WIDTH, 23 << 20, RING * units * TOKENS // 2),
        name="feed",
    )(info, *map(hbm, n_pair), *map(hbm, d_pair), hbm(weights))


def feed_grad(keeps, others, n_slots, n_other, d_slots, d_other):
    units = keeps[0].shape[2]
    slots = [pl.BlockSpec((ROWS, 2 * CHUNK), lambda i: (0, i))] * 4
    slots += [pl.BlockSpec((TOKENS, 2 * CHUNK), lambda i: (0, i))]
    out = (RING, RING, 3, units, 2 * CHUNK)
    return pl.pallas_call(
        feed_grad_kernel,
        grid=(RING,),
        in_specs=[whole(keeps[0].shape)] * 4 + slots * 2,
        out_specs=pl.BlockSpec(memory_space=pltpu.HBM),
        out_shape=pltpu.HBM(out, jnp.bfloat16),
        scratch_shapes=[
            pltpu.VMEM((RING * 2 * units, 2 * TOKENS), jnp.bfloat16),
            pltpu.VMEM((RING * units, 2 * TOKENS), jnp.bfloat16),
            pltpu.VMEM(out, jnp.bfloat16),
            pltpu.SemaphoreType.DMA((RING,)),
        ],
        compiler_params=params(30),
        cost_estimate=cost(12 * RING * units * TOKENS * MODEL_WIDTH, 22 << 20),
        name="feed_grad",
    )(*keeps, *others, *map(hbm, n_slots), hbm(n_other), *map(hbm, d_slots), hbm(d_other))


def feed_down(hs, weights):
    units = hs[0].shape[1]
    return pl.pallas_call(
        feed_down_kernel,
        in_specs=[pl.BlockSpec(memory_space=pltpu.VMEM)] * 2 + [pl.BlockSpec(memory_space=pltpu.HBM)],
        out_specs=[pl.BlockSpec(memory_space=pltpu.VMEM)] * 4,
        out_shape=[struct(SLOT)] * 4,
        scratch_shapes=[
            pltpu.VMEM((TOKENS, RING * units), jnp.bfloat16),
            pltpu.VMEM((CHUNKS // 2, RING * units, 2 * CHUNK), jnp.bfloat16),
            pltpu.SemaphoreType.DMA((CHUNKS, RING)),
        ],
        compiler_params=params(18),
        cost_estimate=cost(2 * RING * units * TOKENS * MODEL_WIDTH, 9 << 20),
        name="feed_down",
    )(*hs, hbm(weights))


def swap_cores(value):
    return lax.ppermute(value, "core", [(0, 1), (1, 0)])


def scatter_core(keep, other):
    return [
        (keep[s].astype(jnp.float32) + other[s].astype(jnp.float32)).astype(jnp.bfloat16)
        for s in range(RING)
    ]


def sum_x(parts):
    return [
        sum(p[s].astype(jnp.float32) for p in parts).astype(jnp.bfloat16) for s in range(RING)
    ]


def after(values, *others):
    return lax.optimization_barrier((list(values), others))[0]


def adamw(weight, first, second, grad, rate, decay):
    first_new = BETA_ONE * first + (1.0 - BETA_ONE) * grad
    second_new = BETA_TWO * second + (1.0 - BETA_TWO) * grad * grad
    fix_one = 1.0 - BETA_ONE**STEP
    fix_two = 1.0 - BETA_TWO**STEP
    update = first_new / fix_one / (jnp.sqrt(second_new / fix_two) + ADAM_EPS)
    return (weight - rate * (update + decay * weight), first_new, second_new)


def local(
    block_input,
    out_grad,
    segments,
    w_query,
    keyvalue_weights,
    w_output,
    w_gateup,
    w_down,
    norm_gains,
    query_first,
    keyval_moment_one,
    output_first,
    gateup_first,
    down_first,
    gains_first,
    query_second,
    keyval_moment_two,
    output_second,
    gateup_second,
    down_second,
    gains_second,
):
    bf16, f32 = jnp.bfloat16, jnp.float32
    x, core, z, y = (lax.axis_index(name) for name in ("x", "core", "z", "y"))
    units = w_down.shape[0]

    kv_rows = keyvalue_weights.astype(bf16).reshape(2, 16, RING, HEAD_SIZE).transpose(2, 1, 0, 3)
    message = jnp.concatenate(
        [
            kv_rows.reshape(RING, 16, 128),
            jnp.broadcast_to(
                jnp.pad(norm_gains.astype(bf16).reshape(1, 1, 32), ((0, 0), (0, 15), (0, 96))),
                (RING, 16, 128),
            ),
        ],
        1,
    )
    small = absolute(scatter_ring_from(relative(message, z), "z"), z)
    kv_piece = jnp.concatenate(
        [small[:2, :16].reshape(32, 128), small[2:, :16].reshape(32, 128)], 1
    )
    gain_piece = jnp.pad(small[:, 16, :32].reshape(1, 128), ((0, 15), (0, 128)))
    kv_piece = jnp.concatenate([kv_piece, gain_piece], 0)

    pack = jnp.concatenate([w_output.astype(bf16), w_query.astype(bf16).T], 0)
    pack = lax.all_gather(pack, SHARE, axis=0, tiled=False)
    x_slots = gather_far_last(block_input, "z")
    (kv_piece,) = after([jnp.stack(gather_ring(kv_piece, "x"))], x_slots[1], x_slots[3])
    k_slots = gather_ring(kv_piece, "y")
    k_other = swap_cores(jnp.stack(after(k_slots, x_slots[2])))
    d_slots = gather_far_last(after([out_grad], *x_slots[1:])[0], "z")
    feed_shard = jnp.concatenate(
        [w_gateup.astype(bf16).transpose(0, 2, 1), w_down.astype(bf16)[None]], 0
    )
    (feed_shard,) = after([feed_shard], pack, d_slots[1], d_slots[3], k_other)
    w_feed = lax.all_gather(feed_shard, SHARE, axis=0, tiled=False)
    w_feed = w_feed.reshape(CHUNKS, RING, 3, units, CHUNK)

    starts = doc_starts(segments[0])
    by_block = lax.dynamic_index_in_dim(starts.reshape(RING, RING, ROWS), y, 1, keepdims=False)
    row_starts = jnp.stack(relative(by_block, z))
    places = (z + RING - jnp.arange(RING, dtype=jnp.int32)) % RING
    begins = places * (RING * ROWS) + y * ROWS
    positions = (begins[:, None] + jnp.arange(ROWS, dtype=jnp.int32) - row_starts).reshape(-1)
    half = HEAD_SIZE // 2
    freqs = 10000.0 ** (-jnp.arange(half, dtype=f32) * 2.0 / HEAD_SIZE)
    angles = freqs[:, None] * positions.astype(f32)[None, :]
    cosine, sine = jnp.cos(angles), jnp.sin(angles)
    info = jnp.concatenate(
        [
            jnp.stack([z, y]).astype(jnp.int32),
            row_starts[:, 0] // ROWS,
            jnp.stack([x, core]).astype(jnp.int32),
        ]
    )
    row_starts = row_starts[:, None, :]

    normed, q_t, kv_own, w_qkv, gains, scales = project_qkv(
        info, x_slots, pack, k_slots, k_other, cosine, sine
    )
    kv = jnp.stack(gather_ring(kv_own, "y")).reshape(BLOCKS, ROWS, 2 * HEAD_SIZE)
    near_o, near_lse, o_1, o_3, *shared = attend(SPLIT[0], info, q_t, kv, row_starts, pack)
    wo, kv_t = shared
    (q_late,) = after([q_t], o_1, d_slots[2])
    far_o, far_lse, o_0, o_2 = attend(SPLIT[1], info, q_late, kv, row_starts, shared=shared)
    o_t = jnp.concatenate(
        [far_o[:, :ROWS], near_o[:, :ROWS], far_o[:, ROWS:], near_o[:, ROWS:]], 1
    )
    lse = jnp.stack([far_lse[0], near_lse[0], far_lse[1], near_lse[1]])
    o_1, o_3 = after([o_1, o_3], d_slots[2])
    d_other = swap_cores(jnp.concatenate(after([d_slots[s] for s in HALVES], o_1), 0))
    o_sum = sum(p.astype(f32) for p in scatter_far_last(o_0, o_1, o_3, o_2, "z"))
    h1 = block_input.astype(f32) + o_sum

    scale_two = rms_scale(h1)
    unit_two = h1 * scale_two
    (normed_two,) = after([(unit_two * gains[1]).astype(bf16)], d_other)
    n_slots = gather_far_last(normed_two, "z")
    keep0, send0, h0, gn2_1, gn2_3 = feed(
        info, [n_slots[s] for s in HALVES[:2]], [d_slots[s] for s in HALVES[:2]], w_feed
    )
    n_other = after([n_slots[s] for s in HALVES], keep0)
    n_other = swap_cores(jnp.concatenate(n_other, 0))
    keep1, send1, h1_half, gn2_0, gn2_2 = feed(
        info, after([n_slots[s] for s in HALVES[2:]], keep0), [d_slots[s] for s in HALVES[2:]], w_feed
    )
    gn2_slots = scatter_ring([gn2_0, gn2_1, gn2_2, gn2_3], "z")
    other0 = swap_cores(send0)
    (send1,) = after([send1], n_other, other0, gn2_slots[1], gn2_slots[3])
    others = other0, swap_cores(send1)
    grad_feed = feed_grad((keep0, keep1), others, n_slots, n_other, d_slots, d_other)
    *gn2_slots, grad_feed = after([*gn2_slots, grad_feed])
    gn2 = sum(p.astype(f32) for p in gn2_slots)
    grad_gain_two = jnp.sum(gn2 * unit_two, 0, keepdims=True)
    dh1 = out_grad.astype(f32) + norm_back(unit_two, scale_two, gains[1], gn2)
    own_feed = lax.psum_scatter(
        grad_feed.reshape(16, 3, units // 2, 2 * CHUNK), ("x", "y"), scatter_dimension=0, tiled=False
    )

    down_slots = feed_down(after([h0, h1_half], *gn2_slots), w_feed)
    dh_slots = gather_far_last(dh1.astype(bf16), "z", *down_slots)
    near, far = SPLIT_BACK
    arguments = wo, o_t, lse, kv, kv_t, row_starts, cosine, sine
    gq_near, sums = attend_back(near, info, q_t, [dh_slots[s] for s in near], *arguments)
    (dh_far,) = after([dh_slots[2]], sums)
    gq_far, *gkv_slots = attend_back(far, info, q_t, [dh_far], *arguments, before=sums)
    gq_t = jnp.concatenate([gq_near[:, : 2 * ROWS], gq_far, gq_near[:, 2 * ROWS :]], 1)
    gkv_slots = scatter_ring(gkv_slots, "y")
    (gq_late,) = after([gq_t], gkv_slots[1], gkv_slots[3])
    keep, send = grad_output_query(info, o_t, gq_late, dh_slots, normed)
    (send,) = after([send], gkv_slots[2])
    gkv_slots = after(gkv_slots, send)
    *gn1_slots, keep_kv, send_kv = input_back(
        info, gq_t, gkv_slots, w_qkv, x_slots, cosine, sine, normed, grad_gain_two, scales, down_slots
    )
    gn1_0, gn1_1, gn1_2, gn1_3 = gn1_slots
    gn1_slots = scatter_far_last(gn1_0, gn1_1, gn1_3, gn1_2, "z")
    parts = zip(scatter_core(keep, swap_cores(send)), scatter_core(keep_kv, swap_cores(send_kv)))
    parts = scatter_ring([jnp.concatenate(p, 1) for p in parts], "x")

    parts_y = scatter_ring(sum_x(parts), "y")
    own_pack = sum(p.astype(f32) for p in parts_y)

    (own_feed,) = after([own_feed], parts_y[1])
    own_feed = jnp.stack([own_feed[..., :CHUNK], own_feed[..., CHUNK:]])
    kept = lax.dynamic_index_in_dim(own_feed, core, 0, keepdims=False)
    other = swap_cores(lax.dynamic_index_in_dim(own_feed, 1 - core, 0, keepdims=False))
    own_feed = jnp.where(
        core == 0, jnp.concatenate([kept, other], 1), jnp.concatenate([other, kept], 1)
    ).astype(f32)
    rate = MODEL_WIDTH ** (-0.5)
    own_gu = own_feed[:2].transpose(0, 2, 1)
    gu = adamw(w_gateup, gateup_first, gateup_second, own_gu, rate, DECAY)
    down = adamw(w_down, down_first, down_second, own_feed[2], FF ** (-0.5), DECAY)

    kv_piece = own_pack[2 * ROWS : 2 * ROWS + 32]
    kv_piece = jnp.concatenate([kv_piece[:, :128], kv_piece[:, 128:]], 0).reshape(RING, 16, 128)
    gain_piece = own_pack[2 * ROWS + 32, :128].reshape(RING, 1, 32)
    message = jnp.concatenate([kv_piece, jnp.pad(gain_piece, ((0, 0), (0, 15), (0, 96)))], 1)
    small = scatter_ring_from(relative(message, z), "z")
    own_o, own_q = after([own_pack[:ROWS], own_pack[ROWS : 2 * ROWS].T], small[1])
    last = sum(p.astype(f32) for p in after(gn1_slots, *parts_y[1:]))
    gn1 = last[:ROWS]
    result = (h1 + last[ROWS:]).astype(bf16)
    own_inputs = block_input.astype(f32)
    scale_one = rms_scale(own_inputs)
    grad_input = (dh1 + norm_back(own_inputs * scale_one, scale_one, gains[0], gn1)).astype(bf16)
    small = absolute(small, z)
    own_kv = small[:, :16].reshape(RING, 16, 2, HEAD_SIZE).transpose(2, 1, 0, 3)
    own_kv = own_kv.reshape(2, 16, RING * HEAD_SIZE)
    own_gains = jnp.sum(small[:, 16, :32], 0).reshape(2, 16)

    q = adamw(w_query, query_first, query_second, own_q, rate, DECAY)
    kvs = adamw(keyvalue_weights, keyval_moment_one, keyval_moment_two, own_kv, rate, DECAY)
    o = adamw(w_output, output_first, output_second, own_o, (MODEL_WIDTH // 64) ** (-0.5), DECAY)
    gain = adamw(norm_gains, gains_first, gains_second, own_gains, GAIN_RATE, 0.0)
    updates = (q, kvs, o, gu, down, gain)
    return (result, grad_input, *(u[i] for i in range(3) for u in updates))


def scatter_ring_from(slots, axis):
    own, after, far, before = scatter_ring(slots, axis)
    return [own, before, far, after]


def solution(mesh):
    view = Mesh(mesh.devices.reshape(4, 2, 4, 4), ("x", "core", "z", "y"))
    dp, tensor = ("x", "core"), ("z", "y")
    both = dp + tensor
    tokens = P(both, None)
    weights = (
        P(dp, tensor),
        P(None, both, None),
        P(tensor, dp),
        P(None, dp, tensor),
        P(tensor, dp),
        P(None, both),
    )
    return jax.shard_map(
        local,
        mesh=view,
        in_specs=(tokens, tokens, P(dp, None), *weights * 3),
        out_specs=(tokens, tokens, *weights * 3),
        check_vma=False,
    )
```

```python
import functools

import jax
import jax.numpy as jnp
from jax import lax
from jax.experimental import pallas as pl
from jax.experimental.pallas import tpu as pltpu
from jax.sharding import Mesh
from jax.sharding import PartitionSpec as P

MODEL_WIDTH = 2048
QUERY_HEADS = 32
KEYVALUE_HEADS = 4
HEAD_SIZE = 64
FF = 5632
STEP = 10

BETA_ONE = 0.9
BETA_TWO = 0.95
ADAM_EPS = 1e-08
DECAY = 0.1
GAIN_RATE = 0.8
NORM_EPS = 1e-05

RING = 4
SHARE = ("x", "core", "y")
ROWS = 128
TOKENS = RING * ROWS
HEADS = QUERY_HEADS // RING
WIDE = HEADS * ROWS
BLOCKS = 16
MASKED = -1e30
HALVES = (1, 3, 0, 2)
CHUNKS, CHUNK = 8, 256
PACK = 2 * ROWS + 48


def doc_starts(segment):
    index = jnp.arange(segment.shape[0], dtype=jnp.int32)
    starts = jnp.concatenate([jnp.ones((1,), dtype=bool), segment[1:] != segment[:-1]])
    return lax.cummax(jnp.where(starts, index, 0))


def shift(value, axis, step):
    return lax.ppermute(value, axis, [(i, (i + step) % RING) for i in range(RING)])


def gather_ring(value, axis):
    far = shift(value, axis, 2)
    return [value, shift(value, axis, 1), far, shift(value, axis, 3)]


def gather_far_last(value, axis, *others):
    near = shift(value, axis, 1), shift(value, axis, 3)
    (value_late,) = after([value], *near, *others)
    return [value, near[0], shift(value_late, axis, 2), near[1]]


def scatter_far_last(own, part_one, part_three, part_two, axis):
    near = shift(part_one, axis, 3), shift(part_three, axis, 1)
    (part_two,) = after([part_two], *near)
    return [own, near[0], shift(part_two, axis, 2), near[1]]


def scatter_ring(parts, axis):
    far = shift(parts[2], axis, 2)
    return [parts[0], shift(parts[1], axis, 3), far, shift(parts[3], axis, 1)]


def absolute(slots, own):
    turned = jnp.stack([slots[0], slots[3], slots[2], slots[1]])
    return lax.dynamic_slice_in_dim(jnp.concatenate([turned, turned]), RING - own, RING, 0)


def relative(stacked, own):
    turned = jnp.concatenate([stacked, stacked])
    return [
        lax.dynamic_index_in_dim(turned, own + RING - s if s else own, 0, keepdims=False)
        for s in range(RING)
    ]


def dot(left, right, left_dim, right_dim):
    return lax.dot_general(
        left, right, (((left_dim,), (right_dim,)), ((), ())), preferred_element_type=jnp.float32
    )


def rms_scale(values):
    return lax.rsqrt(jnp.mean(values * values, axis=-1, keepdims=True) + NORM_EPS)


def norm_back(unit, scale, gain, grad):
    scaled = grad * gain
    return scale * (scaled - unit * jnp.mean(scaled * unit, axis=-1, keepdims=True))


def part(ref, index, size):
    return ref[index * size : (index + 1) * size, :]


def heads_side_by_side(value):
    return jnp.concatenate([part(value, h, HEAD_SIZE) for h in range(HEADS)], axis=1)


def mask_parts(info, starts, step):
    z, y = info[0], info[1]
    place = (z + RING - step) % RING
    begin = place * (RING * ROWS) + y * ROWS
    row = begin + lax.broadcasted_iota(jnp.int32, (1, ROWS), 1)
    rows = jnp.concatenate([row] * HEADS, axis=1)
    start = jnp.concatenate([starts] * HEADS, axis=1)
    return z, y, place * RING + y, rows, start


def block_slot(block, z, y):
    return ((y + RING - block % RING) % RING) * RING + (z + RING - block // RING) % RING


def rope(values, cosine, sine):
    half = HEAD_SIZE // 2
    out = []
    for h in range(values.shape[0] // HEAD_SIZE):
        first = values[h * HEAD_SIZE : h * HEAD_SIZE + half]
        second = values[h * HEAD_SIZE + half : (h + 1) * HEAD_SIZE]
        out += [first * cosine - second * sine, first * sine + second * cosine]
    return jnp.concatenate(out, axis=0)


def turned(place, step):
    return (place + RING - step) % RING


def weight_slots(info, own_refs, other_ref):
    y, x, core = info[1], info[6], info[7]
    for cs in range(2):
        for ys in range(RING):
            for xs in range(RING):
                ref = other_ref.at[ys, xs] if cs else own_refs[ys].at[xs]
                yield turned(x, xs) * 2 + (1 - core if cs else core), turned(y, ys), ref


def place_of(index, size):
    return pl.ds(pl.multiple_of(index * size, size), size)


def gain_spread(which, transposed):
    shape = (CHUNK, 512) if transposed else (512, CHUNK)
    lane = lax.broadcasted_iota(jnp.int32, shape, 1 if transposed else 0)
    column = lax.broadcasted_iota(jnp.int32, shape, 0 if transposed else 1)
    y, z, gain, row = lane // 128, lane // 32 % 4, lane // 16 % 2, lane % 16
    same = (column // 64 == z) & (column // 16 % 4 == y) & (column % 16 == row) & (gain == which)
    return jnp.where(same, 1.0, 0.0).astype(jnp.bfloat16)


def fetch_pack(pack_hbm, which, out_ref, sems):
    return [
        pltpu.make_async_copy(
            pack_hbm.at[xc * RING + y, pl.ds(which * ROWS, ROWS)],
            out_ref.at[pl.ds(y * ROWS, ROWS), pl.ds(xc * CHUNK, CHUNK)],
            sems.at[xc, y],
        )
        for xc in range(CHUNKS)
        for y in range(RING)
    ]


def qkv_kernel(
    info, x0, x1, x2, x3, pack_hbm, k0, k1, k2, k3, k_other, cos_ref, sin_ref,
    n_ref, q_ref, kv_ref, w_ref, gain_ref, scale_ref, wkv_ref, piece_ref, sems,
):
    copies = fetch_pack(pack_hbm, 1, w_ref, sems)
    for copy in copies:
        copy.start()
    for chunk, y, ref in weight_slots(info, (k0, k1, k2, k3), k_other):
        for z in range(RING):
            wkv_ref[chunk, pl.ds(pl.multiple_of(z * 64 + y * 16, 16), 16), :] = ref[
                (z % 2) * 16 : (z % 2 + 1) * 16, (z // 2) * 128 : (z // 2 + 1) * 128
            ]
        piece_ref[chunk, y] = ref[32:48, :128].astype(jnp.float32)
    pieces = [
        jnp.concatenate([piece_ref[xc, y, :1] for y in range(RING)], axis=1) for xc in range(CHUNKS)
    ]
    pieces = jnp.concatenate(pieces, axis=0).astype(jnp.bfloat16)
    gains = [dot(pieces, gain_spread(which, False), 1, 0) for which in range(2)]
    for xc in range(CHUNKS):
        columns = slice(xc * CHUNK, (xc + 1) * CHUNK)
        w_ref[4 * ROWS : 5 * ROWS, columns] = wkv_ref[xc].T
        for which in range(2):
            gain_ref[which : which + 1, columns] = gains[which][xc : xc + 1]
    for s, ref in enumerate((x0, x1, x2, x3)):
        value = ref[...].astype(jnp.float32)
        scale = rms_scale(value)
        scale_ref[s * ROWS : (s + 1) * ROWS] = jnp.broadcast_to(scale, (ROWS, 128))
        n_ref[s * ROWS : (s + 1) * ROWS, :] = (value * scale * gain_ref[:1]).astype(jnp.bfloat16)
    for copy in copies:
        copy.wait()
    qkv = dot(w_ref[...], n_ref[...], 1, 1)
    query = rope(qkv[: 4 * ROWS], cos_ref[...], sin_ref[...]).astype(jnp.bfloat16)
    q_ref[...] = query * jnp.bfloat16(HEAD_SIZE**-0.5)
    key = rope(qkv[4 * ROWS : 4 * ROWS + HEAD_SIZE], cos_ref[...], sin_ref[...])
    key_value = jnp.concatenate([key, qkv[4 * ROWS + HEAD_SIZE :]], axis=0)
    kv_ref[...] = key_value.T.astype(jnp.bfloat16)


def slot_of(slots, step):
    out = slots[0]
    for index in range(1, len(slots)):
        out = out + (slots[index] - slots[index - 1]) * ((step + len(slots) - index) // len(slots))
    return out


def attend_kernel(
    slots, info, q_ref, kv_ref, start_ref, *refs
):
    step = pl.program_id(0)
    first_call = 2 not in slots
    if first_call:
        pack_hbm, o_ref, lse_ref, *outs, wall_ref, kvt_ref, sems = refs
        copies = fetch_pack(pack_hbm, 0, wall_ref, sems)

        @pl.when(step == 0)
        def _():
            for copy in copies:
                copy.start()
            for b in range(BLOCKS):
                kvt_ref[b] = kv_ref[b].T
    else:
        wall_ref, kvt_ref, o_ref, lse_ref, *outs = refs

    slot_now = slot_of(slots, step)
    z, y, last, rows, start = mask_parts(info, start_ref[0], slot_now)
    query = heads_side_by_side(q_ref[...])
    query = jnp.concatenate([query, jnp.zeros_like(query)], axis=0)

    def one(block, carry):
        top, total, acc = carry
        slot = block_slot(block, z, y)
        scores = dot(kv_ref[slot], query, 1, 0)
        key = block * ROWS + lax.broadcasted_iota(jnp.int32, (ROWS, 1), 0)
        scores = jnp.where((key >= start) & (key <= rows), scores, MASKED)
        new_top = jnp.maximum(top, jnp.max(scores, axis=0, keepdims=True))
        weights = jnp.exp(scores - new_top)
        fade = jnp.exp(top - new_top)
        total = total * fade + jnp.sum(weights, axis=0, keepdims=True)
        acc = acc * fade + dot(kvt_ref[slot, HEAD_SIZE:], weights.astype(jnp.bfloat16), 1, 0)
        return new_top, total, acc

    top, total, acc = lax.fori_loop(
        info[2 + slot_now],
        last + 1,
        one,
        (
            jnp.full((1, WIDE), MASKED, jnp.float32),
            jnp.zeros((1, WIDE), jnp.float32),
            jnp.zeros((HEAD_SIZE, WIDE), jnp.float32),
        ),
    )
    out = acc / total
    out = jnp.concatenate([out[:, h * ROWS : (h + 1) * ROWS] for h in range(HEADS)], axis=0)
    o_ref[...] = out.astype(jnp.bfloat16)
    lse_ref[0] = top + jnp.log(total)
    if first_call:

        @pl.when(step == 0)
        def _():
            for copy in copies:
                copy.wait()

    product = dot(out.T.astype(jnp.bfloat16), wall_ref[...], 1, 0).astype(jnp.bfloat16)
    for s, ref in enumerate(outs):

        @pl.when(step == s)
        def _(ref=ref):
            ref[...] = product


def attend_back_kernel(slots, info, q_ref, *refs):
    count = len(slots)
    d_refs, refs = refs[:count], refs[count:]
    wall_ref, o_ref, lse_ref, kv_ref, kvt_ref, start_ref, cos_ref, sin_ref, *refs = refs
    last_call = slots[-1] == 2
    if last_call:
        before_ref, gq_ref, *g_refs, gkv_ref, dh_ref = refs
    else:
        gq_ref, gkv_ref, dh_ref = refs
    step = pl.program_id(0)

    @pl.when(step == 0)
    def _():
        if last_call:
            gkv_ref[...] = before_ref[...]
        else:
            gkv_ref[...] = jnp.zeros_like(gkv_ref)
        for s, ref in enumerate(d_refs):
            dh_ref[s] = ref[...]

    slot_now = slot_of(slots, step)
    z, y, last, rows, start = mask_parts(info, start_ref[0], slot_now)
    query = heads_side_by_side(q_ref[...])
    grad = dot(wall_ref[...], dh_ref[step], 1, 1).astype(jnp.bfloat16)
    grad = heads_side_by_side(grad)
    out = heads_side_by_side(o_ref[...])
    rowdot = jnp.sum(grad.astype(jnp.float32) * out.astype(jnp.float32), axis=0, keepdims=True)
    query = jnp.concatenate([query, jnp.zeros_like(query)], axis=0)
    grad = jnp.concatenate([jnp.zeros_like(grad), grad], axis=0)
    lse = lse_ref[0]

    def one(block, acc):
        slot = block_slot(block, z, y)
        kv = kv_ref[slot]
        scores = dot(kv, query, 1, 0)
        key = block * ROWS + lax.broadcasted_iota(jnp.int32, (ROWS, 1), 0)
        probs = jnp.where((key >= start) & (key <= rows), jnp.exp(scores - lse), 0.0)
        grad_probs = dot(kv, grad, 1, 0)
        grad_scores = (probs * (grad_probs - rowdot)).astype(jnp.bfloat16)
        gkv_ref[slot] += dot(grad_scores, query, 1, 1) + dot(
            probs.astype(jnp.bfloat16), grad, 1, 1
        )
        return acc + dot(kvt_ref[slot, :HEAD_SIZE], grad_scores, 1, 0)

    acc = lax.fori_loop(
        info[2 + slot_now], last + 1, one, jnp.zeros((HEAD_SIZE, WIDE), jnp.float32)
    )
    acc = acc * HEAD_SIZE**-0.5
    acc = jnp.concatenate([acc[:, h * ROWS : (h + 1) * ROWS] for h in range(HEADS)], axis=0)
    gq_ref[...] = rope(acc, cos_ref[...], -sin_ref[...]).astype(jnp.bfloat16)

    if last_call:

        @pl.when(step == count - 1)
        def _():
            for t, ref in enumerate(g_refs):
                for s in range(RING):
                    ref[s * ROWS : (s + 1) * ROWS, :] = gkv_ref[t * RING + s].astype(jnp.bfloat16)


def input_back_kernel(
    info, gq_ref, k0, k1, k2, k3, w_ref, x0, x1, x2, x3, cos_ref, sin_ref, n_ref, gain_two_ref,
    scale_ref, h0, h1, h2, h3, p0, p1, p2, p3, keep_ref, send_ref, row_ref, gkv_ref,
):
    for out, ref in zip((p0, p1, p2, p3), (h0, h1, h2, h3)):
        out[ROWS:] = ref[...]
    y, x, core = info[1], info[6], info[7]
    total = sum(ref[...].astype(jnp.float32) for ref in (k0, k1, k2, k3)).T
    key = rope(total[:HEAD_SIZE], cos_ref[...], -sin_ref[...])
    gkv_ref[...] = jnp.concatenate([key, total[HEAD_SIZE:]], axis=0).astype(jnp.bfloat16)
    row_ref[:, : 4 * ROWS] = gq_ref[...].T
    row_ref[:, 4 * ROWS :] = gkv_ref[...].T
    gains = []
    for xc in range(CHUNKS):
        columns = slice(xc * CHUNK, (xc + 1) * CHUNK)
        product = dot(row_ref[...], w_ref[:, columns], 1, 0)
        gain = jnp.zeros((1, CHUNK), jnp.float32)
        for s, (ref, inputs) in enumerate(zip((p0, p1, p2, p3), (x0, x1, x2, x3))):
            piece = product[s * ROWS : (s + 1) * ROWS]
            ref[:ROWS, columns] = piece.astype(jnp.bfloat16)
            scale = scale_ref[s * ROWS : (s + 1) * ROWS, :1]
            unit = inputs[:, columns].astype(jnp.float32) * scale
            gain += jnp.sum(piece * unit, axis=0, keepdims=True)
        gains.append(gain)
    gains_two = [gain_two_ref[:, xc * CHUNK : (xc + 1) * CHUNK] for xc in range(CHUNKS)]
    gains = sum(
        dot(jnp.concatenate(rows, axis=0).astype(jnp.bfloat16), gain_spread(which, True), 1, 0)
        for which, rows in enumerate((gains, gains_two))
    )
    kv_all = dot(gkv_ref[...], n_ref[...], 1, 0)
    for xc in range(CHUNKS):
        kv = kv_all[:, xc * CHUNK : (xc + 1) * CHUNK].T
        for home in range(RING):
            halves = [
                jnp.concatenate(
                    [
                        kv[z * 64 + home * 16 : z * 64 + home * 16 + 16]
                        for z in (2 * side, 2 * side + 1)
                    ],
                    axis=0,
                )
                for side in range(2)
            ]
            piece = jnp.broadcast_to(gains[xc : xc + 1, home * 128 : (home + 1) * 128], (16, 128))
            piece = jnp.concatenate(
                [jnp.concatenate(halves, axis=1), jnp.concatenate([piece, piece], axis=1)], axis=0
            ).astype(jnp.bfloat16)
            slots = turned(x, xc // 2), turned(y, home)

            @pl.when(core == xc % 2)
            def _(slots=slots, piece=piece):
                keep_ref[slots[0], slots[1]] = piece

            @pl.when(core != xc % 2)
            def _(slots=slots, piece=piece):
                send_ref[slots[0], slots[1]] = piece


def grad_output_query_kernel(info, o_ref, gq_ref, d0, d1, d2, d3, n_ref, keep_ref, send_ref):
    y, core = info[1], info[7]
    for c, out in ((core, keep_ref), (1 - core, send_ref)):
        columns = place_of(c, CHUNK)
        rows = jnp.concatenate([ref[:, columns] for ref in (d0, d1, d2, d3)], axis=0)
        grad_output = dot(o_ref[...], rows, 1, 0).astype(jnp.bfloat16)
        grad_query = dot(gq_ref[...], n_ref[:, columns], 1, 0).astype(jnp.bfloat16)
        for home in range(RING):
            slot = turned(y, home)
            out[0, slot, :ROWS] = part(grad_output, home, ROWS)
            out[0, slot, ROWS:] = part(grad_query, home, ROWS)


def feed_kernel(
    info, n0, n1, d0, d1, w_hbm, keep_ref, send_ref, h_ref, p0, p1,
    gu_ref, down_ref, n_ref, d_ref, hg_ref, row_ref, slot_ref, sems, slot_sems,
):
    units = gu_ref.shape[2]
    half = units // 2
    first = info[7] == 0

    def fetch(xc, y):
        columns = pl.ds(xc * CHUNK, CHUNK)
        return (
            pltpu.make_async_copy(
                w_hbm.at[xc, y, pl.ds(0, 2)], gu_ref.at[y, :, :, columns], sems.at[0, y, xc]
            ),
            pltpu.make_async_copy(w_hbm.at[xc, y, 2], down_ref.at[y, :, columns], sems.at[1, y, xc]),
        )

    slots = [
        pltpu.make_async_copy(ref, slot_ref.at[i], slot_sems.at[i])
        for i, ref in enumerate((n0, n1, d0, d1))
    ]
    for copy in slots:
        copy.start()
    for xc in range(CHUNKS):
        for copy in fetch(xc, 0):
            copy.start()
    for i, copy in enumerate(slots):
        copy.wait()
        out = (n_ref, d_ref)[i // 2]
        out[:, i % 2 * ROWS : (i % 2 + 1) * ROWS] = slot_ref[i].T
    for xc in range(CHUNKS):
        for copy in fetch(xc, 1):
            copy.start()

    def one(y, _):
        @pl.when(y < RING - 2)
        def _():
            for xc in range(CHUNKS):
                for copy in fetch(xc, y + 2):
                    copy.start()

        for xc in range(CHUNKS):
            for copy in fetch(xc, y):
                copy.wait()
        gate_up = dot(gu_ref[y].reshape(2 * units, MODEL_WIDTH), n_ref[...], 1, 0)
        grad_hidden = dot(down_ref[y], d_ref[...], 1, 0)
        gate, upper = gate_up[:units], gate_up[units:]
        sig = 1.0 / (1.0 + jnp.exp(-gate))
        silu = gate * sig
        grad_gate = grad_hidden * upper * (sig + silu * (1.0 - sig))
        grad_up = grad_hidden * silu
        hidden = silu * upper
        hg_ref[y, 0] = grad_gate.astype(jnp.bfloat16)
        hg_ref[y, 1] = grad_up.astype(jnp.bfloat16)
        h_ref[y] = hidden.astype(jnp.bfloat16)
        for k, value in enumerate((grad_gate, grad_up, hidden)):
            low, high = value[:half], value[half:]
            keep_ref[y, k] = jnp.where(first, low, high).astype(jnp.bfloat16)
            send_ref[y, k] = jnp.where(first, high, low).astype(jnp.bfloat16)
        return 0

    lax.fori_loop(0, RING, one, 0)
    row_ref[...] = hg_ref[...].reshape(RING * 2 * units, 2 * ROWS).T

    def back(i, _):
        columns = place_of(i, 2 * CHUNK)
        weights = gu_ref[:, :, :, columns].reshape(RING * 2 * units, 2 * CHUNK)
        total = dot(row_ref[...], weights, 1, 0).astype(jnp.bfloat16)
        p0[:, columns], p1[:, columns] = total[:ROWS], total[ROWS:]
        return 0

    lax.fori_loop(0, CHUNKS // 2, back, 0)


def half_rows(refs):
    return jnp.concatenate([refs[s][...] for s in HALVES], axis=0)


def feed_grad_kernel(
    keep0, keep1, other0, other1, n0, n1, n2, n3, n_other, d0, d1, d2, d3, d_other, g_hbm, gu_ref, down_ref, g_ref, sems
):
    units = keep0.shape[2]
    step = pl.program_id(0)

    @pl.when(step == 0)
    def _():
        for index, ref in enumerate((keep0, keep1, other0, other1)):
            columns = slice(index * 2 * ROWS, (index + 1) * 2 * ROWS)
            gu_ref[:, columns] = ref[:, :2].reshape(RING * 2 * units, 2 * ROWS)
            down_ref[:, columns] = ref[:, 2].reshape(RING * units, 2 * ROWS)

    rows = jnp.concatenate([half_rows((n0, n1, n2, n3)), n_other[...]], axis=0)
    grad = dot(gu_ref[...], rows, 1, 0).astype(jnp.bfloat16)
    g_ref[step, :, :2] = grad.reshape(RING, 2, units, 2 * CHUNK)
    rows = jnp.concatenate([half_rows((d0, d1, d2, d3)), d_other[...]], axis=0)
    grad = dot(down_ref[...], rows, 1, 0).astype(jnp.bfloat16)
    g_ref[step, :, 2] = grad.reshape(RING, units, 2 * CHUNK)
    pltpu.make_async_copy(g_ref.at[step], g_hbm.at[step], sems.at[step]).start()

    @pl.when(step == RING - 1)
    def _():
        for x in range(RING):
            pltpu.make_async_copy(g_ref.at[x], g_hbm.at[x], sems.at[x]).wait()


def feed_down_kernel(h0_ref, h1_ref, w_hbm, p0, p1, p2, p3, row_ref, w_ref, sems):
    units = h0_ref.shape[1]
    copies = [
        [
            pltpu.make_async_copy(
                w_hbm.at[xc, y, 2],
                w_ref.at[xc // 2, pl.ds(y * units, units), pl.ds(xc % 2 * CHUNK, CHUNK)],
                sems.at[xc, y],
            )
            for xc in (2 * step, 2 * step + 1)
            for y in range(RING)
        ]
        for step in range(CHUNKS // 2)
    ]
    for group in copies:
        for copy in group:
            copy.start()
    for half, ref in enumerate((h0_ref, h1_ref)):
        row_ref[half * 2 * ROWS : (half + 1) * 2 * ROWS] = (
            ref[...].reshape(RING * units, 2 * ROWS).T
        )
    for step, group in enumerate(copies):
        for copy in group:
            copy.wait()
        total = dot(row_ref[...], w_ref[step], 1, 0).astype(jnp.bfloat16)
        for index, ref in enumerate((p1, p3, p0, p2)):
            ref[:, step * 2 * CHUNK : (step + 1) * 2 * CHUNK] = part(total, index, ROWS)


def residual_back_kernel(g0, g1, g2, g3, h_ref, dy_ref, gain_ref, dh_ref, dh_low_ref, gg_ref):
    grad = sum(ref[...].astype(jnp.float32) for ref in (g0, g1, g2, g3))
    scale = rms_scale(h_ref[...])
    unit = h_ref[...] * scale

    @pl.when(pl.program_id(0) == 0)
    def _():
        gg_ref[...] = jnp.zeros_like(gg_ref)

    gg_ref[...] += jnp.sum(grad * unit, axis=0, keepdims=True)
    out = dy_ref[...].astype(jnp.float32) + norm_back(unit, scale, gain_ref[...], grad)
    dh_ref[...] = out
    dh_low_ref[...] = out.astype(jnp.bfloat16)


def whole(shape):
    return pl.BlockSpec(shape, lambda *_: (0,) * len(shape))


def struct(shape, dtype=jnp.bfloat16):
    return jax.ShapeDtypeStruct(shape, dtype)


def cost(flops, moved, exps=0):
    return pl.CostEstimate(flops=flops, bytes_accessed=moved, transcendentals=exps)


def params(mebibytes):
    return pltpu.CompilerParams(vmem_limit_bytes=mebibytes << 20)


SLOT = (ROWS, MODEL_WIDTH)
SPLIT = ((1, 3), (0, 2))
SPLIT_BACK = ((0, 1, 3), (2,))


def columns_of(slots, rows):
    return pl.BlockSpec((rows, ROWS), lambda s, info: (0, slot_of(slots, s)))


def row_of(slots, width):
    return pl.BlockSpec((1, 1, width), lambda s, info: (slot_of(slots, s), 0, 0))


def hbm(value):
    return pltpu.with_memory_space_constraint(value, pltpu.HBM)


def project_qkv(info, x_slots, pack, k_slots, k_other, cosine, sine):
    return pl.pallas_call(
        qkv_kernel,
        grid_spec=pltpu.PrefetchScalarGridSpec(
            num_scalar_prefetch=1,
            grid=(1,),
            in_specs=[whole(SLOT)] * 4
            + [pl.BlockSpec(memory_space=pltpu.HBM)]
            + [whole((RING, 48, CHUNK))] * 4
            + [whole((RING, RING, 48, CHUNK))]
            + [whole((32, TOKENS))] * 2,
            out_specs=[
                whole((TOKENS, MODEL_WIDTH)),
                whole((512, TOKENS)),
                whole((TOKENS, 128)),
                whole((640, MODEL_WIDTH)),
                whole((2, MODEL_WIDTH)),
                whole((TOKENS, 128)),
            ],
            scratch_shapes=[
                pltpu.VMEM((CHUNKS, CHUNK, 128), jnp.bfloat16),
                pltpu.VMEM((CHUNKS, RING, 16, 128), jnp.float32),
                pltpu.SemaphoreType.DMA((CHUNKS, RING)),
            ],
        ),
        out_shape=[
            struct((TOKENS, MODEL_WIDTH)),
            struct((512, TOKENS)),
            struct((TOKENS, 128)),
            struct((640, MODEL_WIDTH)),
            struct((2, MODEL_WIDTH), jnp.float32),
            struct((TOKENS, 128), jnp.float32),
        ],
        compiler_params=params(32),
        cost_estimate=cost(2 * 640 * TOKENS * MODEL_WIDTH, 9 << 20),
        name="project_qkv",
    )(info, *map(hbm, x_slots), hbm(pack), *k_slots, k_other, cosine, sine)


def attend(slots, info, q_t, kv, starts, pack=None, shared=()):
    count = len(slots)
    walls = [whole((512, MODEL_WIDTH)), whole((BLOCKS, 128, ROWS))]
    shapes = [struct((512, MODEL_WIDTH)), struct((BLOCKS, 128, ROWS))]
    return pl.pallas_call(
        functools.partial(attend_kernel, slots),
        grid_spec=pltpu.PrefetchScalarGridSpec(
            num_scalar_prefetch=1,
            grid=(count,),
            in_specs=[columns_of(slots, 512), whole((BLOCKS, ROWS, 128)), row_of(slots, ROWS)]
            + (walls if shared else [pl.BlockSpec(memory_space=pltpu.HBM)]),
            out_specs=[
                pl.BlockSpec((512, ROWS), lambda s, info: (0, s)),
                pl.BlockSpec((1, 1, WIDE), lambda s, info: (s, 0, 0)),
            ]
            + [whole(SLOT)] * count
            + ([] if shared else walls),
            scratch_shapes=[] if shared else [pltpu.SemaphoreType.DMA((CHUNKS, RING))],
        ),
        out_shape=[struct((512, count * ROWS)), struct((count, 1, WIDE), jnp.float32)]
        + [struct(SLOT)] * count
        + ([] if shared else shapes),
        compiler_params=params(16),
        cost_estimate=cost(
            count * HEADS * TOKENS * 640 * 128 + count * 512 * ROWS * 2 * MODEL_WIDTH,
            6 << 20,
            count * HEADS * ROWS * 640,
        ),
        name="attend",
    )(info, q_t, kv, starts, *(shared or [hbm(pack)]))


def attend_back(
    slots, info, q_t, dh_slots, wall, o_t, lse, kv, kv_t, starts, cosine, sine, before=None
):
    count = len(slots)
    sums = (BLOCKS, ROWS, 128)
    out_specs = [pl.BlockSpec((512, ROWS), lambda s, info: (0, s))]
    out_shape = [struct((512, count * ROWS))]
    scratch_shapes = []
    if before is None:
        out_specs += [whole(sums)]
        out_shape += [struct(sums, jnp.float32)]
    else:
        out_specs += [whole((TOKENS, 128))] * 4
        out_shape += [struct((TOKENS, 128))] * 4
        scratch_shapes += [pltpu.VMEM(sums, jnp.float32)]
    return pl.pallas_call(
        functools.partial(attend_back_kernel, slots),
        grid_spec=pltpu.PrefetchScalarGridSpec(
            num_scalar_prefetch=1,
            grid=(count,),
            in_specs=[columns_of(slots, 512)]
            + [whole(SLOT)] * count
            + [
                whole((512, MODEL_WIDTH)),
                columns_of(slots, 512),
                row_of(slots, WIDE),
                whole((BLOCKS, ROWS, 128)),
                whole((BLOCKS, 128, ROWS)),
                row_of(slots, ROWS),
                columns_of(slots, HEAD_SIZE // 2),
                columns_of(slots, HEAD_SIZE // 2),
            ]
            + ([] if before is None else [whole(sums)]),
            out_specs=out_specs,
            scratch_shapes=scratch_shapes + [pltpu.VMEM((count, *SLOT), jnp.bfloat16)],
        ),
        out_shape=out_shape,
        compiler_params=params(18),
        cost_estimate=cost(
            3 * count * HEADS * ROWS * 640 * 128 * 4 + count * 512 * ROWS * 2 * MODEL_WIDTH,
            8 << 20,
            count * HEADS * ROWS * 640,
        ),
        name="attend_back",
    )(
        info, q_t, *dh_slots, wall, o_t, lse, kv, kv_t, starts, cosine, sine,
        *([] if before is None else [before]),
    )


def input_back(info, gq_t, gkv_slots, w_qkv, x_slots, cosine, sine, normed, gain_two, scales, down):
    pieces = (RING, RING, 48, CHUNK)
    return pl.pallas_call(
        input_back_kernel,
        grid_spec=pltpu.PrefetchScalarGridSpec(
            num_scalar_prefetch=1,
            grid=(1,),
            in_specs=[whole((512, TOKENS))]
            + [whole((TOKENS, 128))] * 4
            + [whole((640, MODEL_WIDTH))]
            + [whole(SLOT)] * 4
            + [whole((32, TOKENS))] * 2
            + [whole((TOKENS, MODEL_WIDTH)), whole((1, MODEL_WIDTH)), whole((TOKENS, 128))]
            + [whole(SLOT)] * 4,
            out_specs=[whole((2 * ROWS, MODEL_WIDTH))] * 4 + [whole(pieces)] * 2,
            scratch_shapes=[
                pltpu.VMEM((TOKENS, 640), jnp.bfloat16),
                pltpu.VMEM((128, TOKENS), jnp.bfloat16),
            ],
        ),
        out_shape=[pltpu.HBM((2 * ROWS, MODEL_WIDTH), jnp.bfloat16)] * 4 + [struct(pieces)] * 2,
        compiler_params=params(32),
        cost_estimate=cost(2 * 768 * TOKENS * MODEL_WIDTH, 15 << 20),
        name="input_back",
    )(
        info, gq_t, *gkv_slots, w_qkv, *map(hbm, x_slots), cosine, sine, normed, gain_two, scales, *down,
    )


def pack_specs(rows):
    spec = pl.BlockSpec((1, RING, rows, CHUNK), lambda s, info: (s, 0, 0, 0))
    return [spec, spec], [struct((RING, RING, rows, CHUNK))] * 2


def pair_columns(rows):
    return pl.BlockSpec((rows, 2 * CHUNK), lambda s, info: (0, (info[6] + RING - s) % RING))


def grad_output_query(info, o_t, gq_t, dh_slots, normed):
    out_specs, out_shape = pack_specs(2 * ROWS)
    return pl.pallas_call(
        grad_output_query_kernel,
        grid_spec=pltpu.PrefetchScalarGridSpec(
            num_scalar_prefetch=1,
            grid=(RING,),
            in_specs=[whole((512, TOKENS))] * 2
            + [pair_columns(ROWS)] * 4
            + [pair_columns(TOKENS)],
            out_specs=out_specs,
        ),
        out_shape=out_shape,
        compiler_params=params(14),
        cost_estimate=cost(4 * 512 * TOKENS * MODEL_WIDTH, 9 << 20),
        name="grad_output_query",
    )(info, o_t, gq_t, *dh_slots, normed)


def feed(info, n_pair, d_pair, weights):
    units = weights.shape[3]
    pair = (2 * ROWS, MODEL_WIDTH)
    split = (RING, 3, units // 2, 2 * ROWS)
    return pl.pallas_call(
        feed_kernel,
        in_specs=[pl.BlockSpec(memory_space=pltpu.SMEM)]
        + [pl.BlockSpec(memory_space=pl.ANY)] * 4
        + [pl.BlockSpec(memory_space=pltpu.HBM)],
        out_specs=[pl.BlockSpec(memory_space=pltpu.VMEM)] * 5,
        out_shape=[struct(split)] * 2 + [struct((RING, units, 2 * ROWS))] + [struct(SLOT)] * 2,
        scratch_shapes=[
            pltpu.VMEM((RING, 2, units, MODEL_WIDTH), jnp.bfloat16),
            pltpu.VMEM((RING, units, MODEL_WIDTH), jnp.bfloat16),
            pltpu.VMEM(pair[::-1], jnp.bfloat16),
            pltpu.VMEM(pair[::-1], jnp.bfloat16),
            pltpu.VMEM((RING, 2, units, 2 * ROWS), jnp.bfloat16),
            pltpu.VMEM((2 * ROWS, RING * 2 * units), jnp.bfloat16),
            pltpu.VMEM((4, *SLOT), jnp.bfloat16),
            pltpu.SemaphoreType.DMA((2, RING, CHUNKS)),
            pltpu.SemaphoreType.DMA((4,)),
        ],
        compiler_params=params(30),
        cost_estimate=cost(5 * RING * units * TOKENS * MODEL_WIDTH, 23 << 20, RING * units * TOKENS // 2),
        name="feed",
    )(info, *map(hbm, n_pair), *map(hbm, d_pair), hbm(weights))


def feed_grad(keeps, others, n_slots, n_other, d_slots, d_other):
    units = keeps[0].shape[2]
    slots = [pl.BlockSpec((ROWS, 2 * CHUNK), lambda i: (0, i))] * 4
    slots += [pl.BlockSpec((TOKENS, 2 * CHUNK), lambda i: (0, i))]
    out = (RING, RING, 3, units, 2 * CHUNK)
    return pl.pallas_call(
        feed_grad_kernel,
        grid=(RING,),
        in_specs=[whole(keeps[0].shape)] * 4 + slots * 2,
        out_specs=pl.BlockSpec(memory_space=pltpu.HBM),
        out_shape=pltpu.HBM(out, jnp.bfloat16),
        scratch_shapes=[
            pltpu.VMEM((RING * 2 * units, 2 * TOKENS), jnp.bfloat16),
            pltpu.VMEM((RING * units, 2 * TOKENS), jnp.bfloat16),
            pltpu.VMEM(out, jnp.bfloat16),
            pltpu.SemaphoreType.DMA((RING,)),
        ],
        compiler_params=params(30),
        cost_estimate=cost(12 * RING * units * TOKENS * MODEL_WIDTH, 22 << 20),
        name="feed_grad",
    )(*keeps, *others, *map(hbm, n_slots), hbm(n_other), *map(hbm, d_slots), hbm(d_other))


def residual_back(grads, h1, out_grad, gain):
    rows = pl.BlockSpec((ROWS // 2, MODEL_WIDTH), lambda i: (i, 0))
    vector = pl.BlockSpec((1, MODEL_WIDTH), lambda i: (0, 0))
    return pl.pallas_call(
        residual_back_kernel,
        grid=(2,),
        in_specs=[rows] * 6 + [vector],
        out_specs=[rows, rows, vector],
        out_shape=[struct(SLOT, jnp.float32), struct(SLOT), struct((1, MODEL_WIDTH), jnp.float32)],
        compiler_params=params(16),
        cost_estimate=cost(30 * ROWS * MODEL_WIDTH, 5 << 20),
        name="residual_back",
    )(*map(hbm, grads), hbm(h1), hbm(out_grad), gain)


def feed_down(hs, weights):
    units = hs[0].shape[1]
    return pl.pallas_call(
        feed_down_kernel,
        in_specs=[pl.BlockSpec(memory_space=pltpu.VMEM)] * 2 + [pl.BlockSpec(memory_space=pltpu.HBM)],
        out_specs=[pl.BlockSpec(memory_space=pltpu.VMEM)] * 4,
        out_shape=[struct(SLOT)] * 4,
        scratch_shapes=[
            pltpu.VMEM((TOKENS, RING * units), jnp.bfloat16),
            pltpu.VMEM((CHUNKS // 2, RING * units, 2 * CHUNK), jnp.bfloat16),
            pltpu.SemaphoreType.DMA((CHUNKS, RING)),
        ],
        compiler_params=params(18),
        cost_estimate=cost(2 * RING * units * TOKENS * MODEL_WIDTH, 9 << 20),
        name="feed_down",
    )(*hs, hbm(weights))


def adamw(weight, first, second, grad, rate, decay):
    first_new = BETA_ONE * first + (1.0 - BETA_ONE) * grad
    second_new = BETA_TWO * second + (1.0 - BETA_TWO) * grad * grad
    fix_one = 1.0 - BETA_ONE**STEP
    fix_two = 1.0 - BETA_TWO**STEP
    update = first_new / fix_one / (jnp.sqrt(second_new / fix_two) + ADAM_EPS)
    return (weight - rate * (update + decay * weight), first_new, second_new)


def adam_feed_kernel(info, own_ref, other_ref, *refs):
    step, core = pl.program_id(0), info[7]
    own = jnp.where(core == 0, own_ref[:, :, :CHUNK], own_ref[:, :, CHUNK:])
    grad = jnp.where(step == core, own, other_ref[...]).astype(jnp.float32)
    for k, (g, rate) in enumerate(((grad[:2], MODEL_WIDTH**-0.5), (grad[2], FF**-0.5))):
        ins, outs = refs[3 * k : 3 * k + 3], refs[6 + 3 * k : 9 + 3 * k]
        values = adamw(*(ref[...] for ref in ins), g, rate, DECAY)
        for ref, value in zip(outs, values):
            ref[...] = value


def adam_feed(info, own, other, gateup, down):
    units = down[0].shape[0]
    half = units // 2
    specs = [pl.BlockSpec((2, half, CHUNK), lambda i, info: (0, i, 0))] * 3
    specs += [pl.BlockSpec((half, CHUNK), lambda i, info: (i, 0))] * 3
    arrays = [*gateup, *down]
    return pl.pallas_call(
        adam_feed_kernel,
        grid_spec=pltpu.PrefetchScalarGridSpec(
            num_scalar_prefetch=1,
            grid=(2,),
            in_specs=[whole(own.shape), whole(other.shape)] + specs,
            out_specs=specs,
        ),
        out_shape=[struct(a.shape, jnp.float32) for a in arrays],
        compiler_params=params(16),
        cost_estimate=cost(30 * 3 * units * CHUNK, 24 * 3 * units * CHUNK),
        name="adam_feed",
    )(info, hbm(own), other, *map(hbm, arrays))


def adam_attention_kernel(*refs):
    parts, refs = refs[:RING], refs[RING:]
    total = sum(ref[: 2 * ROWS].astype(jnp.float32) for ref in parts)
    grads = total[ROWS:].T, total[:ROWS]
    for k, (g, rate) in enumerate(zip(grads, (MODEL_WIDTH**-0.5, (MODEL_WIDTH // 64) ** -0.5))):
        ins, outs = refs[3 * k : 3 * k + 3], refs[6 + 3 * k : 9 + 3 * k]
        values = adamw(*(ref[...] for ref in ins), g, rate, DECAY)
        for ref, value in zip(outs, values):
            ref[...] = value


def adam_attention(parts, query, output):
    arrays = [*query, *output]
    specs = [whole(a.shape) for a in arrays]
    return pl.pallas_call(
        adam_attention_kernel,
        grid=(1,),
        in_specs=[whole(p.shape) for p in parts] + specs,
        out_specs=specs,
        out_shape=[struct(a.shape, jnp.float32) for a in arrays],
        compiler_params=params(16),
        cost_estimate=cost(60 * ROWS * CHUNK, 50 * ROWS * CHUNK),
        name="adam_attention",
    )(*parts, *map(hbm, arrays))


def swap_cores(value):
    return lax.ppermute(value, "core", [(0, 1), (1, 0)])


def scatter_core(keep, other):
    return [
        (keep[s].astype(jnp.float32) + other[s].astype(jnp.float32)).astype(jnp.bfloat16)
        for s in range(RING)
    ]


def sum_x(parts):
    return [
        sum(p[s].astype(jnp.float32) for p in parts).astype(jnp.bfloat16) for s in range(RING)
    ]


def after(values, *others):
    return lax.optimization_barrier((list(values), others))[0]


def local(
    block_input,
    out_grad,
    segments,
    w_query,
    keyvalue_weights,
    w_output,
    w_gateup,
    w_down,
    norm_gains,
    query_first,
    keyval_moment_one,
    output_first,
    gateup_first,
    down_first,
    gains_first,
    query_second,
    keyval_moment_two,
    output_second,
    gateup_second,
    down_second,
    gains_second,
):
    bf16, f32 = jnp.bfloat16, jnp.float32
    x, core, z, y = (lax.axis_index(name) for name in ("x", "core", "z", "y"))
    units = w_down.shape[0]

    kv_rows = keyvalue_weights.astype(bf16).reshape(2, 16, RING, HEAD_SIZE).transpose(2, 1, 0, 3)
    message = jnp.concatenate(
        [
            kv_rows.reshape(RING, 16, 128),
            jnp.broadcast_to(
                jnp.pad(norm_gains.astype(bf16).reshape(1, 1, 32), ((0, 0), (0, 15), (0, 96))),
                (RING, 16, 128),
            ),
        ],
        1,
    )
    small = absolute(scatter_ring_from(relative(message, z), "z"), z)
    kv_piece = jnp.concatenate(
        [small[:2, :16].reshape(32, 128), small[2:, :16].reshape(32, 128)], 1
    )
    gain_piece = jnp.pad(small[:, 16, :32].reshape(1, 128), ((0, 15), (0, 128)))
    kv_piece = jnp.concatenate([kv_piece, gain_piece], 0)

    pack = jnp.concatenate([w_output.astype(bf16), w_query.astype(bf16).T], 0)
    pack = lax.all_gather(pack, SHARE, axis=0, tiled=False)
    x_slots = gather_far_last(block_input, "z")
    (kv_piece,) = after([jnp.stack(gather_ring(kv_piece, "x"))], x_slots[1], x_slots[3])
    k_slots = gather_ring(kv_piece, "y")
    k_other = swap_cores(jnp.stack(after(k_slots, x_slots[2])))
    d_slots = gather_far_last(after([out_grad], *x_slots[1:])[0], "z")
    feed_shard = jnp.concatenate(
        [w_gateup.astype(bf16).transpose(0, 2, 1), w_down.astype(bf16)[None]], 0
    )
    (feed_shard,) = after([feed_shard], pack, d_slots[1], d_slots[3], k_other)
    w_feed = lax.all_gather(feed_shard, SHARE, axis=0, tiled=False)
    w_feed = w_feed.reshape(CHUNKS, RING, 3, units, CHUNK)

    starts = doc_starts(segments[0])
    by_block = lax.dynamic_index_in_dim(starts.reshape(RING, RING, ROWS), y, 1, keepdims=False)
    row_starts = jnp.stack(relative(by_block, z))
    places = (z + RING - jnp.arange(RING, dtype=jnp.int32)) % RING
    begins = places * (RING * ROWS) + y * ROWS
    positions = (begins[:, None] + jnp.arange(ROWS, dtype=jnp.int32) - row_starts).reshape(-1)
    half = HEAD_SIZE // 2
    freqs = 10000.0 ** (-jnp.arange(half, dtype=f32) * 2.0 / HEAD_SIZE)
    angles = freqs[:, None] * positions.astype(f32)[None, :]
    cosine, sine = jnp.cos(angles), jnp.sin(angles)
    info = jnp.concatenate(
        [
            jnp.stack([z, y]).astype(jnp.int32),
            row_starts[:, 0] // ROWS,
            jnp.stack([x, core]).astype(jnp.int32),
        ]
    )
    row_starts = row_starts[:, None, :]

    normed, q_t, kv_own, w_qkv, gains, scales = project_qkv(
        info, x_slots, pack, k_slots, k_other, cosine, sine
    )
    kv = jnp.stack(gather_ring(kv_own, "y")).reshape(BLOCKS, ROWS, 2 * HEAD_SIZE)
    d_all = jnp.concatenate([d_slots[s] for s in HALVES], 0)
    q_t, d_all = after([q_t, d_all])
    d_other = swap_cores(d_all)
    near_o, near_lse, o_1, o_3, *shared = attend(SPLIT[0], info, q_t, kv, row_starts, pack)
    wo, kv_t = shared
    (q_late,) = after([q_t], o_1, d_slots[2])
    far_o, far_lse, o_0, o_2 = attend(SPLIT[1], info, q_late, kv, row_starts, shared=shared)
    o_t = jnp.concatenate(
        [far_o[:, :ROWS], near_o[:, :ROWS], far_o[:, ROWS:], near_o[:, ROWS:]], 1
    )
    lse = jnp.stack([far_lse[0], near_lse[0], far_lse[1], near_lse[1]])
    o_1, o_3 = after([o_1, o_3], d_slots[2])
    o_slots = scatter_far_last(o_0, o_1, o_3, o_2, "z")
    o_sum = sum(p.astype(f32) for p in o_slots)
    h1 = block_input.astype(f32) + o_sum

    scale_two = rms_scale(h1)
    unit_two = h1 * scale_two
    (normed_two,) = after([(unit_two * gains[1]).astype(bf16)], d_other)
    n_slots = gather_far_last(normed_two, "z")
    keep0, send0, h0, gn2_1, gn2_3 = feed(
        info, [n_slots[s] for s in HALVES[:2]], [d_slots[s] for s in HALVES[:2]], w_feed
    )
    n_other = after([n_slots[s] for s in HALVES], keep0)
    n_other = swap_cores(jnp.concatenate(n_other, 0))
    keep1, send1, h1_half, gn2_0, gn2_2 = feed(
        info, after([n_slots[s] for s in HALVES[2:]], keep0), [d_slots[s] for s in HALVES[2:]], w_feed
    )
    gn2_slots = scatter_ring([gn2_0, gn2_1, gn2_2, gn2_3], "z")
    other0 = swap_cores(send0)
    (send1,) = after([send1], n_other, other0, gn2_slots[1], gn2_slots[3])
    others = other0, swap_cores(send1)
    grad_feed = feed_grad((keep0, keep1), others, n_slots, n_other, d_slots, d_other)
    *gn2_slots, grad_feed = after([*gn2_slots, grad_feed])
    dh1, dh1_low, grad_gain_two = residual_back(gn2_slots, h1, out_grad, gains[1:])
    own_feed = lax.psum_scatter(
        grad_feed.reshape(16, 3, units // 2, 2 * CHUNK), ("x", "y"), scatter_dimension=0, tiled=False
    )

    down_slots = feed_down(after([h0, h1_half], *gn2_slots), w_feed)
    dh_slots = gather_far_last(dh1_low, "z", *down_slots)
    near, far = SPLIT_BACK
    arguments = wo, o_t, lse, kv, kv_t, row_starts, cosine, sine
    gq_near, sums = attend_back(near, info, q_t, [dh_slots[s] for s in near], *arguments)
    (dh_far,) = after([dh_slots[2]], sums)
    gq_far, *gkv_slots = attend_back(far, info, q_t, [dh_far], *arguments, before=sums)
    gq_t = jnp.concatenate([gq_near[:, : 2 * ROWS], gq_far, gq_near[:, 2 * ROWS :]], 1)
    gkv_slots = scatter_ring(gkv_slots, "y")
    (gq_late,) = after([gq_t], gkv_slots[1], gkv_slots[3])
    keep, send = grad_output_query(info, o_t, gq_late, dh_slots, normed)
    (send,) = after([send], gkv_slots[2])
    gkv_slots = after(gkv_slots, send)
    *gn1_slots, keep_kv, send_kv = input_back(
        info, gq_t, gkv_slots, w_qkv, x_slots, cosine, sine, normed, grad_gain_two, scales, down_slots
    )
    gn1_0, gn1_1, gn1_2, gn1_3 = gn1_slots
    gn1_slots = scatter_far_last(gn1_0, gn1_1, gn1_3, gn1_2, "z")
    parts = zip(scatter_core(keep, swap_cores(send)), scatter_core(keep_kv, swap_cores(send_kv)))
    parts = scatter_ring([jnp.concatenate(p, 1) for p in parts], "x")

    parts_y = scatter_ring(sum_x(parts), "y")

    own_pack = sum(p[2 * ROWS :].astype(f32) for p in parts_y)

    kv_piece = own_pack[:32]
    kv_piece = jnp.concatenate([kv_piece[:, :128], kv_piece[:, 128:]], 0).reshape(RING, 16, 128)
    gain_piece = own_pack[32, :128].reshape(RING, 1, 32)
    message = jnp.concatenate([kv_piece, jnp.pad(gain_piece, ((0, 0), (0, 15), (0, 96)))], 1)
    small = scatter_ring_from(relative(message, z), "z")

    (own_feed,) = after([own_feed], small[1])
    other_send = jnp.where(core == 0, own_feed[..., CHUNK:], own_feed[..., :CHUNK])
    other = swap_cores(other_send)
    attention = adam_attention(
        after(parts_y, other_send),
        (w_query, query_first, query_second),
        (w_output, output_first, output_second),
    )
    q, o = attention[:3], attention[3:]
    turn = (0, 2, 1)
    feed_arrays = adam_feed(
        info,
        own_feed,
        other,
        [a.transpose(turn) for a in (w_gateup, gateup_first, gateup_second)],
        (w_down, down_first, down_second),
    )
    gu = [a.transpose(turn) for a in feed_arrays[:3]]
    down = feed_arrays[3:]
    last = sum(p.astype(f32) for p in after(gn1_slots, *parts_y[1:]))
    gn1 = last[:ROWS]
    result = (h1 + last[ROWS:]).astype(bf16)
    own_inputs = block_input.astype(f32)
    scale_one = rms_scale(own_inputs)
    grad_input = (dh1 + norm_back(own_inputs * scale_one, scale_one, gains[0], gn1)).astype(bf16)
    small[2:] = after(small[2:], *feed_arrays)
    small = absolute(small, z)
    own_kv = small[:, :16].reshape(RING, 16, 2, HEAD_SIZE).transpose(2, 1, 0, 3)
    own_kv = own_kv.reshape(2, 16, RING * HEAD_SIZE)
    own_gains = jnp.sum(small[:, 16, :32], 0).reshape(2, 16)

    rate = MODEL_WIDTH ** (-0.5)
    kvs = adamw(keyvalue_weights, keyval_moment_one, keyval_moment_two, own_kv, rate, DECAY)
    gain = adamw(norm_gains, gains_first, gains_second, own_gains, GAIN_RATE, 0.0)
    updates = (q, kvs, o, gu, down, gain)
    return (result, grad_input, *(u[i] for i in range(3) for u in updates))


def scatter_ring_from(slots, axis):
    own, after, far, before = scatter_ring(slots, axis)
    return [own, before, far, after]


def solution(mesh):
    view = Mesh(mesh.devices.reshape(4, 2, 4, 4), ("x", "core", "z", "y"))
    dp, tensor = ("x", "core"), ("z", "y")
    both = dp + tensor
    tokens = P(both, None)
    weights = (
        P(dp, tensor),
        P(None, both, None),
        P(tensor, dp),
        P(None, dp, tensor),
        P(tensor, dp),
        P(None, both),
    )
    return jax.shard_map(
        local,
        mesh=view,
        in_specs=(tokens, tokens, P(dp, None), *weights * 3),
        out_specs=(tokens, tokens, *weights * 3),
        check_vma=False,
    )
```

```python
import functools

import jax
import jax.numpy as jnp
from jax import lax
from jax.experimental import pallas as pl
from jax.experimental.pallas import tpu as pltpu
from jax.sharding import Mesh
from jax.sharding import PartitionSpec as P

MODEL_WIDTH = 2048
QUERY_HEADS = 32
KEYVALUE_HEADS = 4
HEAD_SIZE = 64
FF = 5632
STEP = 10

BETA_ONE = 0.9
BETA_TWO = 0.95
ADAM_EPS = 1e-08
DECAY = 0.1
GAIN_RATE = 0.8
NORM_EPS = 1e-05

RING = 4
SHARE = ("x", "core", "y")
ROWS = 128
TOKENS = RING * ROWS
HEADS = QUERY_HEADS // RING
WIDE = HEADS * ROWS
BLOCKS = 16
MASKED = -1e30
HALVES = (1, 3, 0, 2)
CHUNKS, CHUNK = 8, 256
PACK = 2 * ROWS + 48


def doc_starts(segment):
    index = jnp.arange(segment.shape[0], dtype=jnp.int32)
    starts = jnp.concatenate([jnp.ones((1,), dtype=bool), segment[1:] != segment[:-1]])
    return lax.cummax(jnp.where(starts, index, 0))


def shift(value, axis, step):
    return lax.ppermute(value, axis, [(i, (i + step) % RING) for i in range(RING)])


def gather_ring(value, axis):
    far = shift(value, axis, 2)
    return [value, shift(value, axis, 1), far, shift(value, axis, 3)]


def gather_far_last(value, axis, *others):
    near = shift(value, axis, 1), shift(value, axis, 3)
    (value_late,) = after([value], *near, *others)
    return [value, near[0], shift(value_late, axis, 2), near[1]]


def scatter_far_last(own, part_one, part_three, part_two, axis):
    near = shift(part_one, axis, 3), shift(part_three, axis, 1)
    (part_two,) = after([part_two], *near)
    return [own, near[0], shift(part_two, axis, 2), near[1]]


def scatter_ring(parts, axis):
    far = shift(parts[2], axis, 2)
    return [parts[0], shift(parts[1], axis, 3), far, shift(parts[3], axis, 1)]


def absolute(slots, own):
    turned = jnp.stack([slots[0], slots[3], slots[2], slots[1]])
    return lax.dynamic_slice_in_dim(jnp.concatenate([turned, turned]), RING - own, RING, 0)


def relative(stacked, own):
    turned = jnp.concatenate([stacked, stacked])
    return [
        lax.dynamic_index_in_dim(turned, own + RING - s if s else own, 0, keepdims=False)
        for s in range(RING)
    ]


def dot(left, right, left_dim, right_dim):
    return lax.dot_general(
        left, right, (((left_dim,), (right_dim,)), ((), ())), preferred_element_type=jnp.float32
    )


def rms_scale(values):
    return lax.rsqrt(jnp.mean(values * values, axis=-1, keepdims=True) + NORM_EPS)


def norm_back(unit, scale, gain, grad):
    scaled = grad * gain
    return scale * (scaled - unit * jnp.mean(scaled * unit, axis=-1, keepdims=True))


def part(ref, index, size):
    return ref[index * size : (index + 1) * size, :]


def heads_side_by_side(value):
    return jnp.concatenate([part(value, h, HEAD_SIZE) for h in range(HEADS)], axis=1)


def mask_parts(info, starts, step):
    z, y = info[0], info[1]
    place = (z + RING - step) % RING
    begin = place * (RING * ROWS) + y * ROWS
    row = begin + lax.broadcasted_iota(jnp.int32, (1, ROWS), 1)
    rows = jnp.concatenate([row] * HEADS, axis=1)
    start = jnp.concatenate([starts] * HEADS, axis=1)
    return z, y, place * RING + y, rows, start


def block_slot(block, z, y):
    return ((y + RING - block % RING) % RING) * RING + (z + RING - block // RING) % RING


def rope(values, cosine, sine):
    half = HEAD_SIZE // 2
    out = []
    for h in range(values.shape[0] // HEAD_SIZE):
        first = values[h * HEAD_SIZE : h * HEAD_SIZE + half]
        second = values[h * HEAD_SIZE + half : (h + 1) * HEAD_SIZE]
        out += [first * cosine - second * sine, first * sine + second * cosine]
    return jnp.concatenate(out, axis=0)


def turned(place, step):
    return (place + RING - step) % RING


def weight_slots(info, own_refs, other_ref):
    y, x, core = info[1], info[6], info[7]
    for cs in range(2):
        for ys in range(RING):
            for xs in range(RING):
                ref = other_ref.at[ys, xs] if cs else own_refs[ys].at[xs]
                yield turned(x, xs) * 2 + (1 - core if cs else core), turned(y, ys), ref


def place_of(index, size):
    return pl.ds(pl.multiple_of(index * size, size), size)


def gain_spread(which, transposed):
    shape = (CHUNK, 512) if transposed else (512, CHUNK)
    lane = lax.broadcasted_iota(jnp.int32, shape, 1 if transposed else 0)
    column = lax.broadcasted_iota(jnp.int32, shape, 0 if transposed else 1)
    y, z, gain, row = lane // 128, lane // 32 % 4, lane // 16 % 2, lane % 16
    same = (column // 64 == z) & (column // 16 % 4 == y) & (column % 16 == row) & (gain == which)
    return jnp.where(same, 1.0, 0.0).astype(jnp.bfloat16)


def fetch_pack(pack_hbm, which, out_ref, sems):
    return [
        pltpu.make_async_copy(
            pack_hbm.at[xc * RING + y, pl.ds(which * ROWS, ROWS)],
            out_ref.at[pl.ds(y * ROWS, ROWS), pl.ds(xc * CHUNK, CHUNK)],
            sems.at[xc, y],
        )
        for xc in range(CHUNKS)
        for y in range(RING)
    ]


def qkv_kernel(
    info, x0, x1, x2, x3, pack_hbm, k0, k1, k2, k3, k_other, cos_ref, sin_ref,
    n_ref, q_ref, kv_ref, w_ref, gain_ref, scale_ref, wkv_ref, piece_ref, sems,
):
    copies = fetch_pack(pack_hbm, 1, w_ref, sems)
    for copy in copies:
        copy.start()
    for chunk, y, ref in weight_slots(info, (k0, k1, k2, k3), k_other):
        for z in range(RING):
            wkv_ref[chunk, pl.ds(pl.multiple_of(z * 64 + y * 16, 16), 16), :] = ref[
                (z % 2) * 16 : (z % 2 + 1) * 16, (z // 2) * 128 : (z // 2 + 1) * 128
            ]
        piece_ref[chunk, y] = ref[32:48, :128].astype(jnp.float32)
    pieces = [
        jnp.concatenate([piece_ref[xc, y, :1] for y in range(RING)], axis=1) for xc in range(CHUNKS)
    ]
    pieces = jnp.concatenate(pieces, axis=0).astype(jnp.bfloat16)
    gains = [dot(pieces, gain_spread(which, False), 1, 0) for which in range(2)]
    for xc in range(CHUNKS):
        columns = slice(xc * CHUNK, (xc + 1) * CHUNK)
        w_ref[4 * ROWS : 5 * ROWS, columns] = wkv_ref[xc].T
        for which in range(2):
            gain_ref[which : which + 1, columns] = gains[which][xc : xc + 1]
    for s, ref in enumerate((x0, x1, x2, x3)):
        value = ref[...].astype(jnp.float32)
        scale = rms_scale(value)
        scale_ref[s * ROWS : (s + 1) * ROWS] = jnp.broadcast_to(scale, (ROWS, 128))
        n_ref[s * ROWS : (s + 1) * ROWS, :] = (value * scale * gain_ref[:1]).astype(jnp.bfloat16)
    for copy in copies:
        copy.wait()
    qkv = dot(w_ref[...], n_ref[...], 1, 1)
    query = rope(qkv[: 4 * ROWS], cos_ref[...], sin_ref[...]).astype(jnp.bfloat16)
    q_ref[...] = query * jnp.bfloat16(HEAD_SIZE**-0.5)
    key = rope(qkv[4 * ROWS : 4 * ROWS + HEAD_SIZE], cos_ref[...], sin_ref[...])
    key_value = jnp.concatenate([key, qkv[4 * ROWS + HEAD_SIZE :]], axis=0)
    kv_ref[...] = key_value.T.astype(jnp.bfloat16)


def slot_of(slots, step):
    out = slots[0]
    for index in range(1, len(slots)):
        out = out + (slots[index] - slots[index - 1]) * ((step + len(slots) - index) // len(slots))
    return out


def attend_kernel(
    slots, info, q_ref, kv_ref, start_ref, *refs
):
    step = pl.program_id(0)
    first_call = 2 not in slots
    if first_call:
        pack_hbm, o_ref, lse_ref, *outs, wall_ref, kvt_ref, sems = refs
        copies = fetch_pack(pack_hbm, 0, wall_ref, sems)

        @pl.when(step == 0)
        def _():
            for copy in copies:
                copy.start()
            for b in range(BLOCKS):
                kvt_ref[b] = kv_ref[b].T
    else:
        wall_ref, kvt_ref, o_ref, lse_ref, *outs = refs

    slot_now = slot_of(slots, step)
    z, y, last, rows, start = mask_parts(info, start_ref[0], slot_now)
    query = heads_side_by_side(q_ref[...])
    query = jnp.concatenate([query, jnp.zeros_like(query)], axis=0)

    def one(block, carry):
        top, total, acc = carry
        slot = block_slot(block, z, y)
        scores = dot(kv_ref[slot], query, 1, 0)
        key = block * ROWS + lax.broadcasted_iota(jnp.int32, (ROWS, 1), 0)
        scores = jnp.where((key >= start) & (key <= rows), scores, MASKED)
        new_top = jnp.maximum(top, jnp.max(scores, axis=0, keepdims=True))
        weights = jnp.exp(scores - new_top)
        fade = jnp.exp(top - new_top)
        total = total * fade + jnp.sum(weights, axis=0, keepdims=True)
        acc = acc * fade + dot(kvt_ref[slot, HEAD_SIZE:], weights.astype(jnp.bfloat16), 1, 0)
        return new_top, total, acc

    top, total, acc = lax.fori_loop(
        info[2 + slot_now],
        last + 1,
        one,
        (
            jnp.full((1, WIDE), MASKED, jnp.float32),
            jnp.zeros((1, WIDE), jnp.float32),
            jnp.zeros((HEAD_SIZE, WIDE), jnp.float32),
        ),
    )
    out = acc / total
    out = jnp.concatenate([out[:, h * ROWS : (h + 1) * ROWS] for h in range(HEADS)], axis=0)
    o_ref[...] = out.astype(jnp.bfloat16)
    lse_ref[0] = top + jnp.log(total)
    if first_call:

        @pl.when(step == 0)
        def _():
            for copy in copies:
                copy.wait()

    product = dot(out.T.astype(jnp.bfloat16), wall_ref[...], 1, 0).astype(jnp.bfloat16)
    for s, ref in enumerate(outs):

        @pl.when(step == s)
        def _(ref=ref):
            ref[...] = product


def attend_back_kernel(slots, info, q_ref, *refs):
    count = len(slots)
    d_refs, refs = refs[:count], refs[count:]
    wall_ref, o_ref, lse_ref, kv_ref, kvt_ref, start_ref, cos_ref, sin_ref, *refs = refs
    last_call = slots[-1] == 2
    if last_call:
        before_ref, gq_ref, *g_refs, gkv_ref, dh_ref = refs
    else:
        gq_ref, gkv_ref, dh_ref = refs
    step = pl.program_id(0)

    @pl.when(step == 0)
    def _():
        if last_call:
            gkv_ref[...] = before_ref[...]
        else:
            gkv_ref[...] = jnp.zeros_like(gkv_ref)
        for s, ref in enumerate(d_refs):
            dh_ref[s] = ref[...]

    slot_now = slot_of(slots, step)
    z, y, last, rows, start = mask_parts(info, start_ref[0], slot_now)
    query = heads_side_by_side(q_ref[...])
    grad = dot(wall_ref[...], dh_ref[step], 1, 1).astype(jnp.bfloat16)
    grad = heads_side_by_side(grad)
    out = heads_side_by_side(o_ref[...])
    rowdot = jnp.sum(grad.astype(jnp.float32) * out.astype(jnp.float32), axis=0, keepdims=True)
    query = jnp.concatenate([query, jnp.zeros_like(query)], axis=0)
    grad = jnp.concatenate([jnp.zeros_like(grad), grad], axis=0)
    lse = lse_ref[0]

    def one(block, acc):
        slot = block_slot(block, z, y)
        kv = kv_ref[slot]
        scores = dot(kv, query, 1, 0)
        key = block * ROWS + lax.broadcasted_iota(jnp.int32, (ROWS, 1), 0)
        probs = jnp.where((key >= start) & (key <= rows), jnp.exp(scores - lse), 0.0)
        grad_probs = dot(kv, grad, 1, 0)
        grad_scores = (probs * (grad_probs - rowdot)).astype(jnp.bfloat16)
        gkv_ref[slot] += dot(grad_scores, query, 1, 1) + dot(
            probs.astype(jnp.bfloat16), grad, 1, 1
        )
        return acc + dot(kvt_ref[slot, :HEAD_SIZE], grad_scores, 1, 0)

    acc = lax.fori_loop(
        info[2 + slot_now], last + 1, one, jnp.zeros((HEAD_SIZE, WIDE), jnp.float32)
    )
    acc = acc * HEAD_SIZE**-0.5
    acc = jnp.concatenate([acc[:, h * ROWS : (h + 1) * ROWS] for h in range(HEADS)], axis=0)
    gq_ref[...] = rope(acc, cos_ref[...], -sin_ref[...]).astype(jnp.bfloat16)

    if last_call:

        @pl.when(step == count - 1)
        def _():
            for t, ref in enumerate(g_refs):
                for s in range(RING):
                    ref[s * ROWS : (s + 1) * ROWS, :] = gkv_ref[t * RING + s].astype(jnp.bfloat16)


def input_back_kernel(
    info, gq_ref, k0, k1, k2, k3, w_ref, x0, x1, x2, x3, cos_ref, sin_ref, n_ref, gain_two_ref,
    scale_ref, h0, h1, h2, h3, p0, p1, p2, p3, keep_ref, send_ref, row_ref, gkv_ref,
):
    for out, ref in zip((p0, p1, p2, p3), (h0, h1, h2, h3)):
        out[ROWS:] = ref[...]
    y, x, core = info[1], info[6], info[7]
    total = sum(ref[...].astype(jnp.float32) for ref in (k0, k1, k2, k3)).T
    key = rope(total[:HEAD_SIZE], cos_ref[...], -sin_ref[...])
    gkv_ref[...] = jnp.concatenate([key, total[HEAD_SIZE:]], axis=0).astype(jnp.bfloat16)
    row_ref[:, : 4 * ROWS] = gq_ref[...].T
    row_ref[:, 4 * ROWS :] = gkv_ref[...].T
    gains = []
    for xc in range(CHUNKS):
        columns = slice(xc * CHUNK, (xc + 1) * CHUNK)
        product = dot(row_ref[...], w_ref[:, columns], 1, 0)
        gain = jnp.zeros((1, CHUNK), jnp.float32)
        for s, (ref, inputs) in enumerate(zip((p0, p1, p2, p3), (x0, x1, x2, x3))):
            piece = product[s * ROWS : (s + 1) * ROWS]
            ref[:ROWS, columns] = piece.astype(jnp.bfloat16)
            scale = scale_ref[s * ROWS : (s + 1) * ROWS, :1]
            unit = inputs[:, columns].astype(jnp.float32) * scale
            gain += jnp.sum(piece * unit, axis=0, keepdims=True)
        gains.append(gain)
    gains_two = [gain_two_ref[:, xc * CHUNK : (xc + 1) * CHUNK] for xc in range(CHUNKS)]
    gains = sum(
        dot(jnp.concatenate(rows, axis=0).astype(jnp.bfloat16), gain_spread(which, True), 1, 0)
        for which, rows in enumerate((gains, gains_two))
    )
    kv_all = dot(gkv_ref[...], n_ref[...], 1, 0)
    for xc in range(CHUNKS):
        kv = kv_all[:, xc * CHUNK : (xc + 1) * CHUNK].T
        for home in range(RING):
            halves = [
                jnp.concatenate(
                    [
                        kv[z * 64 + home * 16 : z * 64 + home * 16 + 16]
                        for z in (2 * side, 2 * side + 1)
                    ],
                    axis=0,
                )
                for side in range(2)
            ]
            piece = jnp.broadcast_to(gains[xc : xc + 1, home * 128 : (home + 1) * 128], (16, 128))
            piece = jnp.concatenate(
                [jnp.concatenate(halves, axis=1), jnp.concatenate([piece, piece], axis=1)], axis=0
            ).astype(jnp.bfloat16)
            slots = turned(x, xc // 2), turned(y, home)

            @pl.when(core == xc % 2)
            def _(slots=slots, piece=piece):
                keep_ref[slots[0], slots[1]] = piece

            @pl.when(core != xc % 2)
            def _(slots=slots, piece=piece):
                send_ref[slots[0], slots[1]] = piece


def grad_output_query_kernel(info, o_ref, gq_ref, d0, d1, d2, d3, n_ref, keep_ref, send_ref):
    y, core = info[1], info[7]
    for c, out in ((core, keep_ref), (1 - core, send_ref)):
        columns = place_of(c, CHUNK)
        rows = jnp.concatenate([ref[:, columns] for ref in (d0, d1, d2, d3)], axis=0)
        grad_output = dot(o_ref[...], rows, 1, 0).astype(jnp.bfloat16)
        grad_query = dot(gq_ref[...], n_ref[:, columns], 1, 0).astype(jnp.bfloat16)
        for home in range(RING):
            slot = turned(y, home)
            out[0, slot, :ROWS] = part(grad_output, home, ROWS)
            out[0, slot, ROWS:] = part(grad_query, home, ROWS)


def feed_kernel(
    info, n0, n1, d0, d1, w_hbm, keep_ref, send_ref, h_ref, p0, p1,
    gu_ref, down_ref, n_ref, d_ref, hg_ref, row_ref, slot_ref, sems, slot_sems,
):
    units = gu_ref.shape[2]
    half = units // 2
    first = info[7] == 0

    def fetch(xc, y):
        columns = pl.ds(xc * CHUNK, CHUNK)
        return (
            pltpu.make_async_copy(
                w_hbm.at[xc, y, pl.ds(0, 2)], gu_ref.at[y, :, :, columns], sems.at[0, y, xc]
            ),
            pltpu.make_async_copy(w_hbm.at[xc, y, 2], down_ref.at[y, :, columns], sems.at[1, y, xc]),
        )

    slots = [
        pltpu.make_async_copy(ref, slot_ref.at[i], slot_sems.at[i])
        for i, ref in enumerate((n0, n1, d0, d1))
    ]
    for copy in slots:
        copy.start()
    for xc in range(CHUNKS):
        for copy in fetch(xc, 0):
            copy.start()
    for i, copy in enumerate(slots):
        copy.wait()
        out = (n_ref, d_ref)[i // 2]
        out[:, i % 2 * ROWS : (i % 2 + 1) * ROWS] = slot_ref[i].T
    for xc in range(CHUNKS):
        for copy in fetch(xc, 1):
            copy.start()

    def one(y, _):
        @pl.when(y < RING - 2)
        def _():
            for xc in range(CHUNKS):
                for copy in fetch(xc, y + 2):
                    copy.start()

        for xc in range(CHUNKS):
            for copy in fetch(xc, y):
                copy.wait()
        gate_up = dot(gu_ref[y].reshape(2 * units, MODEL_WIDTH), n_ref[...], 1, 0)
        grad_hidden = dot(down_ref[y], d_ref[...], 1, 0)
        gate, upper = gate_up[:units], gate_up[units:]
        sig = 1.0 / (1.0 + jnp.exp(-gate))
        silu = gate * sig
        grad_gate = grad_hidden * upper * (sig + silu * (1.0 - sig))
        grad_up = grad_hidden * silu
        hidden = silu * upper
        hg_ref[y, 0] = grad_gate.astype(jnp.bfloat16)
        hg_ref[y, 1] = grad_up.astype(jnp.bfloat16)
        h_ref[y] = hidden.astype(jnp.bfloat16)
        for k, value in enumerate((grad_gate, grad_up, hidden)):
            low, high = value[:half], value[half:]
            keep_ref[y, k] = jnp.where(first, low, high).astype(jnp.bfloat16)
            send_ref[y, k] = jnp.where(first, high, low).astype(jnp.bfloat16)
        return 0

    lax.fori_loop(0, RING, one, 0)
    row_ref[...] = hg_ref[...].reshape(RING * 2 * units, 2 * ROWS).T

    def back(i, _):
        columns = place_of(i, 2 * CHUNK)
        weights = gu_ref[:, :, :, columns].reshape(RING * 2 * units, 2 * CHUNK)
        total = dot(row_ref[...], weights, 1, 0).astype(jnp.bfloat16)
        p0[:, columns], p1[:, columns] = total[:ROWS], total[ROWS:]
        return 0

    lax.fori_loop(0, CHUNKS // 2, back, 0)


def half_rows(refs):
    return jnp.concatenate([refs[s][...] for s in HALVES], axis=0)


def feed_grad_kernel(
    keep0, keep1, other0, other1, n0, n1, n2, n3, n_other, d0, d1, d2, d3, d_other, g_hbm, gu_ref, down_ref, g_ref, sems
):
    units = keep0.shape[2]
    step = pl.program_id(0)

    @pl.when(step == 0)
    def _():
        for index, ref in enumerate((keep0, keep1, other0, other1)):
            columns = slice(index * 2 * ROWS, (index + 1) * 2 * ROWS)
            gu_ref[:, columns] = ref[:, :2].reshape(RING * 2 * units, 2 * ROWS)
            down_ref[:, columns] = ref[:, 2].reshape(RING * units, 2 * ROWS)

    rows = jnp.concatenate([half_rows((n0, n1, n2, n3)), n_other[...]], axis=0)
    grad = dot(gu_ref[...], rows, 1, 0).astype(jnp.bfloat16)
    g_ref[step, :, :2] = grad.reshape(RING, 2, units, 2 * CHUNK)
    rows = jnp.concatenate([half_rows((d0, d1, d2, d3)), d_other[...]], axis=0)
    grad = dot(down_ref[...], rows, 1, 0).astype(jnp.bfloat16)
    g_ref[step, :, 2] = grad.reshape(RING, units, 2 * CHUNK)
    pltpu.make_async_copy(g_ref.at[step], g_hbm.at[step], sems.at[step]).start()

    @pl.when(step == RING - 1)
    def _():
        for x in range(RING):
            pltpu.make_async_copy(g_ref.at[x], g_hbm.at[x], sems.at[x]).wait()


def feed_down_kernel(h0_ref, h1_ref, w_hbm, p0, p1, p2, p3, row_ref, w_ref, sems):
    units = h0_ref.shape[1]
    copies = [
        [
            pltpu.make_async_copy(
                w_hbm.at[xc, y, 2],
                w_ref.at[xc // 2, pl.ds(y * units, units), pl.ds(xc % 2 * CHUNK, CHUNK)],
                sems.at[xc, y],
            )
            for xc in (2 * step, 2 * step + 1)
            for y in range(RING)
        ]
        for step in range(CHUNKS // 2)
    ]
    for group in copies:
        for copy in group:
            copy.start()
    for half, ref in enumerate((h0_ref, h1_ref)):
        row_ref[half * 2 * ROWS : (half + 1) * 2 * ROWS] = (
            ref[...].reshape(RING * units, 2 * ROWS).T
        )
    for step, group in enumerate(copies):
        for copy in group:
            copy.wait()
        total = dot(row_ref[...], w_ref[step], 1, 0).astype(jnp.bfloat16)
        for index, ref in enumerate((p1, p3, p0, p2)):
            ref[:, step * 2 * CHUNK : (step + 1) * 2 * CHUNK] = part(total, index, ROWS)


def residual_back_kernel(g0, g1, g2, g3, h_ref, dy_ref, gain_ref, dh_ref, dh_low_ref, gg_ref):
    grad = sum(ref[...].astype(jnp.float32) for ref in (g0, g1, g2, g3))
    scale = rms_scale(h_ref[...])
    unit = h_ref[...] * scale

    @pl.when(pl.program_id(0) == 0)
    def _():
        gg_ref[...] = jnp.zeros_like(gg_ref)

    gg_ref[...] += jnp.sum(grad * unit, axis=0, keepdims=True)
    out = dy_ref[...].astype(jnp.float32) + norm_back(unit, scale, gain_ref[...], grad)
    dh_ref[...] = out
    dh_low_ref[...] = out.astype(jnp.bfloat16)


def whole(shape):
    return pl.BlockSpec(shape, lambda *_: (0,) * len(shape))


def struct(shape, dtype=jnp.bfloat16):
    return jax.ShapeDtypeStruct(shape, dtype)


def cost(flops, moved, exps=0):
    return pl.CostEstimate(flops=flops, bytes_accessed=moved, transcendentals=exps)


def params(mebibytes):
    return pltpu.CompilerParams(vmem_limit_bytes=mebibytes << 20)


SLOT = (ROWS, MODEL_WIDTH)
SPLIT = ((1, 3), (0, 2))
SPLIT_BACK = ((0, 1, 3), (2,))


def columns_of(slots, rows):
    return pl.BlockSpec((rows, ROWS), lambda s, info: (0, slot_of(slots, s)))


def row_of(slots, width):
    return pl.BlockSpec((1, 1, width), lambda s, info: (slot_of(slots, s), 0, 0))


def hbm(value):
    return pltpu.with_memory_space_constraint(value, pltpu.HBM)


def project_qkv(info, x_slots, pack, k_slots, k_other, cosine, sine):
    return pl.pallas_call(
        qkv_kernel,
        grid_spec=pltpu.PrefetchScalarGridSpec(
            num_scalar_prefetch=1,
            grid=(1,),
            in_specs=[whole(SLOT)] * 4
            + [pl.BlockSpec(memory_space=pltpu.HBM)]
            + [whole((RING, 48, CHUNK))] * 4
            + [whole((RING, RING, 48, CHUNK))]
            + [whole((32, TOKENS))] * 2,
            out_specs=[
                whole((TOKENS, MODEL_WIDTH)),
                whole((512, TOKENS)),
                whole((TOKENS, 128)),
                whole((640, MODEL_WIDTH)),
                whole((2, MODEL_WIDTH)),
                whole((TOKENS, 128)),
            ],
            scratch_shapes=[
                pltpu.VMEM((CHUNKS, CHUNK, 128), jnp.bfloat16),
                pltpu.VMEM((CHUNKS, RING, 16, 128), jnp.float32),
                pltpu.SemaphoreType.DMA((CHUNKS, RING)),
            ],
        ),
        out_shape=[
            struct((TOKENS, MODEL_WIDTH)),
            struct((512, TOKENS)),
            struct((TOKENS, 128)),
            struct((640, MODEL_WIDTH)),
            struct((2, MODEL_WIDTH), jnp.float32),
            struct((TOKENS, 128), jnp.float32),
        ],
        compiler_params=params(32),
        cost_estimate=cost(2 * 640 * TOKENS * MODEL_WIDTH, 9 << 20),
        name="project_qkv",
    )(info, *map(hbm, x_slots), hbm(pack), *k_slots, k_other, cosine, sine)


def attend(slots, info, q_t, kv, starts, pack=None, shared=()):
    count = len(slots)
    walls = [whole((512, MODEL_WIDTH)), whole((BLOCKS, 128, ROWS))]
    shapes = [struct((512, MODEL_WIDTH)), struct((BLOCKS, 128, ROWS))]
    return pl.pallas_call(
        functools.partial(attend_kernel, slots),
        grid_spec=pltpu.PrefetchScalarGridSpec(
            num_scalar_prefetch=1,
            grid=(count,),
            in_specs=[columns_of(slots, 512), whole((BLOCKS, ROWS, 128)), row_of(slots, ROWS)]
            + (walls if shared else [pl.BlockSpec(memory_space=pltpu.HBM)]),
            out_specs=[
                pl.BlockSpec((512, ROWS), lambda s, info: (0, s)),
                pl.BlockSpec((1, 1, WIDE), lambda s, info: (s, 0, 0)),
            ]
            + [whole(SLOT)] * count
            + ([] if shared else walls),
            scratch_shapes=[] if shared else [pltpu.SemaphoreType.DMA((CHUNKS, RING))],
        ),
        out_shape=[struct((512, count * ROWS)), struct((count, 1, WIDE), jnp.float32)]
        + [struct(SLOT)] * count
        + ([] if shared else shapes),
        compiler_params=params(16),
        cost_estimate=cost(
            count * HEADS * TOKENS * 640 * 128 + count * 512 * ROWS * 2 * MODEL_WIDTH,
            6 << 20,
            count * HEADS * ROWS * 640,
        ),
        name="attend",
    )(info, q_t, kv, starts, *(shared or [hbm(pack)]))


def attend_back(
    slots, info, q_t, dh_slots, wall, o_t, lse, kv, kv_t, starts, cosine, sine, before=None
):
    count = len(slots)
    sums = (BLOCKS, ROWS, 128)
    out_specs = [pl.BlockSpec((512, ROWS), lambda s, info: (0, s))]
    out_shape = [struct((512, count * ROWS))]
    scratch_shapes = []
    if before is None:
        out_specs += [whole(sums)]
        out_shape += [struct(sums, jnp.float32)]
    else:
        out_specs += [whole((TOKENS, 128))] * 4
        out_shape += [struct((TOKENS, 128))] * 4
        scratch_shapes += [pltpu.VMEM(sums, jnp.float32)]
    return pl.pallas_call(
        functools.partial(attend_back_kernel, slots),
        grid_spec=pltpu.PrefetchScalarGridSpec(
            num_scalar_prefetch=1,
            grid=(count,),
            in_specs=[columns_of(slots, 512)]
            + [whole(SLOT)] * count
            + [
                whole((512, MODEL_WIDTH)),
                columns_of(slots, 512),
                row_of(slots, WIDE),
                whole((BLOCKS, ROWS, 128)),
                whole((BLOCKS, 128, ROWS)),
                row_of(slots, ROWS),
                columns_of(slots, HEAD_SIZE // 2),
                columns_of(slots, HEAD_SIZE // 2),
            ]
            + ([] if before is None else [whole(sums)]),
            out_specs=out_specs,
            scratch_shapes=scratch_shapes + [pltpu.VMEM((count, *SLOT), jnp.bfloat16)],
        ),
        out_shape=out_shape,
        compiler_params=params(18),
        cost_estimate=cost(
            3 * count * HEADS * ROWS * 640 * 128 * 4 + count * 512 * ROWS * 2 * MODEL_WIDTH,
            8 << 20,
            count * HEADS * ROWS * 640,
        ),
        name="attend_back",
    )(
        info, q_t, *dh_slots, wall, o_t, lse, kv, kv_t, starts, cosine, sine,
        *([] if before is None else [before]),
    )


def input_back(info, gq_t, gkv_slots, w_qkv, x_slots, cosine, sine, normed, gain_two, scales, down):
    pieces = (RING, RING, 48, CHUNK)
    return pl.pallas_call(
        input_back_kernel,
        grid_spec=pltpu.PrefetchScalarGridSpec(
            num_scalar_prefetch=1,
            grid=(1,),
            in_specs=[whole((512, TOKENS))]
            + [whole((TOKENS, 128))] * 4
            + [whole((640, MODEL_WIDTH))]
            + [whole(SLOT)] * 4
            + [whole((32, TOKENS))] * 2
            + [whole((TOKENS, MODEL_WIDTH)), whole((1, MODEL_WIDTH)), whole((TOKENS, 128))]
            + [whole(SLOT)] * 4,
            out_specs=[whole((2 * ROWS, MODEL_WIDTH))] * 4 + [whole(pieces)] * 2,
            scratch_shapes=[
                pltpu.VMEM((TOKENS, 640), jnp.bfloat16),
                pltpu.VMEM((128, TOKENS), jnp.bfloat16),
            ],
        ),
        out_shape=[pltpu.HBM((2 * ROWS, MODEL_WIDTH), jnp.bfloat16)] * 4 + [struct(pieces)] * 2,
        compiler_params=params(32),
        cost_estimate=cost(2 * 768 * TOKENS * MODEL_WIDTH, 15 << 20),
        name="input_back",
    )(
        info, gq_t, *gkv_slots, w_qkv, *map(hbm, x_slots), cosine, sine, normed, gain_two, scales, *down,
    )


def pack_specs(rows):
    spec = pl.BlockSpec((1, RING, rows, CHUNK), lambda s, info: (s, 0, 0, 0))
    return [spec, spec], [struct((RING, RING, rows, CHUNK))] * 2


def pair_columns(rows):
    return pl.BlockSpec((rows, 2 * CHUNK), lambda s, info: (0, (info[6] + RING - s) % RING))


def grad_output_query(info, o_t, gq_t, dh_slots, normed):
    out_specs, out_shape = pack_specs(2 * ROWS)
    return pl.pallas_call(
        grad_output_query_kernel,
        grid_spec=pltpu.PrefetchScalarGridSpec(
            num_scalar_prefetch=1,
            grid=(RING,),
            in_specs=[whole((512, TOKENS))] * 2
            + [pair_columns(ROWS)] * 4
            + [pair_columns(TOKENS)],
            out_specs=out_specs,
        ),
        out_shape=out_shape,
        compiler_params=params(14),
        cost_estimate=cost(4 * 512 * TOKENS * MODEL_WIDTH, 9 << 20),
        name="grad_output_query",
    )(info, o_t, gq_t, *dh_slots, normed)


def feed(info, n_pair, d_pair, weights):
    units = weights.shape[3]
    pair = (2 * ROWS, MODEL_WIDTH)
    split = (RING, 3, units // 2, 2 * ROWS)
    return pl.pallas_call(
        feed_kernel,
        in_specs=[pl.BlockSpec(memory_space=pltpu.SMEM)]
        + [pl.BlockSpec(memory_space=pl.ANY)] * 4
        + [pl.BlockSpec(memory_space=pltpu.HBM)],
        out_specs=[pl.BlockSpec(memory_space=pltpu.VMEM)] * 5,
        out_shape=[struct(split)] * 2 + [struct((RING, units, 2 * ROWS))] + [struct(SLOT)] * 2,
        scratch_shapes=[
            pltpu.VMEM((RING, 2, units, MODEL_WIDTH), jnp.bfloat16),
            pltpu.VMEM((RING, units, MODEL_WIDTH), jnp.bfloat16),
            pltpu.VMEM(pair[::-1], jnp.bfloat16),
            pltpu.VMEM(pair[::-1], jnp.bfloat16),
            pltpu.VMEM((RING, 2, units, 2 * ROWS), jnp.bfloat16),
            pltpu.VMEM((2 * ROWS, RING * 2 * units), jnp.bfloat16),
            pltpu.VMEM((4, *SLOT), jnp.bfloat16),
            pltpu.SemaphoreType.DMA((2, RING, CHUNKS)),
            pltpu.SemaphoreType.DMA((4,)),
        ],
        compiler_params=params(30),
        cost_estimate=cost(5 * RING * units * TOKENS * MODEL_WIDTH, 23 << 20, RING * units * TOKENS // 2),
        name="feed",
    )(info, *map(hbm, n_pair), *map(hbm, d_pair), hbm(weights))


def feed_grad(keeps, others, n_slots, n_other, d_slots, d_other):
    units = keeps[0].shape[2]
    slots = [pl.BlockSpec((ROWS, 2 * CHUNK), lambda i: (0, i))] * 4
    slots += [pl.BlockSpec((TOKENS, 2 * CHUNK), lambda i: (0, i))]
    out = (RING, RING, 3, units, 2 * CHUNK)
    return pl.pallas_call(
        feed_grad_kernel,
        grid=(RING,),
        in_specs=[whole(keeps[0].shape)] * 4 + slots * 2,
        out_specs=pl.BlockSpec(memory_space=pltpu.HBM),
        out_shape=pltpu.HBM(out, jnp.bfloat16),
        scratch_shapes=[
            pltpu.VMEM((RING * 2 * units, 2 * TOKENS), jnp.bfloat16),
            pltpu.VMEM((RING * units, 2 * TOKENS), jnp.bfloat16),
            pltpu.VMEM(out, jnp.bfloat16),
            pltpu.SemaphoreType.DMA((RING,)),
        ],
        compiler_params=params(30),
        cost_estimate=cost(12 * RING * units * TOKENS * MODEL_WIDTH, 22 << 20),
        name="feed_grad",
    )(*keeps, *others, *map(hbm, n_slots), hbm(n_other), *map(hbm, d_slots), hbm(d_other))


def last_kernel(*refs):
    (gn_refs, down_refs), refs = (refs[:RING], refs[RING : 2 * RING]), refs[2 * RING :]
    h_ref, dh_ref, x_ref, gain_ref, result_ref, grad_ref = refs
    down = sum(ref[...].astype(jnp.float32) for ref in down_refs)
    result_ref[...] = (h_ref[...] + down).astype(jnp.bfloat16)
    grad = sum(ref[...].astype(jnp.float32) for ref in gn_refs)
    value = x_ref[...].astype(jnp.float32)
    scale = rms_scale(value)
    out = dh_ref[...] + norm_back(value * scale, scale, gain_ref[...], grad)
    grad_ref[...] = out.astype(jnp.bfloat16)


def last(parts, h1, dh1, inputs, gain):
    half = ROWS // 2
    rows = pl.BlockSpec((half, MODEL_WIDTH), lambda i: (i, 0))
    lower = pl.BlockSpec((half, MODEL_WIDTH), lambda i: (i + 2, 0))
    vector = pl.BlockSpec((1, MODEL_WIDTH), lambda i: (0, 0))
    return pl.pallas_call(
        last_kernel,
        grid=(2,),
        in_specs=[rows] * 4 + [lower] * 4 + [rows] * 3 + [vector],
        out_specs=[rows] * 2,
        out_shape=[struct(SLOT)] * 2,
        compiler_params=params(16),
        cost_estimate=cost(30 * ROWS * MODEL_WIDTH, 8 << 20),
        name="last",
    )(*map(hbm, parts), *map(hbm, parts), hbm(h1), hbm(dh1), hbm(inputs), gain)


def residual_back(grads, h1, out_grad, gain):
    rows = pl.BlockSpec((ROWS // 2, MODEL_WIDTH), lambda i: (i, 0))
    vector = pl.BlockSpec((1, MODEL_WIDTH), lambda i: (0, 0))
    return pl.pallas_call(
        residual_back_kernel,
        grid=(2,),
        in_specs=[rows] * 6 + [vector],
        out_specs=[rows, rows, vector],
        out_shape=[struct(SLOT, jnp.float32), struct(SLOT), struct((1, MODEL_WIDTH), jnp.float32)],
        compiler_params=params(16),
        cost_estimate=cost(30 * ROWS * MODEL_WIDTH, 5 << 20),
        name="residual_back",
    )(*map(hbm, grads), hbm(h1), hbm(out_grad), gain)


def feed_down(hs, weights):
    units = hs[0].shape[1]
    return pl.pallas_call(
        feed_down_kernel,
        in_specs=[pl.BlockSpec(memory_space=pltpu.VMEM)] * 2 + [pl.BlockSpec(memory_space=pltpu.HBM)],
        out_specs=[pl.BlockSpec(memory_space=pltpu.VMEM)] * 4,
        out_shape=[struct(SLOT)] * 4,
        scratch_shapes=[
            pltpu.VMEM((TOKENS, RING * units), jnp.bfloat16),
            pltpu.VMEM((CHUNKS // 2, RING * units, 2 * CHUNK), jnp.bfloat16),
            pltpu.SemaphoreType.DMA((CHUNKS, RING)),
        ],
        compiler_params=params(18),
        cost_estimate=cost(2 * RING * units * TOKENS * MODEL_WIDTH, 9 << 20),
        name="feed_down",
    )(*hs, hbm(weights))


def adamw(weight, first, second, grad, rate, decay):
    first_new = BETA_ONE * first + (1.0 - BETA_ONE) * grad
    second_new = BETA_TWO * second + (1.0 - BETA_TWO) * grad * grad
    fix_one = 1.0 - BETA_ONE**STEP
    fix_two = 1.0 - BETA_TWO**STEP
    update = first_new / fix_one / (jnp.sqrt(second_new / fix_two) + ADAM_EPS)
    return (weight - rate * (update + decay * weight), first_new, second_new)


def adam_feed_kernel(info, own_ref, other_ref, *refs):
    step, core = pl.program_id(0), info[7]
    own = jnp.where(core == 0, own_ref[:, :, :CHUNK], own_ref[:, :, CHUNK:])
    grad = jnp.where(step == core, own, other_ref[...]).astype(jnp.float32)
    for k, (g, rate) in enumerate(((grad[:2], MODEL_WIDTH**-0.5), (grad[2], FF**-0.5))):
        ins, outs = refs[3 * k : 3 * k + 3], refs[6 + 3 * k : 9 + 3 * k]
        values = adamw(*(ref[...] for ref in ins), g, rate, DECAY)
        for ref, value in zip(outs, values):
            ref[...] = value


def adam_feed(info, own, other, gateup, down):
    units = down[0].shape[0]
    half = units // 2
    specs = [pl.BlockSpec((2, half, CHUNK), lambda i, info: (0, i, 0))] * 3
    specs += [pl.BlockSpec((half, CHUNK), lambda i, info: (i, 0))] * 3
    arrays = [*gateup, *down]
    return pl.pallas_call(
        adam_feed_kernel,
        grid_spec=pltpu.PrefetchScalarGridSpec(
            num_scalar_prefetch=1,
            grid=(2,),
            in_specs=[whole(own.shape), whole(other.shape)] + specs,
            out_specs=specs,
        ),
        out_shape=[struct(a.shape, jnp.float32) for a in arrays],
        compiler_params=params(16),
        cost_estimate=cost(30 * 3 * units * CHUNK, 24 * 3 * units * CHUNK),
        name="adam_feed",
    )(info, hbm(own), other, *map(hbm, arrays))


def adam_attention_kernel(*refs):
    parts, refs = refs[:RING], refs[RING:]
    total = sum(ref[: 2 * ROWS].astype(jnp.float32) for ref in parts)
    grads = total[ROWS:].T, total[:ROWS]
    for k, (g, rate) in enumerate(zip(grads, (MODEL_WIDTH**-0.5, (MODEL_WIDTH // 64) ** -0.5))):
        ins, outs = refs[3 * k : 3 * k + 3], refs[6 + 3 * k : 9 + 3 * k]
        values = adamw(*(ref[...] for ref in ins), g, rate, DECAY)
        for ref, value in zip(outs, values):
            ref[...] = value


def adam_attention(parts, query, output):
    arrays = [*query, *output]
    specs = [whole(a.shape) for a in arrays]
    return pl.pallas_call(
        adam_attention_kernel,
        grid=(1,),
        in_specs=[whole(p.shape) for p in parts] + specs,
        out_specs=specs,
        out_shape=[struct(a.shape, jnp.float32) for a in arrays],
        compiler_params=params(16),
        cost_estimate=cost(60 * ROWS * CHUNK, 50 * ROWS * CHUNK),
        name="adam_attention",
    )(*parts, *map(hbm, arrays))


def swap_cores(value):
    return lax.ppermute(value, "core", [(0, 1), (1, 0)])


def scatter_core(keep, other):
    return [
        (keep[s].astype(jnp.float32) + other[s].astype(jnp.float32)).astype(jnp.bfloat16)
        for s in range(RING)
    ]


def sum_x(parts):
    return [
        sum(p[s].astype(jnp.float32) for p in parts).astype(jnp.bfloat16) for s in range(RING)
    ]


def after(values, *others):
    return lax.optimization_barrier((list(values), others))[0]


def local(
    block_input,
    out_grad,
    segments,
    w_query,
    keyvalue_weights,
    w_output,
    w_gateup,
    w_down,
    norm_gains,
    query_first,
    keyval_moment_one,
    output_first,
    gateup_first,
    down_first,
    gains_first,
    query_second,
    keyval_moment_two,
    output_second,
    gateup_second,
    down_second,
    gains_second,
):
    bf16, f32 = jnp.bfloat16, jnp.float32
    x, core, z, y = (lax.axis_index(name) for name in ("x", "core", "z", "y"))
    units = w_down.shape[0]

    kv_rows = keyvalue_weights.astype(bf16).reshape(2, 16, RING, HEAD_SIZE).transpose(2, 1, 0, 3)
    message = jnp.concatenate(
        [
            kv_rows.reshape(RING, 16, 128),
            jnp.broadcast_to(
                jnp.pad(norm_gains.astype(bf16).reshape(1, 1, 32), ((0, 0), (0, 15), (0, 96))),
                (RING, 16, 128),
            ),
        ],
        1,
    )
    small = absolute(scatter_ring_from(relative(message, z), "z"), z)
    kv_piece = jnp.concatenate(
        [small[:2, :16].reshape(32, 128), small[2:, :16].reshape(32, 128)], 1
    )
    gain_piece = jnp.pad(small[:, 16, :32].reshape(1, 128), ((0, 15), (0, 128)))
    kv_piece = jnp.concatenate([kv_piece, gain_piece], 0)

    pack = jnp.concatenate([w_output.astype(bf16), w_query.astype(bf16).T], 0)
    pack = lax.all_gather(pack, SHARE, axis=0, tiled=False)
    x_slots = gather_far_last(block_input, "z")
    (kv_piece,) = after([jnp.stack(gather_ring(kv_piece, "x"))], x_slots[1], x_slots[3])
    k_slots = gather_ring(kv_piece, "y")
    k_other = swap_cores(jnp.stack(after(k_slots, x_slots[2])))
    d_slots = gather_far_last(after([out_grad], *x_slots[1:])[0], "z")
    feed_shard = jnp.concatenate(
        [w_gateup.astype(bf16).transpose(0, 2, 1), w_down.astype(bf16)[None]], 0
    )
    (feed_shard,) = after([feed_shard], pack, d_slots[1], d_slots[3], k_other)
    w_feed = lax.all_gather(feed_shard, SHARE, axis=0, tiled=False)
    w_feed = w_feed.reshape(CHUNKS, RING, 3, units, CHUNK)

    starts = doc_starts(segments[0])
    by_block = lax.dynamic_index_in_dim(starts.reshape(RING, RING, ROWS), y, 1, keepdims=False)
    row_starts = jnp.stack(relative(by_block, z))
    places = (z + RING - jnp.arange(RING, dtype=jnp.int32)) % RING
    begins = places * (RING * ROWS) + y * ROWS
    positions = (begins[:, None] + jnp.arange(ROWS, dtype=jnp.int32) - row_starts).reshape(-1)
    half = HEAD_SIZE // 2
    freqs = 10000.0 ** (-jnp.arange(half, dtype=f32) * 2.0 / HEAD_SIZE)
    angles = freqs[:, None] * positions.astype(f32)[None, :]
    cosine, sine = jnp.cos(angles), jnp.sin(angles)
    info = jnp.concatenate(
        [
            jnp.stack([z, y]).astype(jnp.int32),
            row_starts[:, 0] // ROWS,
            jnp.stack([x, core]).astype(jnp.int32),
        ]
    )
    row_starts = row_starts[:, None, :]

    normed, q_t, kv_own, w_qkv, gains, scales = project_qkv(
        info, x_slots, pack, k_slots, k_other, cosine, sine
    )
    kv = jnp.stack(gather_ring(kv_own, "y")).reshape(BLOCKS, ROWS, 2 * HEAD_SIZE)
    d_all = jnp.concatenate([d_slots[s] for s in HALVES], 0)
    q_t, d_all = after([q_t, d_all])
    d_other = swap_cores(d_all)
    near_o, near_lse, o_1, o_3, *shared = attend(SPLIT[0], info, q_t, kv, row_starts, pack)
    wo, kv_t = shared
    (q_late,) = after([q_t], o_1, d_slots[2])
    far_o, far_lse, o_0, o_2 = attend(SPLIT[1], info, q_late, kv, row_starts, shared=shared)
    o_t = jnp.concatenate(
        [far_o[:, :ROWS], near_o[:, :ROWS], far_o[:, ROWS:], near_o[:, ROWS:]], 1
    )
    lse = jnp.stack([far_lse[0], near_lse[0], far_lse[1], near_lse[1]])
    o_1, o_3 = after([o_1, o_3], d_slots[2])
    o_slots = scatter_far_last(o_0, o_1, o_3, o_2, "z")
    o_sum = sum(p.astype(f32) for p in o_slots)
    h1 = block_input.astype(f32) + o_sum

    scale_two = rms_scale(h1)
    unit_two = h1 * scale_two
    (normed_two,) = after([(unit_two * gains[1]).astype(bf16)], d_other)
    n_slots = gather_far_last(normed_two, "z")
    keep0, send0, h0, gn2_1, gn2_3 = feed(
        info, [n_slots[s] for s in HALVES[:2]], [d_slots[s] for s in HALVES[:2]], w_feed
    )
    n_other = after([n_slots[s] for s in HALVES], keep0)
    n_other = swap_cores(jnp.concatenate(n_other, 0))
    keep1, send1, h1_half, gn2_0, gn2_2 = feed(
        info, after([n_slots[s] for s in HALVES[2:]], keep0), [d_slots[s] for s in HALVES[2:]], w_feed
    )
    gn2_slots = scatter_ring([gn2_0, gn2_1, gn2_2, gn2_3], "z")
    other0 = swap_cores(send0)
    (send1,) = after([send1], n_other, other0, gn2_slots[1], gn2_slots[3])
    others = other0, swap_cores(send1)
    grad_feed = feed_grad((keep0, keep1), others, n_slots, n_other, d_slots, d_other)
    *gn2_slots, grad_feed = after([*gn2_slots, grad_feed])
    dh1, dh1_low, grad_gain_two = residual_back(gn2_slots, h1, out_grad, gains[1:])
    own_feed = lax.psum_scatter(
        grad_feed.reshape(16, 3, units // 2, 2 * CHUNK), ("x", "y"), scatter_dimension=0, tiled=False
    )

    down_slots = feed_down(after([h0, h1_half], *gn2_slots), w_feed)
    dh_slots = gather_far_last(dh1_low, "z", *down_slots)
    near, far = SPLIT_BACK
    arguments = wo, o_t, lse, kv, kv_t, row_starts, cosine, sine
    gq_near, sums = attend_back(near, info, q_t, [dh_slots[s] for s in near], *arguments)
    (dh_far,) = after([dh_slots[2]], sums)
    gq_far, *gkv_slots = attend_back(far, info, q_t, [dh_far], *arguments, before=sums)
    gq_t = jnp.concatenate([gq_near[:, : 2 * ROWS], gq_far, gq_near[:, 2 * ROWS :]], 1)
    gkv_slots = scatter_ring(gkv_slots, "y")
    (gq_late,) = after([gq_t], gkv_slots[1], gkv_slots[3])
    keep, send = grad_output_query(info, o_t, gq_late, dh_slots, normed)
    (send,) = after([send], gkv_slots[2])
    gkv_slots = after(gkv_slots, send)
    *gn1_slots, keep_kv, send_kv = input_back(
        info, gq_t, gkv_slots, w_qkv, x_slots, cosine, sine, normed, grad_gain_two, scales, down_slots
    )
    gn1_0, gn1_1, gn1_2, gn1_3 = gn1_slots
    gn1_slots = scatter_far_last(gn1_0, gn1_1, gn1_3, gn1_2, "z")
    parts = zip(scatter_core(keep, swap_cores(send)), scatter_core(keep_kv, swap_cores(send_kv)))
    parts = scatter_ring([jnp.concatenate(p, 1) for p in parts], "x")

    parts_y = scatter_ring(sum_x(parts), "y")

    parts_y = after(parts_y, gn1_slots[2])
    own_pack = sum(p[2 * ROWS :].astype(f32) for p in parts_y)

    kv_piece = own_pack[:32]
    kv_piece = jnp.concatenate([kv_piece[:, :128], kv_piece[:, 128:]], 0).reshape(RING, 16, 128)
    gain_piece = own_pack[32, :128].reshape(RING, 1, 32)
    message = jnp.concatenate([kv_piece, jnp.pad(gain_piece, ((0, 0), (0, 15), (0, 96)))], 1)
    small = scatter_ring_from(relative(message, z), "z")

    result, grad_input = last(after(gn1_slots, *parts_y[1:]), h1, dh1, block_input, gains[:1])
    (own_feed,) = after([own_feed], small[1], grad_input)
    other_send = jnp.where(core == 0, own_feed[..., CHUNK:], own_feed[..., :CHUNK])
    other = swap_cores(other_send)
    attention = adam_attention(
        after(parts_y, other_send),
        (w_query, query_first, query_second),
        (w_output, output_first, output_second),
    )
    q, o = attention[:3], attention[3:]
    turn = (0, 2, 1)
    feed_arrays = adam_feed(
        info,
        own_feed,
        other,
        [a.transpose(turn) for a in (w_gateup, gateup_first, gateup_second)],
        (w_down, down_first, down_second),
    )
    gu = [a.transpose(turn) for a in feed_arrays[:3]]
    down = feed_arrays[3:]
    small[2:] = after(small[2:], *feed_arrays)
    small = absolute(small, z)
    own_kv = small[:, :16].reshape(RING, 16, 2, HEAD_SIZE).transpose(2, 1, 0, 3)
    own_kv = own_kv.reshape(2, 16, RING * HEAD_SIZE)
    own_gains = jnp.sum(small[:, 16, :32], 0).reshape(2, 16)

    rate = MODEL_WIDTH ** (-0.5)
    kvs = adamw(keyvalue_weights, keyval_moment_one, keyval_moment_two, own_kv, rate, DECAY)
    gain = adamw(norm_gains, gains_first, gains_second, own_gains, GAIN_RATE, 0.0)
    updates = (q, kvs, o, gu, down, gain)
    return (result, grad_input, *(u[i] for i in range(3) for u in updates))


def scatter_ring_from(slots, axis):
    own, after, far, before = scatter_ring(slots, axis)
    return [own, before, far, after]


def solution(mesh):
    view = Mesh(mesh.devices.reshape(4, 2, 4, 4), ("x", "core", "z", "y"))
    dp, tensor = ("x", "core"), ("z", "y")
    both = dp + tensor
    tokens = P(both, None)
    weights = (
        P(dp, tensor),
        P(None, both, None),
        P(tensor, dp),
        P(None, dp, tensor),
        P(tensor, dp),
        P(None, both),
    )
    return jax.shard_map(
        local,
        mesh=view,
        in_specs=(tokens, tokens, P(dp, None), *weights * 3),
        out_specs=(tokens, tokens, *weights * 3),
        check_vma=False,
    )
```

```python
import functools

import jax
import jax.numpy as jnp
from jax import lax
from jax.experimental import pallas as pl
from jax.experimental.pallas import tpu as pltpu
from jax.sharding import Mesh
from jax.sharding import PartitionSpec as P

MODEL_WIDTH = 2048
QUERY_HEADS = 32
KEYVALUE_HEADS = 4
HEAD_SIZE = 64
FF = 5632
STEP = 10

BETA_ONE = 0.9
BETA_TWO = 0.95
ADAM_EPS = 1e-08
DECAY = 0.1
GAIN_RATE = 0.8
NORM_EPS = 1e-05

RING = 4
SHARE = ("x", "core", "y")
ROWS = 128
TOKENS = RING * ROWS
HEADS = QUERY_HEADS // RING
WIDE = HEADS * ROWS
BLOCKS = 16
MASKED = -1e30
HALVES = (1, 3, 0, 2)
CHUNKS, CHUNK = 8, 256
PACK = 2 * ROWS + 48


def doc_starts(segment):
    index = jnp.arange(segment.shape[0], dtype=jnp.int32)
    starts = jnp.concatenate([jnp.ones((1,), dtype=bool), segment[1:] != segment[:-1]])
    return lax.cummax(jnp.where(starts, index, 0))


def shift(value, axis, step):
    return lax.ppermute(value, axis, [(i, (i + step) % RING) for i in range(RING)])


def gather_ring(value, axis):
    far = shift(value, axis, 2)
    return [value, shift(value, axis, 1), far, shift(value, axis, 3)]


def gather_far_last(value, axis, *others):
    near = shift(value, axis, 1), shift(value, axis, 3)
    (value_late,) = after([value], *near, *others)
    return [value, near[0], shift(value_late, axis, 2), near[1]]


def scatter_far_last(own, part_one, part_three, part_two, axis):
    near = shift(part_one, axis, 3), shift(part_three, axis, 1)
    (part_two,) = after([part_two], *near)
    return [own, near[0], shift(part_two, axis, 2), near[1]]


def scatter_ring(parts, axis):
    far = shift(parts[2], axis, 2)
    return [parts[0], shift(parts[1], axis, 3), far, shift(parts[3], axis, 1)]


def absolute(slots, own):
    turned = jnp.stack([slots[0], slots[3], slots[2], slots[1]])
    return lax.dynamic_slice_in_dim(jnp.concatenate([turned, turned]), RING - own, RING, 0)


def relative(stacked, own):
    turned = jnp.concatenate([stacked, stacked])
    return [
        lax.dynamic_index_in_dim(turned, own + RING - s if s else own, 0, keepdims=False)
        for s in range(RING)
    ]


def dot(left, right, left_dim, right_dim):
    return lax.dot_general(
        left, right, (((left_dim,), (right_dim,)), ((), ())), preferred_element_type=jnp.float32
    )


def rms_scale(values):
    return lax.rsqrt(jnp.mean(values * values, axis=-1, keepdims=True) + NORM_EPS)


def norm_back(unit, scale, gain, grad):
    scaled = grad * gain
    return scale * (scaled - unit * jnp.mean(scaled * unit, axis=-1, keepdims=True))


def part(ref, index, size):
    return ref[index * size : (index + 1) * size, :]


def heads_side_by_side(value):
    return jnp.concatenate([part(value, h, HEAD_SIZE) for h in range(HEADS)], axis=1)


def mask_parts(info, starts, step):
    z, y = info[0], info[1]
    place = (z + RING - step) % RING
    begin = place * (RING * ROWS) + y * ROWS
    row = begin + lax.broadcasted_iota(jnp.int32, (1, ROWS), 1)
    rows = jnp.concatenate([row] * HEADS, axis=1)
    start = jnp.concatenate([starts] * HEADS, axis=1)
    return z, y, place * RING + y, rows, start


def block_slot(block, z, y):
    return ((y + RING - block % RING) % RING) * RING + (z + RING - block // RING) % RING


def rope(values, cosine, sine):
    half = HEAD_SIZE // 2
    out = []
    for h in range(values.shape[0] // HEAD_SIZE):
        first = values[h * HEAD_SIZE : h * HEAD_SIZE + half]
        second = values[h * HEAD_SIZE + half : (h + 1) * HEAD_SIZE]
        out += [first * cosine - second * sine, first * sine + second * cosine]
    return jnp.concatenate(out, axis=0)


def turned(place, step):
    return (place + RING - step) % RING


def weight_slots(info, own_refs, other_ref):
    y, x, core = info[1], info[6], info[7]
    for cs in range(2):
        for ys in range(RING):
            for xs in range(RING):
                ref = other_ref.at[ys, xs] if cs else own_refs[ys].at[xs]
                yield turned(x, xs) * 2 + (1 - core if cs else core), turned(y, ys), ref


def place_of(index, size):
    return pl.ds(pl.multiple_of(index * size, size), size)


def gain_spread(which, transposed):
    shape = (CHUNK, 512) if transposed else (512, CHUNK)
    lane = lax.broadcasted_iota(jnp.int32, shape, 1 if transposed else 0)
    column = lax.broadcasted_iota(jnp.int32, shape, 0 if transposed else 1)
    y, z, gain, row = lane // 128, lane // 32 % 4, lane // 16 % 2, lane % 16
    same = (column // 64 == z) & (column // 16 % 4 == y) & (column % 16 == row) & (gain == which)
    return jnp.where(same, 1.0, 0.0).astype(jnp.bfloat16)


def fetch_pack(pack_hbm, which, out_ref, sems):
    return [
        pltpu.make_async_copy(
            pack_hbm.at[xc * RING + y, pl.ds(which * ROWS, ROWS)],
            out_ref.at[pl.ds(y * ROWS, ROWS), pl.ds(xc * CHUNK, CHUNK)],
            sems.at[xc, y],
        )
        for xc in range(CHUNKS)
        for y in range(RING)
    ]


def qkv_kernel(
    info, x0, x1, x2, x3, pack_hbm, k0, k1, k2, k3, k_other, cos_ref, sin_ref,
    n_ref, q_ref, kv_ref, w_ref, gain_ref, scale_ref, wkv_ref, piece_ref, sems,
):
    copies = fetch_pack(pack_hbm, 1, w_ref, sems)
    for copy in copies:
        copy.start()
    for chunk, y, ref in weight_slots(info, (k0, k1, k2, k3), k_other):
        for z in range(RING):
            wkv_ref[chunk, pl.ds(pl.multiple_of(z * 64 + y * 16, 16), 16), :] = ref[
                (z % 2) * 16 : (z % 2 + 1) * 16, (z // 2) * 128 : (z // 2 + 1) * 128
            ]
        piece_ref[chunk, y] = ref[32:48, :128].astype(jnp.float32)
    pieces = [
        jnp.concatenate([piece_ref[xc, y, :1] for y in range(RING)], axis=1) for xc in range(CHUNKS)
    ]
    pieces = jnp.concatenate(pieces, axis=0).astype(jnp.bfloat16)
    gains = [dot(pieces, gain_spread(which, False), 1, 0) for which in range(2)]
    for xc in range(CHUNKS):
        columns = slice(xc * CHUNK, (xc + 1) * CHUNK)
        w_ref[4 * ROWS : 5 * ROWS, columns] = wkv_ref[xc].T
        for which in range(2):
            gain_ref[which : which + 1, columns] = gains[which][xc : xc + 1]
    for s, ref in enumerate((x0, x1, x2, x3)):
        value = ref[...].astype(jnp.float32)
        scale = rms_scale(value)
        scale_ref[s * ROWS : (s + 1) * ROWS] = jnp.broadcast_to(scale, (ROWS, 128))
        n_ref[s * ROWS : (s + 1) * ROWS, :] = (value * scale * gain_ref[:1]).astype(jnp.bfloat16)
    for copy in copies:
        copy.wait()
    qkv = dot(w_ref[...], n_ref[...], 1, 1)
    query = rope(qkv[: 4 * ROWS], cos_ref[...], sin_ref[...]).astype(jnp.bfloat16)
    q_ref[...] = query * jnp.bfloat16(HEAD_SIZE**-0.5)
    key = rope(qkv[4 * ROWS : 4 * ROWS + HEAD_SIZE], cos_ref[...], sin_ref[...])
    key_value = jnp.concatenate([key, qkv[4 * ROWS + HEAD_SIZE :]], axis=0)
    kv_ref[...] = key_value.T.astype(jnp.bfloat16)


def slot_of(slots, step):
    out = slots[0]
    for index in range(1, len(slots)):
        out = out + (slots[index] - slots[index - 1]) * ((step + len(slots) - index) // len(slots))
    return out


def attend_kernel(
    slots, info, q_ref, kv_ref, start_ref, *refs
):
    step = pl.program_id(0)
    first_call = 2 not in slots
    if first_call:
        pack_hbm, o_ref, lse_ref, *outs, wall_ref, kvt_ref, sems = refs
        copies = fetch_pack(pack_hbm, 0, wall_ref, sems)

        @pl.when(step == 0)
        def _():
            for copy in copies:
                copy.start()
            for b in range(BLOCKS):
                kvt_ref[b] = kv_ref[b].T
    else:
        wall_ref, kvt_ref, o_ref, lse_ref, *outs = refs

    slot_now = slot_of(slots, step)
    z, y, last, rows, start = mask_parts(info, start_ref[0], slot_now)
    query = heads_side_by_side(q_ref[...])
    query = jnp.concatenate([query, jnp.zeros_like(query)], axis=0)

    def one(block, carry):
        top, total, acc = carry
        slot = block_slot(block, z, y)
        scores = dot(kv_ref[slot], query, 1, 0)
        key = block * ROWS + lax.broadcasted_iota(jnp.int32, (ROWS, 1), 0)
        scores = jnp.where((key >= start) & (key <= rows), scores, MASKED)
        new_top = jnp.maximum(top, jnp.max(scores, axis=0, keepdims=True))
        weights = jnp.exp(scores - new_top)
        fade = jnp.exp(top - new_top)
        total = total * fade + jnp.sum(weights, axis=0, keepdims=True)
        acc = acc * fade + dot(kvt_ref[slot, HEAD_SIZE:], weights.astype(jnp.bfloat16), 1, 0)
        return new_top, total, acc

    top, total, acc = lax.fori_loop(
        info[2 + slot_now],
        last + 1,
        one,
        (
            jnp.full((1, WIDE), MASKED, jnp.float32),
            jnp.zeros((1, WIDE), jnp.float32),
            jnp.zeros((HEAD_SIZE, WIDE), jnp.float32),
        ),
    )
    out = acc / total
    out = jnp.concatenate([out[:, h * ROWS : (h + 1) * ROWS] for h in range(HEADS)], axis=0)
    o_ref[...] = out.astype(jnp.bfloat16)
    lse_ref[0] = top + jnp.log(total)
    if first_call:

        @pl.when(step == 0)
        def _():
            for copy in copies:
                copy.wait()

    product = dot(out.T.astype(jnp.bfloat16), wall_ref[...], 1, 0).astype(jnp.bfloat16)
    for s, ref in enumerate(outs):

        @pl.when(step == s)
        def _(ref=ref):
            ref[...] = product


def attend_back_kernel(slots, info, q_ref, *refs):
    count = len(slots)
    d_refs, refs = refs[:count], refs[count:]
    wall_ref, o_ref, lse_ref, kv_ref, kvt_ref, start_ref, cos_ref, sin_ref, *refs = refs
    last_call = slots[-1] == 2
    if last_call:
        before_ref, gq_ref, *g_refs, gkv_ref, dh_ref = refs
    else:
        gq_ref, gkv_ref, dh_ref = refs
    step = pl.program_id(0)

    @pl.when(step == 0)
    def _():
        if last_call:
            gkv_ref[...] = before_ref[...]
        else:
            gkv_ref[...] = jnp.zeros_like(gkv_ref)
        for s, ref in enumerate(d_refs):
            dh_ref[s] = ref[...]

    slot_now = slot_of(slots, step)
    z, y, last, rows, start = mask_parts(info, start_ref[0], slot_now)
    query = heads_side_by_side(q_ref[...])
    grad = dot(wall_ref[...], dh_ref[step], 1, 1).astype(jnp.bfloat16)
    grad = heads_side_by_side(grad)
    out = heads_side_by_side(o_ref[...])
    rowdot = jnp.sum(grad.astype(jnp.float32) * out.astype(jnp.float32), axis=0, keepdims=True)
    query = jnp.concatenate([query, jnp.zeros_like(query)], axis=0)
    grad = jnp.concatenate([jnp.zeros_like(grad), grad], axis=0)
    lse = lse_ref[0]

    def one(block, acc):
        slot = block_slot(block, z, y)
        kv = kv_ref[slot]
        scores = dot(kv, query, 1, 0)
        key = block * ROWS + lax.broadcasted_iota(jnp.int32, (ROWS, 1), 0)
        probs = jnp.where((key >= start) & (key <= rows), jnp.exp(scores - lse), 0.0)
        grad_probs = dot(kv, grad, 1, 0)
        grad_scores = (probs * (grad_probs - rowdot)).astype(jnp.bfloat16)
        gkv_ref[slot] += dot(grad_scores, query, 1, 1) + dot(
            probs.astype(jnp.bfloat16), grad, 1, 1
        )
        return acc + dot(kvt_ref[slot, :HEAD_SIZE], grad_scores, 1, 0)

    acc = lax.fori_loop(
        info[2 + slot_now], last + 1, one, jnp.zeros((HEAD_SIZE, WIDE), jnp.float32)
    )
    acc = acc * HEAD_SIZE**-0.5
    acc = jnp.concatenate([acc[:, h * ROWS : (h + 1) * ROWS] for h in range(HEADS)], axis=0)
    gq_ref[...] = rope(acc, cos_ref[...], -sin_ref[...]).astype(jnp.bfloat16)

    if last_call:

        @pl.when(step == count - 1)
        def _():
            for t, ref in enumerate(g_refs):
                for s in range(RING):
                    ref[s * ROWS : (s + 1) * ROWS, :] = gkv_ref[t * RING + s].astype(jnp.bfloat16)


def input_back_kernel(
    info, gq_ref, k0, k1, k2, k3, w_ref, x0, x1, x2, x3, cos_ref, sin_ref, n_ref, gain_two_ref,
    scale_ref, h0, h1, h2, h3, p0, p1, p2, p3, keep_ref, send_ref, row_ref, gkv_ref,
):
    for out, ref in zip((p0, p1, p2, p3), (h0, h1, h2, h3)):
        out[ROWS:] = ref[...]
    y, x, core = info[1], info[6], info[7]
    total = sum(ref[...].astype(jnp.float32) for ref in (k0, k1, k2, k3)).T
    key = rope(total[:HEAD_SIZE], cos_ref[...], -sin_ref[...])
    gkv_ref[...] = jnp.concatenate([key, total[HEAD_SIZE:]], axis=0).astype(jnp.bfloat16)
    row_ref[:, : 4 * ROWS] = gq_ref[...].T
    row_ref[:, 4 * ROWS :] = gkv_ref[...].T
    gains = []
    for xc in range(CHUNKS):
        columns = slice(xc * CHUNK, (xc + 1) * CHUNK)
        product = dot(row_ref[...], w_ref[:, columns], 1, 0)
        gain = jnp.zeros((1, CHUNK), jnp.float32)
        for s, (ref, inputs) in enumerate(zip((p0, p1, p2, p3), (x0, x1, x2, x3))):
            piece = product[s * ROWS : (s + 1) * ROWS]
            ref[:ROWS, columns] = piece.astype(jnp.bfloat16)
            scale = scale_ref[s * ROWS : (s + 1) * ROWS, :1]
            unit = inputs[:, columns].astype(jnp.float32) * scale
            gain += jnp.sum(piece * unit, axis=0, keepdims=True)
        gains.append(gain)
    gains_two = [gain_two_ref[:, xc * CHUNK : (xc + 1) * CHUNK] for xc in range(CHUNKS)]
    gains = sum(
        dot(jnp.concatenate(rows, axis=0).astype(jnp.bfloat16), gain_spread(which, True), 1, 0)
        for which, rows in enumerate((gains, gains_two))
    )
    kv_all = dot(gkv_ref[...], n_ref[...], 1, 0)
    for xc in range(CHUNKS):
        kv = kv_all[:, xc * CHUNK : (xc + 1) * CHUNK].T
        for home in range(RING):
            halves = [
                jnp.concatenate(
                    [
                        kv[z * 64 + home * 16 : z * 64 + home * 16 + 16]
                        for z in (2 * side, 2 * side + 1)
                    ],
                    axis=0,
                )
                for side in range(2)
            ]
            piece = jnp.broadcast_to(gains[xc : xc + 1, home * 128 : (home + 1) * 128], (16, 128))
            piece = jnp.concatenate(
                [jnp.concatenate(halves, axis=1), jnp.concatenate([piece, piece], axis=1)], axis=0
            ).astype(jnp.bfloat16)
            slots = turned(x, xc // 2), turned(y, home)

            @pl.when(core == xc % 2)
            def _(slots=slots, piece=piece):
                keep_ref[slots[0], slots[1]] = piece

            @pl.when(core != xc % 2)
            def _(slots=slots, piece=piece):
                send_ref[slots[0], slots[1]] = piece


def grad_output_query_kernel(info, o_ref, gq_ref, d0, d1, d2, d3, n_ref, keep_ref, send_ref):
    y, core = info[1], info[7]
    for c, out in ((core, keep_ref), (1 - core, send_ref)):
        columns = place_of(c, CHUNK)
        rows = jnp.concatenate([ref[:, columns] for ref in (d0, d1, d2, d3)], axis=0)
        grad_output = dot(o_ref[...], rows, 1, 0).astype(jnp.bfloat16)
        grad_query = dot(gq_ref[...], n_ref[:, columns], 1, 0).astype(jnp.bfloat16)
        for home in range(RING):
            slot = turned(y, home)
            out[0, slot, :ROWS] = part(grad_output, home, ROWS)
            out[0, slot, ROWS:] = part(grad_query, home, ROWS)


def feed_kernel(
    info, n0, n1, d0, d1, w_hbm, keep_ref, send_ref, h_ref, p0, p1,
    gu_ref, down_ref, n_ref, d_ref, hg_ref, row_ref, slot_ref, sems, slot_sems,
):
    units = gu_ref.shape[2]
    half = units // 2
    first = info[7] == 0

    def fetch(xc, y):
        columns = pl.ds(xc * CHUNK, CHUNK)
        return (
            pltpu.make_async_copy(
                w_hbm.at[xc, y, pl.ds(0, 2)], gu_ref.at[y, :, :, columns], sems.at[0, y, xc]
            ),
            pltpu.make_async_copy(w_hbm.at[xc, y, 2], down_ref.at[y, :, columns], sems.at[1, y, xc]),
        )

    slots = [
        pltpu.make_async_copy(ref, slot_ref.at[i], slot_sems.at[i])
        for i, ref in enumerate((n0, n1, d0, d1))
    ]
    for copy in slots:
        copy.start()
    for xc in range(CHUNKS):
        for copy in fetch(xc, 0):
            copy.start()
    for i, copy in enumerate(slots):
        copy.wait()
        out = (n_ref, d_ref)[i // 2]
        out[:, i % 2 * ROWS : (i % 2 + 1) * ROWS] = slot_ref[i].T
    for xc in range(CHUNKS):
        for copy in fetch(xc, 1):
            copy.start()

    def one(y, _):
        @pl.when(y < RING - 2)
        def _():
            for xc in range(CHUNKS):
                for copy in fetch(xc, y + 2):
                    copy.start()

        for xc in range(CHUNKS):
            for copy in fetch(xc, y):
                copy.wait()
        gate_up = dot(gu_ref[y].reshape(2 * units, MODEL_WIDTH), n_ref[...], 1, 0)
        grad_hidden = dot(down_ref[y], d_ref[...], 1, 0)
        gate, upper = gate_up[:units], gate_up[units:]
        sig = 1.0 / (1.0 + jnp.exp(-gate))
        silu = gate * sig
        grad_gate = grad_hidden * upper * (sig + silu * (1.0 - sig))
        grad_up = grad_hidden * silu
        hidden = silu * upper
        hg_ref[y, 0] = grad_gate.astype(jnp.bfloat16)
        hg_ref[y, 1] = grad_up.astype(jnp.bfloat16)
        h_ref[y] = hidden.astype(jnp.bfloat16)
        for k, value in enumerate((grad_gate, grad_up, hidden)):
            low, high = value[:half], value[half:]
            keep_ref[y, k] = jnp.where(first, low, high).astype(jnp.bfloat16)
            send_ref[y, k] = jnp.where(first, high, low).astype(jnp.bfloat16)
        return 0

    lax.fori_loop(0, RING, one, 0)
    row_ref[...] = hg_ref[...].reshape(RING * 2 * units, 2 * ROWS).T

    def back(i, _):
        columns = place_of(i, 2 * CHUNK)
        weights = gu_ref[:, :, :, columns].reshape(RING * 2 * units, 2 * CHUNK)
        total = dot(row_ref[...], weights, 1, 0).astype(jnp.bfloat16)
        p0[:, columns], p1[:, columns] = total[:ROWS], total[ROWS:]
        return 0

    lax.fori_loop(0, CHUNKS // 2, back, 0)


def half_rows(refs):
    return jnp.concatenate([refs[s][...] for s in HALVES], axis=0)


def feed_grad_kernel(
    keep0, keep1, other0, other1, n0, n1, n2, n3, m0, m1, m2, m3, d0, d1, d2, d3, d_other, g_hbm, gu_ref, down_ref, g_ref, sems
):
    units = keep0.shape[2]
    step = pl.program_id(0)

    @pl.when(step == 0)
    def _():
        for index, ref in enumerate((keep0, keep1, other0, other1)):
            columns = slice(index * 2 * ROWS, (index + 1) * 2 * ROWS)
            gu_ref[:, columns] = ref[:, :2].reshape(RING * 2 * units, 2 * ROWS)
            down_ref[:, columns] = ref[:, 2].reshape(RING * units, 2 * ROWS)

    rows = jnp.concatenate([half_rows((n0, n1, n2, n3)), half_rows((m0, m1, m2, m3))], axis=0)
    grad = dot(gu_ref[...], rows, 1, 0).astype(jnp.bfloat16)
    g_ref[step, :, :2] = grad.reshape(RING, 2, units, 2 * CHUNK)
    rows = jnp.concatenate([half_rows((d0, d1, d2, d3)), d_other[...]], axis=0)
    grad = dot(down_ref[...], rows, 1, 0).astype(jnp.bfloat16)
    g_ref[step, :, 2] = grad.reshape(RING, units, 2 * CHUNK)
    pltpu.make_async_copy(g_ref.at[step], g_hbm.at[step], sems.at[step]).start()

    @pl.when(step == RING - 1)
    def _():
        for x in range(RING):
            pltpu.make_async_copy(g_ref.at[x], g_hbm.at[x], sems.at[x]).wait()


def feed_down_kernel(h0_ref, h1_ref, w_hbm, p0, p1, p2, p3, row_ref, w_ref, sems):
    units = h0_ref.shape[1]
    copies = [
        [
            pltpu.make_async_copy(
                w_hbm.at[xc, y, 2],
                w_ref.at[xc // 2, pl.ds(y * units, units), pl.ds(xc % 2 * CHUNK, CHUNK)],
                sems.at[xc, y],
            )
            for xc in (2 * step, 2 * step + 1)
            for y in range(RING)
        ]
        for step in range(CHUNKS // 2)
    ]
    for group in copies:
        for copy in group:
            copy.start()
    for half, ref in enumerate((h0_ref, h1_ref)):
        row_ref[half * 2 * ROWS : (half + 1) * 2 * ROWS] = (
            ref[...].reshape(RING * units, 2 * ROWS).T
        )
    for step, group in enumerate(copies):
        for copy in group:
            copy.wait()
        total = dot(row_ref[...], w_ref[step], 1, 0).astype(jnp.bfloat16)
        for index, ref in enumerate((p1, p3, p0, p2)):
            ref[:, step * 2 * CHUNK : (step + 1) * 2 * CHUNK] = part(total, index, ROWS)


def residual_back_kernel(g0, g1, g2, g3, h_ref, dy_ref, gain_ref, dh_ref, dh_low_ref, gg_ref):
    grad = sum(ref[...].astype(jnp.float32) for ref in (g0, g1, g2, g3))
    scale = rms_scale(h_ref[...])
    unit = h_ref[...] * scale

    @pl.when(pl.program_id(0) == 0)
    def _():
        gg_ref[...] = jnp.zeros_like(gg_ref)

    gg_ref[...] += jnp.sum(grad * unit, axis=0, keepdims=True)
    out = dy_ref[...].astype(jnp.float32) + norm_back(unit, scale, gain_ref[...], grad)
    dh_ref[...] = out
    dh_low_ref[...] = out.astype(jnp.bfloat16)


def whole(shape):
    return pl.BlockSpec(shape, lambda *_: (0,) * len(shape))


def struct(shape, dtype=jnp.bfloat16):
    return jax.ShapeDtypeStruct(shape, dtype)


def cost(flops, moved, exps=0):
    return pl.CostEstimate(flops=flops, bytes_accessed=moved, transcendentals=exps)


def params(mebibytes):
    return pltpu.CompilerParams(vmem_limit_bytes=mebibytes << 20)


SLOT = (ROWS, MODEL_WIDTH)
SPLIT = ((1, 3), (0, 2))
SPLIT_BACK = ((0, 1, 3), (2,))


def columns_of(slots, rows):
    return pl.BlockSpec((rows, ROWS), lambda s, info: (0, slot_of(slots, s)))


def row_of(slots, width):
    return pl.BlockSpec((1, 1, width), lambda s, info: (slot_of(slots, s), 0, 0))


def hbm(value):
    return pltpu.with_memory_space_constraint(value, pltpu.HBM)


def project_qkv(info, x_slots, pack, k_slots, k_other, cosine, sine):
    return pl.pallas_call(
        qkv_kernel,
        grid_spec=pltpu.PrefetchScalarGridSpec(
            num_scalar_prefetch=1,
            grid=(1,),
            in_specs=[whole(SLOT)] * 4
            + [pl.BlockSpec(memory_space=pltpu.HBM)]
            + [whole((RING, 48, CHUNK))] * 4
            + [whole((RING, RING, 48, CHUNK))]
            + [whole((32, TOKENS))] * 2,
            out_specs=[
                whole((TOKENS, MODEL_WIDTH)),
                whole((512, TOKENS)),
                whole((TOKENS, 128)),
                whole((640, MODEL_WIDTH)),
                whole((2, MODEL_WIDTH)),
                whole((TOKENS, 128)),
            ],
            scratch_shapes=[
                pltpu.VMEM((CHUNKS, CHUNK, 128), jnp.bfloat16),
                pltpu.VMEM((CHUNKS, RING, 16, 128), jnp.float32),
                pltpu.SemaphoreType.DMA((CHUNKS, RING)),
            ],
        ),
        out_shape=[
            struct((TOKENS, MODEL_WIDTH)),
            struct((512, TOKENS)),
            struct((TOKENS, 128)),
            struct((640, MODEL_WIDTH)),
            struct((2, MODEL_WIDTH), jnp.float32),
            struct((TOKENS, 128), jnp.float32),
        ],
        compiler_params=params(32),
        cost_estimate=cost(2 * 640 * TOKENS * MODEL_WIDTH, 9 << 20),
        name="project_qkv",
    )(info, *map(hbm, x_slots), hbm(pack), *k_slots, k_other, cosine, sine)


def attend(slots, info, q_t, kv, starts, pack=None, shared=()):
    count = len(slots)
    walls = [whole((512, MODEL_WIDTH)), whole((BLOCKS, 128, ROWS))]
    shapes = [struct((512, MODEL_WIDTH)), struct((BLOCKS, 128, ROWS))]
    return pl.pallas_call(
        functools.partial(attend_kernel, slots),
        grid_spec=pltpu.PrefetchScalarGridSpec(
            num_scalar_prefetch=1,
            grid=(count,),
            in_specs=[columns_of(slots, 512), whole((BLOCKS, ROWS, 128)), row_of(slots, ROWS)]
            + (walls if shared else [pl.BlockSpec(memory_space=pltpu.HBM)]),
            out_specs=[
                pl.BlockSpec((512, ROWS), lambda s, info: (0, s)),
                pl.BlockSpec((1, 1, WIDE), lambda s, info: (s, 0, 0)),
            ]
            + [whole(SLOT)] * count
            + ([] if shared else walls),
            scratch_shapes=[] if shared else [pltpu.SemaphoreType.DMA((CHUNKS, RING))],
        ),
        out_shape=[struct((512, count * ROWS)), struct((count, 1, WIDE), jnp.float32)]
        + [struct(SLOT)] * count
        + ([] if shared else shapes),
        compiler_params=params(16),
        cost_estimate=cost(
            count * HEADS * TOKENS * 640 * 128 + count * 512 * ROWS * 2 * MODEL_WIDTH,
            6 << 20,
            count * HEADS * ROWS * 640,
        ),
        name="attend",
    )(info, q_t, kv, starts, *(shared or [hbm(pack)]))


def attend_back(
    slots, info, q_t, dh_slots, wall, o_t, lse, kv, kv_t, starts, cosine, sine, before=None
):
    count = len(slots)
    sums = (BLOCKS, ROWS, 128)
    out_specs = [pl.BlockSpec((512, ROWS), lambda s, info: (0, s))]
    out_shape = [struct((512, count * ROWS))]
    scratch_shapes = []
    if before is None:
        out_specs += [whole(sums)]
        out_shape += [struct(sums, jnp.float32)]
    else:
        out_specs += [whole((TOKENS, 128))] * 4
        out_shape += [struct((TOKENS, 128))] * 4
        scratch_shapes += [pltpu.VMEM(sums, jnp.float32)]
    return pl.pallas_call(
        functools.partial(attend_back_kernel, slots),
        grid_spec=pltpu.PrefetchScalarGridSpec(
            num_scalar_prefetch=1,
            grid=(count,),
            in_specs=[columns_of(slots, 512)]
            + [whole(SLOT)] * count
            + [
                whole((512, MODEL_WIDTH)),
                columns_of(slots, 512),
                row_of(slots, WIDE),
                whole((BLOCKS, ROWS, 128)),
                whole((BLOCKS, 128, ROWS)),
                row_of(slots, ROWS),
                columns_of(slots, HEAD_SIZE // 2),
                columns_of(slots, HEAD_SIZE // 2),
            ]
            + ([] if before is None else [whole(sums)]),
            out_specs=out_specs,
            scratch_shapes=scratch_shapes + [pltpu.VMEM((count, *SLOT), jnp.bfloat16)],
        ),
        out_shape=out_shape,
        compiler_params=params(18),
        cost_estimate=cost(
            3 * count * HEADS * ROWS * 640 * 128 * 4 + count * 512 * ROWS * 2 * MODEL_WIDTH,
            8 << 20,
            count * HEADS * ROWS * 640,
        ),
        name="attend_back",
    )(
        info, q_t, *dh_slots, wall, o_t, lse, kv, kv_t, starts, cosine, sine,
        *([] if before is None else [before]),
    )


def input_back(info, gq_t, gkv_slots, w_qkv, x_slots, cosine, sine, normed, gain_two, scales, down):
    pieces = (RING, RING, 48, CHUNK)
    return pl.pallas_call(
        input_back_kernel,
        grid_spec=pltpu.PrefetchScalarGridSpec(
            num_scalar_prefetch=1,
            grid=(1,),
            in_specs=[whole((512, TOKENS))]
            + [whole((TOKENS, 128))] * 4
            + [whole((640, MODEL_WIDTH))]
            + [whole(SLOT)] * 4
            + [whole((32, TOKENS))] * 2
            + [whole((TOKENS, MODEL_WIDTH)), whole((1, MODEL_WIDTH)), whole((TOKENS, 128))]
            + [whole(SLOT)] * 4,
            out_specs=[whole((2 * ROWS, MODEL_WIDTH))] * 4 + [whole(pieces)] * 2,
            scratch_shapes=[
                pltpu.VMEM((TOKENS, 640), jnp.bfloat16),
                pltpu.VMEM((128, TOKENS), jnp.bfloat16),
            ],
        ),
        out_shape=[pltpu.HBM((2 * ROWS, MODEL_WIDTH), jnp.bfloat16)] * 4 + [struct(pieces)] * 2,
        compiler_params=params(32),
        cost_estimate=cost(2 * 768 * TOKENS * MODEL_WIDTH, 15 << 20),
        name="input_back",
    )(
        info, gq_t, *gkv_slots, w_qkv, *map(hbm, x_slots), cosine, sine, normed, gain_two, scales, *down,
    )


def pack_specs(rows):
    spec = pl.BlockSpec((1, RING, rows, CHUNK), lambda s, info: (s, 0, 0, 0))
    return [spec, spec], [struct((RING, RING, rows, CHUNK))] * 2


def pair_columns(rows):
    return pl.BlockSpec((rows, 2 * CHUNK), lambda s, info: (0, (info[6] + RING - s) % RING))


def grad_output_query(info, o_t, gq_t, dh_slots, normed):
    out_specs, out_shape = pack_specs(2 * ROWS)
    return pl.pallas_call(
        grad_output_query_kernel,
        grid_spec=pltpu.PrefetchScalarGridSpec(
            num_scalar_prefetch=1,
            grid=(RING,),
            in_specs=[whole((512, TOKENS))] * 2
            + [pair_columns(ROWS)] * 4
            + [pair_columns(TOKENS)],
            out_specs=out_specs,
        ),
        out_shape=out_shape,
        compiler_params=params(14),
        cost_estimate=cost(4 * 512 * TOKENS * MODEL_WIDTH, 9 << 20),
        name="grad_output_query",
    )(info, o_t, gq_t, *dh_slots, normed)


def feed(info, n_pair, d_pair, weights):
    units = weights.shape[3]
    pair = (2 * ROWS, MODEL_WIDTH)
    split = (RING, 3, units // 2, 2 * ROWS)
    return pl.pallas_call(
        feed_kernel,
        in_specs=[pl.BlockSpec(memory_space=pltpu.SMEM)]
        + [pl.BlockSpec(memory_space=pl.ANY)] * 4
        + [pl.BlockSpec(memory_space=pltpu.HBM)],
        out_specs=[pl.BlockSpec(memory_space=pltpu.VMEM)] * 5,
        out_shape=[struct(split)] * 2 + [struct((RING, units, 2 * ROWS))] + [struct(SLOT)] * 2,
        scratch_shapes=[
            pltpu.VMEM((RING, 2, units, MODEL_WIDTH), jnp.bfloat16),
            pltpu.VMEM((RING, units, MODEL_WIDTH), jnp.bfloat16),
            pltpu.VMEM(pair[::-1], jnp.bfloat16),
            pltpu.VMEM(pair[::-1], jnp.bfloat16),
            pltpu.VMEM((RING, 2, units, 2 * ROWS), jnp.bfloat16),
            pltpu.VMEM((2 * ROWS, RING * 2 * units), jnp.bfloat16),
            pltpu.VMEM((4, *SLOT), jnp.bfloat16),
            pltpu.SemaphoreType.DMA((2, RING, CHUNKS)),
            pltpu.SemaphoreType.DMA((4,)),
        ],
        compiler_params=params(30),
        cost_estimate=cost(5 * RING * units * TOKENS * MODEL_WIDTH, 23 << 20, RING * units * TOKENS // 2),
        name="feed",
    )(info, *map(hbm, n_pair), *map(hbm, d_pair), hbm(weights))


def feed_grad(keeps, others, n_slots, n_other, d_slots, d_other):
    units = keeps[0].shape[2]
    slots = [pl.BlockSpec((ROWS, 2 * CHUNK), lambda i: (0, i))] * 4
    joined = [pl.BlockSpec((TOKENS, 2 * CHUNK), lambda i: (0, i))]
    out = (RING, RING, 3, units, 2 * CHUNK)
    return pl.pallas_call(
        feed_grad_kernel,
        grid=(RING,),
        in_specs=[whole(keeps[0].shape)] * 4 + slots * 3 + joined,
        out_specs=pl.BlockSpec(memory_space=pltpu.HBM),
        out_shape=pltpu.HBM(out, jnp.bfloat16),
        scratch_shapes=[
            pltpu.VMEM((RING * 2 * units, 2 * TOKENS), jnp.bfloat16),
            pltpu.VMEM((RING * units, 2 * TOKENS), jnp.bfloat16),
            pltpu.VMEM(out, jnp.bfloat16),
            pltpu.SemaphoreType.DMA((RING,)),
        ],
        compiler_params=params(30),
        cost_estimate=cost(12 * RING * units * TOKENS * MODEL_WIDTH, 22 << 20),
        name="feed_grad",
    )(*keeps, *others, *map(hbm, n_slots), *n_other, *map(hbm, d_slots), hbm(d_other))


def last_kernel(*refs):
    (gn_refs, down_refs), refs = (refs[:RING], refs[RING : 2 * RING]), refs[2 * RING :]
    h_ref, dh_ref, x_ref, gain_ref, result_ref, grad_ref = refs
    down = sum(ref[...].astype(jnp.float32) for ref in down_refs)
    result_ref[...] = (h_ref[...] + down).astype(jnp.bfloat16)
    grad = sum(ref[...].astype(jnp.float32) for ref in gn_refs)
    value = x_ref[...].astype(jnp.float32)
    scale = rms_scale(value)
    out = dh_ref[...] + norm_back(value * scale, scale, gain_ref[...], grad)
    grad_ref[...] = out.astype(jnp.bfloat16)


def last(parts, h1, dh1, inputs, gain):
    half = ROWS // 2
    rows = pl.BlockSpec((half, MODEL_WIDTH), lambda i: (i, 0))
    lower = pl.BlockSpec((half, MODEL_WIDTH), lambda i: (i + 2, 0))
    vector = pl.BlockSpec((1, MODEL_WIDTH), lambda i: (0, 0))
    return pl.pallas_call(
        last_kernel,
        grid=(2,),
        in_specs=[rows] * 4 + [lower] * 4 + [rows] * 3 + [vector],
        out_specs=[rows] * 2,
        out_shape=[struct(SLOT)] * 2,
        compiler_params=params(16),
        cost_estimate=cost(30 * ROWS * MODEL_WIDTH, 8 << 20),
        name="last",
    )(*map(hbm, parts), *map(hbm, parts), hbm(h1), hbm(dh1), hbm(inputs), gain)


def residual_back(grads, h1, out_grad, gain):
    rows = pl.BlockSpec((ROWS // 2, MODEL_WIDTH), lambda i: (i, 0))
    vector = pl.BlockSpec((1, MODEL_WIDTH), lambda i: (0, 0))
    return pl.pallas_call(
        residual_back_kernel,
        grid=(2,),
        in_specs=[rows] * 6 + [vector],
        out_specs=[rows, rows, vector],
        out_shape=[struct(SLOT, jnp.float32), struct(SLOT), struct((1, MODEL_WIDTH), jnp.float32)],
        compiler_params=params(16),
        cost_estimate=cost(30 * ROWS * MODEL_WIDTH, 5 << 20),
        name="residual_back",
    )(*map(hbm, grads), hbm(h1), hbm(out_grad), gain)


def feed_down(hs, weights):
    units = hs[0].shape[1]
    return pl.pallas_call(
        feed_down_kernel,
        in_specs=[pl.BlockSpec(memory_space=pltpu.VMEM)] * 2 + [pl.BlockSpec(memory_space=pltpu.HBM)],
        out_specs=[pl.BlockSpec(memory_space=pltpu.VMEM)] * 4,
        out_shape=[struct(SLOT)] * 4,
        scratch_shapes=[
            pltpu.VMEM((TOKENS, RING * units), jnp.bfloat16),
            pltpu.VMEM((CHUNKS // 2, RING * units, 2 * CHUNK), jnp.bfloat16),
            pltpu.SemaphoreType.DMA((CHUNKS, RING)),
        ],
        compiler_params=params(18),
        cost_estimate=cost(2 * RING * units * TOKENS * MODEL_WIDTH, 9 << 20),
        name="feed_down",
    )(*hs, hbm(weights))


def adamw(weight, first, second, grad, rate, decay):
    first_new = BETA_ONE * first + (1.0 - BETA_ONE) * grad
    second_new = BETA_TWO * second + (1.0 - BETA_TWO) * grad * grad
    fix_one = 1.0 - BETA_ONE**STEP
    fix_two = 1.0 - BETA_TWO**STEP
    update = first_new / fix_one / (jnp.sqrt(second_new / fix_two) + ADAM_EPS)
    return (weight - rate * (update + decay * weight), first_new, second_new)


def adam_feed_kernel(info, own_ref, other_ref, *refs):
    step, core = pl.program_id(0), info[7]
    own = jnp.where(core == 0, own_ref[:, :, :CHUNK], own_ref[:, :, CHUNK:])
    grad = jnp.where(step == core, own, other_ref[...]).astype(jnp.float32)
    for k, (g, rate) in enumerate(((grad[:2], MODEL_WIDTH**-0.5), (grad[2], FF**-0.5))):
        ins, outs = refs[3 * k : 3 * k + 3], refs[6 + 3 * k : 9 + 3 * k]
        values = adamw(*(ref[...] for ref in ins), g, rate, DECAY)
        for ref, value in zip(outs, values):
            ref[...] = value


def adam_feed(info, own, other, gateup, down):
    units = down[0].shape[0]
    half = units // 2
    specs = [pl.BlockSpec((2, half, CHUNK), lambda i, info: (0, i, 0))] * 3
    specs += [pl.BlockSpec((half, CHUNK), lambda i, info: (i, 0))] * 3
    arrays = [*gateup, *down]
    return pl.pallas_call(
        adam_feed_kernel,
        grid_spec=pltpu.PrefetchScalarGridSpec(
            num_scalar_prefetch=1,
            grid=(2,),
            in_specs=[whole(own.shape), whole(other.shape)] + specs,
            out_specs=specs,
        ),
        out_shape=[struct(a.shape, jnp.float32) for a in arrays],
        compiler_params=params(16),
        cost_estimate=cost(30 * 3 * units * CHUNK, 24 * 3 * units * CHUNK),
        name="adam_feed",
    )(info, hbm(own), other, *map(hbm, arrays))


def adam_attention_kernel(*refs):
    parts, refs = refs[:RING], refs[RING:]
    total = sum(ref[: 2 * ROWS].astype(jnp.float32) for ref in parts)
    grads = total[ROWS:].T, total[:ROWS]
    for k, (g, rate) in enumerate(zip(grads, (MODEL_WIDTH**-0.5, (MODEL_WIDTH // 64) ** -0.5))):
        ins, outs = refs[3 * k : 3 * k + 3], refs[6 + 3 * k : 9 + 3 * k]
        values = adamw(*(ref[...] for ref in ins), g, rate, DECAY)
        for ref, value in zip(outs, values):
            ref[...] = value


def adam_attention(parts, query, output):
    arrays = [*query, *output]
    specs = [whole(a.shape) for a in arrays]
    return pl.pallas_call(
        adam_attention_kernel,
        grid=(1,),
        in_specs=[whole(p.shape) for p in parts] + specs,
        out_specs=specs,
        out_shape=[struct(a.shape, jnp.float32) for a in arrays],
        compiler_params=params(16),
        cost_estimate=cost(60 * ROWS * CHUNK, 50 * ROWS * CHUNK),
        name="adam_attention",
    )(*parts, *map(hbm, arrays))


def swap_cores(value):
    return lax.ppermute(value, "core", [(0, 1), (1, 0)])


def scatter_core(keep, other):
    return [
        (keep[s].astype(jnp.float32) + other[s].astype(jnp.float32)).astype(jnp.bfloat16)
        for s in range(RING)
    ]


def sum_x(parts):
    return [
        sum(p[s].astype(jnp.float32) for p in parts).astype(jnp.bfloat16) for s in range(RING)
    ]


def after(values, *others):
    return lax.optimization_barrier((list(values), others))[0]


def local(
    block_input,
    out_grad,
    segments,
    w_query,
    keyvalue_weights,
    w_output,
    w_gateup,
    w_down,
    norm_gains,
    query_first,
    keyval_moment_one,
    output_first,
    gateup_first,
    down_first,
    gains_first,
    query_second,
    keyval_moment_two,
    output_second,
    gateup_second,
    down_second,
    gains_second,
):
    bf16, f32 = jnp.bfloat16, jnp.float32
    x, core, z, y = (lax.axis_index(name) for name in ("x", "core", "z", "y"))
    units = w_down.shape[0]

    kv_rows = keyvalue_weights.astype(bf16).reshape(2, 16, RING, HEAD_SIZE).transpose(2, 1, 0, 3)
    message = jnp.concatenate(
        [
            kv_rows.reshape(RING, 16, 128),
            jnp.broadcast_to(
                jnp.pad(norm_gains.astype(bf16).reshape(1, 1, 32), ((0, 0), (0, 15), (0, 96))),
                (RING, 16, 128),
            ),
        ],
        1,
    )
    small = absolute(scatter_ring_from(relative(message, z), "z"), z)
    kv_piece = jnp.concatenate(
        [small[:2, :16].reshape(32, 128), small[2:, :16].reshape(32, 128)], 1
    )
    gain_piece = jnp.pad(small[:, 16, :32].reshape(1, 128), ((0, 15), (0, 128)))
    kv_piece = jnp.concatenate([kv_piece, gain_piece], 0)

    pack = jnp.concatenate([w_output.astype(bf16), w_query.astype(bf16).T], 0)
    pack = lax.all_gather(pack, SHARE, axis=0, tiled=False)
    x_slots = gather_far_last(block_input, "z")
    (kv_piece,) = after([jnp.stack(gather_ring(kv_piece, "x"))], x_slots[1], x_slots[3])
    k_slots = gather_ring(kv_piece, "y")
    k_other = swap_cores(jnp.stack(after(k_slots, x_slots[2])))
    d_slots = gather_far_last(after([out_grad], *x_slots[1:])[0], "z")
    feed_shard = jnp.concatenate(
        [w_gateup.astype(bf16).transpose(0, 2, 1), w_down.astype(bf16)[None]], 0
    )
    (feed_shard,) = after([feed_shard], pack, d_slots[1], d_slots[3], k_other)
    w_feed = lax.all_gather(feed_shard, SHARE, axis=0, tiled=False)
    w_feed = w_feed.reshape(CHUNKS, RING, 3, units, CHUNK)

    starts = doc_starts(segments[0])
    by_block = lax.dynamic_index_in_dim(starts.reshape(RING, RING, ROWS), y, 1, keepdims=False)
    row_starts = jnp.stack(relative(by_block, z))
    places = (z + RING - jnp.arange(RING, dtype=jnp.int32)) % RING
    begins = places * (RING * ROWS) + y * ROWS
    positions = (begins[:, None] + jnp.arange(ROWS, dtype=jnp.int32) - row_starts).reshape(-1)
    half = HEAD_SIZE // 2
    freqs = 10000.0 ** (-jnp.arange(half, dtype=f32) * 2.0 / HEAD_SIZE)
    angles = freqs[:, None] * positions.astype(f32)[None, :]
    cosine, sine = jnp.cos(angles), jnp.sin(angles)
    info = jnp.concatenate(
        [
            jnp.stack([z, y]).astype(jnp.int32),
            row_starts[:, 0] // ROWS,
            jnp.stack([x, core]).astype(jnp.int32),
        ]
    )
    row_starts = row_starts[:, None, :]

    normed, q_t, kv_own, w_qkv, gains, scales = project_qkv(
        info, x_slots, pack, k_slots, k_other, cosine, sine
    )
    kv = jnp.stack(gather_ring(kv_own, "y")).reshape(BLOCKS, ROWS, 2 * HEAD_SIZE)
    d_all = jnp.concatenate([d_slots[s] for s in HALVES], 0)
    q_t, d_all = after([q_t, d_all])
    d_other = swap_cores(d_all)
    near_o, near_lse, o_1, o_3, *shared = attend(SPLIT[0], info, q_t, kv, row_starts, pack)
    wo, kv_t = shared
    (q_late,) = after([q_t], o_1, d_slots[2])
    far_o, far_lse, o_0, o_2 = attend(SPLIT[1], info, q_late, kv, row_starts, shared=shared)
    o_t = jnp.concatenate(
        [far_o[:, :ROWS], near_o[:, :ROWS], far_o[:, ROWS:], near_o[:, ROWS:]], 1
    )
    lse = jnp.stack([far_lse[0], near_lse[0], far_lse[1], near_lse[1]])
    o_1, o_3 = after([o_1, o_3], d_slots[2])
    o_slots = scatter_far_last(o_0, o_1, o_3, o_2, "z")
    o_sum = sum(p.astype(f32) for p in o_slots)
    h1 = block_input.astype(f32) + o_sum

    scale_two = rms_scale(h1)
    unit_two = h1 * scale_two
    (normed_two,) = after([(unit_two * gains[1]).astype(bf16)], d_other)
    n_slots = gather_far_last(normed_two, "z")
    keep0, send0, h0, gn2_1, gn2_3 = feed(
        info, [n_slots[s] for s in HALVES[:2]], [d_slots[s] for s in HALVES[:2]], w_feed
    )
    n_other = [swap_cores(value) for value in n_slots]
    keep1, send1, h1_half, gn2_0, gn2_2 = feed(
        info, after([n_slots[s] for s in HALVES[2:]], keep0), [d_slots[s] for s in HALVES[2:]], w_feed
    )
    gn2_slots = scatter_ring([gn2_0, gn2_1, gn2_2, gn2_3], "z")
    other0 = swap_cores(send0)
    (send1,) = after([send1], *n_other, other0, gn2_slots[1], gn2_slots[3])
    others = other0, swap_cores(send1)
    grad_feed = feed_grad((keep0, keep1), others, n_slots, n_other, d_slots, d_other)
    *gn2_slots, grad_feed = after([*gn2_slots, grad_feed])
    dh1, dh1_low, grad_gain_two = residual_back(gn2_slots, h1, out_grad, gains[1:])
    own_feed = lax.psum_scatter(
        grad_feed.reshape(16, 3, units // 2, 2 * CHUNK), ("x", "y"), scatter_dimension=0, tiled=False
    )

    down_slots = feed_down(after([h0, h1_half], *gn2_slots), w_feed)
    dh_slots = gather_far_last(dh1_low, "z", *down_slots)
    near, far = SPLIT_BACK
    arguments = wo, o_t, lse, kv, kv_t, row_starts, cosine, sine
    gq_near, sums = attend_back(near, info, q_t, [dh_slots[s] for s in near], *arguments)
    (dh_far,) = after([dh_slots[2]], sums)
    gq_far, *gkv_slots = attend_back(far, info, q_t, [dh_far], *arguments, before=sums)
    gq_t = jnp.concatenate([gq_near[:, : 2 * ROWS], gq_far, gq_near[:, 2 * ROWS :]], 1)
    gkv_slots = scatter_ring(gkv_slots, "y")
    (gq_late,) = after([gq_t], gkv_slots[1], gkv_slots[3])
    keep, send = grad_output_query(info, o_t, gq_late, dh_slots, normed)
    (send,) = after([send], gkv_slots[2])
    gkv_slots = after(gkv_slots, send)
    *gn1_slots, keep_kv, send_kv = input_back(
        info, gq_t, gkv_slots, w_qkv, x_slots, cosine, sine, normed, grad_gain_two, scales, down_slots
    )
    gn1_0, gn1_1, gn1_2, gn1_3 = gn1_slots
    gn1_slots = scatter_far_last(gn1_0, gn1_1, gn1_3, gn1_2, "z")
    parts = zip(scatter_core(keep, swap_cores(send)), scatter_core(keep_kv, swap_cores(send_kv)))
    parts = scatter_ring([jnp.concatenate(p, 1) for p in parts], "x")

    parts_y = scatter_ring(sum_x(parts), "y")

    parts_y = after(parts_y, gn1_slots[2])
    own_pack = sum(p[2 * ROWS :].astype(f32) for p in parts_y)

    kv_piece = own_pack[:32]
    kv_piece = jnp.concatenate([kv_piece[:, :128], kv_piece[:, 128:]], 0).reshape(RING, 16, 128)
    gain_piece = own_pack[32, :128].reshape(RING, 1, 32)
    message = jnp.concatenate([kv_piece, jnp.pad(gain_piece, ((0, 0), (0, 15), (0, 96)))], 1)
    small = scatter_ring_from(relative(message, z), "z")

    result, grad_input = last(after(gn1_slots, *parts_y[1:]), h1, dh1, block_input, gains[:1])
    (own_feed,) = after([own_feed], small[1], grad_input)
    other_send = jnp.where(core == 0, own_feed[..., CHUNK:], own_feed[..., :CHUNK])
    other = swap_cores(other_send)
    attention = adam_attention(
        after(parts_y, other_send),
        (w_query, query_first, query_second),
        (w_output, output_first, output_second),
    )
    q, o = attention[:3], attention[3:]
    turn = (0, 2, 1)
    feed_arrays = adam_feed(
        info,
        own_feed,
        other,
        [a.transpose(turn) for a in (w_gateup, gateup_first, gateup_second)],
        (w_down, down_first, down_second),
    )
    gu = [a.transpose(turn) for a in feed_arrays[:3]]
    down = feed_arrays[3:]
    small[2:] = after(small[2:], *feed_arrays)
    small = absolute(small, z)
    own_kv = small[:, :16].reshape(RING, 16, 2, HEAD_SIZE).transpose(2, 1, 0, 3)
    own_kv = own_kv.reshape(2, 16, RING * HEAD_SIZE)
    own_gains = jnp.sum(small[:, 16, :32], 0).reshape(2, 16)

    rate = MODEL_WIDTH ** (-0.5)
    kvs = adamw(keyvalue_weights, keyval_moment_one, keyval_moment_two, own_kv, rate, DECAY)
    gain = adamw(norm_gains, gains_first, gains_second, own_gains, GAIN_RATE, 0.0)
    updates = (q, kvs, o, gu, down, gain)
    return (result, grad_input, *(u[i] for i in range(3) for u in updates))


def scatter_ring_from(slots, axis):
    own, after, far, before = scatter_ring(slots, axis)
    return [own, before, far, after]


def solution(mesh):
    view = Mesh(mesh.devices.reshape(4, 2, 4, 4), ("x", "core", "z", "y"))
    dp, tensor = ("x", "core"), ("z", "y")
    both = dp + tensor
    tokens = P(both, None)
    weights = (
        P(dp, tensor),
        P(None, both, None),
        P(tensor, dp),
        P(None, dp, tensor),
        P(tensor, dp),
        P(None, both),
    )
    return jax.shard_map(
        local,
        mesh=view,
        in_specs=(tokens, tokens, P(dp, None), *weights * 3),
        out_specs=(tokens, tokens, *weights * 3),
        check_vma=False,
    )
```

```python
import functools

import jax
import jax.numpy as jnp
from jax import lax
from jax.experimental import pallas as pl
from jax.experimental.pallas import tpu as pltpu
from jax.sharding import Mesh
from jax.sharding import PartitionSpec as P

MODEL_WIDTH = 2048
QUERY_HEADS = 32
KEYVALUE_HEADS = 4
HEAD_SIZE = 64
FF = 5632
STEP = 10

BETA_ONE = 0.9
BETA_TWO = 0.95
ADAM_EPS = 1e-08
DECAY = 0.1
GAIN_RATE = 0.8
NORM_EPS = 1e-05

RING = 4
SHARE = ("x", "core", "y")
ROWS = 128
TOKENS = RING * ROWS
HEADS = QUERY_HEADS // RING
WIDE = HEADS * ROWS
BLOCKS = 16
MASKED = -1e30
HALVES = (1, 3, 0, 2)
CHUNKS, CHUNK = 8, 256
PACK = 2 * ROWS + 48


def doc_starts(segment):
    index = jnp.arange(segment.shape[0], dtype=jnp.int32)
    starts = jnp.concatenate([jnp.ones((1,), dtype=bool), segment[1:] != segment[:-1]])
    return lax.cummax(jnp.where(starts, index, 0))


def shift(value, axis, step):
    return lax.ppermute(value, axis, [(i, (i + step) % RING) for i in range(RING)])


def gather_ring(value, axis):
    far = shift(value, axis, 2)
    return [value, shift(value, axis, 1), far, shift(value, axis, 3)]


def gather_far_last(value, axis, *others):
    near = shift(value, axis, 1), shift(value, axis, 3)
    (value_late,) = after([value], *near, *others)
    return [value, near[0], shift(value_late, axis, 2), near[1]]


def scatter_far_last(own, part_one, part_three, part_two, axis):
    near = shift(part_one, axis, 3), shift(part_three, axis, 1)
    (part_two,) = after([part_two], *near)
    return [own, near[0], shift(part_two, axis, 2), near[1]]


def scatter_ring(parts, axis):
    far = shift(parts[2], axis, 2)
    return [parts[0], shift(parts[1], axis, 3), far, shift(parts[3], axis, 1)]


def absolute(slots, own):
    turned = jnp.stack([slots[0], slots[3], slots[2], slots[1]])
    return lax.dynamic_slice_in_dim(jnp.concatenate([turned, turned]), RING - own, RING, 0)


def relative(stacked, own):
    turned = jnp.concatenate([stacked, stacked])
    return [
        lax.dynamic_index_in_dim(turned, own + RING - s if s else own, 0, keepdims=False)
        for s in range(RING)
    ]


def dot(left, right, left_dim, right_dim):
    return lax.dot_general(
        left, right, (((left_dim,), (right_dim,)), ((), ())), preferred_element_type=jnp.float32
    )


def rms_scale(values):
    return lax.rsqrt(jnp.mean(values * values, axis=-1, keepdims=True) + NORM_EPS)


def norm_back(unit, scale, gain, grad):
    scaled = grad * gain
    return scale * (scaled - unit * jnp.mean(scaled * unit, axis=-1, keepdims=True))


def part(ref, index, size):
    return ref[index * size : (index + 1) * size, :]


def heads_side_by_side(value):
    return jnp.concatenate([part(value, h, HEAD_SIZE) for h in range(HEADS)], axis=1)


def mask_parts(info, starts, step):
    z, y = info[0], info[1]
    place = (z + RING - step) % RING
    begin = place * (RING * ROWS) + y * ROWS
    row = begin + lax.broadcasted_iota(jnp.int32, (1, ROWS), 1)
    rows = jnp.concatenate([row] * HEADS, axis=1)
    start = jnp.concatenate([starts] * HEADS, axis=1)
    return z, y, place * RING + y, rows, start


def block_slot(block, z, y):
    return ((y + RING - block % RING) % RING) * RING + (z + RING - block // RING) % RING


def rope(values, cosine, sine):
    half = HEAD_SIZE // 2
    out = []
    for h in range(values.shape[0] // HEAD_SIZE):
        first = values[h * HEAD_SIZE : h * HEAD_SIZE + half]
        second = values[h * HEAD_SIZE + half : (h + 1) * HEAD_SIZE]
        out += [first * cosine - second * sine, first * sine + second * cosine]
    return jnp.concatenate(out, axis=0)


def turned(place, step):
    return (place + RING - step) % RING


def weight_slots(info, own_refs, other_ref):
    y, x, core = info[1], info[6], info[7]
    for cs in range(2):
        for ys in range(RING):
            for xs in range(RING):
                ref = other_ref.at[ys, xs] if cs else own_refs[ys].at[xs]
                yield turned(x, xs) * 2 + (1 - core if cs else core), turned(y, ys), ref


def place_of(index, size):
    return pl.ds(pl.multiple_of(index * size, size), size)


def gain_spread(which, transposed):
    shape = (CHUNK, 512) if transposed else (512, CHUNK)
    lane = lax.broadcasted_iota(jnp.int32, shape, 1 if transposed else 0)
    column = lax.broadcasted_iota(jnp.int32, shape, 0 if transposed else 1)
    y, z, gain, row = lane // 128, lane // 32 % 4, lane // 16 % 2, lane % 16
    same = (column // 64 == z) & (column // 16 % 4 == y) & (column % 16 == row) & (gain == which)
    return jnp.where(same, 1.0, 0.0).astype(jnp.bfloat16)


def fetch_pack(pack_hbm, which, out_ref, sems):
    return [
        pltpu.make_async_copy(
            pack_hbm.at[xc * RING + y, pl.ds(which * ROWS, ROWS)],
            out_ref.at[pl.ds(y * ROWS, ROWS), pl.ds(xc * CHUNK, CHUNK)],
            sems.at[xc, y],
        )
        for xc in range(CHUNKS)
        for y in range(RING)
    ]


def qkv_kernel(
    info, x0, x1, x2, x3, pack_hbm, k0, k1, k2, k3, k_other, cos_ref, sin_ref,
    n_ref, q_ref, kv_ref, w_ref, gain_ref, scale_ref, wkv_ref, piece_ref, sems,
):
    copies = fetch_pack(pack_hbm, 1, w_ref, sems)
    for copy in copies:
        copy.start()
    for chunk, y, ref in weight_slots(info, (k0, k1, k2, k3), k_other):
        for z in range(RING):
            wkv_ref[chunk, pl.ds(pl.multiple_of(z * 64 + y * 16, 16), 16), :] = ref[
                (z % 2) * 16 : (z % 2 + 1) * 16, (z // 2) * 128 : (z // 2 + 1) * 128
            ]
        piece_ref[chunk, y] = ref[32:48, :128].astype(jnp.float32)
    pieces = [
        jnp.concatenate([piece_ref[xc, y, :1] for y in range(RING)], axis=1) for xc in range(CHUNKS)
    ]
    pieces = jnp.concatenate(pieces, axis=0).astype(jnp.bfloat16)
    gains = [dot(pieces, gain_spread(which, False), 1, 0) for which in range(2)]
    for xc in range(CHUNKS):
        columns = slice(xc * CHUNK, (xc + 1) * CHUNK)
        w_ref[4 * ROWS : 5 * ROWS, columns] = wkv_ref[xc].T
        for which in range(2):
            gain_ref[which : which + 1, columns] = gains[which][xc : xc + 1]
    for s, ref in enumerate((x0, x1, x2, x3)):
        value = ref[...].astype(jnp.float32)
        scale = rms_scale(value)
        scale_ref[s * ROWS : (s + 1) * ROWS] = jnp.broadcast_to(scale, (ROWS, 128))
        n_ref[s * ROWS : (s + 1) * ROWS, :] = (value * scale * gain_ref[:1]).astype(jnp.bfloat16)
    for copy in copies:
        copy.wait()
    qkv = dot(w_ref[...], n_ref[...], 1, 1)
    query = rope(qkv[: 4 * ROWS], cos_ref[...], sin_ref[...]).astype(jnp.bfloat16)
    q_ref[...] = query * jnp.bfloat16(HEAD_SIZE**-0.5)
    key = rope(qkv[4 * ROWS : 4 * ROWS + HEAD_SIZE], cos_ref[...], sin_ref[...])
    key_value = jnp.concatenate([key, qkv[4 * ROWS + HEAD_SIZE :]], axis=0)
    kv_ref[...] = key_value.T.astype(jnp.bfloat16)


def slot_of(slots, step):
    out = slots[0]
    for index in range(1, len(slots)):
        out = out + (slots[index] - slots[index - 1]) * ((step + len(slots) - index) // len(slots))
    return out


def attend_kernel(
    slots, info, q_ref, kv_ref, start_ref, *refs
):
    step = pl.program_id(0)
    first_call = 2 not in slots
    if first_call:
        pack_hbm, o_ref, lse_ref, *outs, wall_ref, kvt_ref, sems = refs
        copies = fetch_pack(pack_hbm, 0, wall_ref, sems)

        @pl.when(step == 0)
        def _():
            for copy in copies:
                copy.start()
            for b in range(BLOCKS):
                kvt_ref[b] = kv_ref[b].T
    else:
        wall_ref, kvt_ref, o_ref, lse_ref, *outs = refs

    slot_now = slot_of(slots, step)
    z, y, last, rows, start = mask_parts(info, start_ref[0], slot_now)
    query = heads_side_by_side(q_ref[...])
    query = jnp.concatenate([query, jnp.zeros_like(query)], axis=0)

    def one(block, carry):
        top, total, acc = carry
        slot = block_slot(block, z, y)
        scores = dot(kv_ref[slot], query, 1, 0)
        key = block * ROWS + lax.broadcasted_iota(jnp.int32, (ROWS, 1), 0)
        scores = jnp.where((key >= start) & (key <= rows), scores, MASKED)
        new_top = jnp.maximum(top, jnp.max(scores, axis=0, keepdims=True))
        weights = jnp.exp(scores - new_top)
        fade = jnp.exp(top - new_top)
        total = total * fade + jnp.sum(weights, axis=0, keepdims=True)
        acc = acc * fade + dot(kvt_ref[slot, HEAD_SIZE:], weights.astype(jnp.bfloat16), 1, 0)
        return new_top, total, acc

    top, total, acc = lax.fori_loop(
        info[2 + slot_now],
        last + 1,
        one,
        (
            jnp.full((1, WIDE), MASKED, jnp.float32),
            jnp.zeros((1, WIDE), jnp.float32),
            jnp.zeros((HEAD_SIZE, WIDE), jnp.float32),
        ),
    )
    out = acc / total
    out = jnp.concatenate([out[:, h * ROWS : (h + 1) * ROWS] for h in range(HEADS)], axis=0)
    o_ref[...] = out.astype(jnp.bfloat16)
    lse_ref[0] = top + jnp.log(total)
    if first_call:

        @pl.when(step == 0)
        def _():
            for copy in copies:
                copy.wait()

    product = dot(out.T.astype(jnp.bfloat16), wall_ref[...], 1, 0).astype(jnp.bfloat16)
    for s, ref in enumerate(outs):

        @pl.when(step == s)
        def _(ref=ref):
            ref[...] = product


def attend_back_kernel(slots, info, q_ref, *refs):
    count = len(slots)
    d_refs, refs = refs[:count], refs[count:]
    wall_ref, o_ref, lse_ref, kv_ref, kvt_ref, start_ref, cos_ref, sin_ref, *refs = refs
    last_call = slots[-1] == 2
    if last_call:
        before_ref, gq_ref, *g_refs, gkv_ref, dh_ref = refs
    else:
        gq_ref, gkv_ref, dh_ref = refs
    step = pl.program_id(0)

    @pl.when(step == 0)
    def _():
        if last_call:
            gkv_ref[...] = before_ref[...]
        else:
            gkv_ref[...] = jnp.zeros_like(gkv_ref)
        for s, ref in enumerate(d_refs):
            dh_ref[s] = ref[...]

    slot_now = slot_of(slots, step)
    z, y, last, rows, start = mask_parts(info, start_ref[0], slot_now)
    query = heads_side_by_side(q_ref[...])
    grad = dot(wall_ref[...], dh_ref[step], 1, 1).astype(jnp.bfloat16)
    grad = heads_side_by_side(grad)
    out = heads_side_by_side(o_ref[...])
    rowdot = jnp.sum(grad.astype(jnp.float32) * out.astype(jnp.float32), axis=0, keepdims=True)
    query = jnp.concatenate([query, jnp.zeros_like(query)], axis=0)
    grad = jnp.concatenate([jnp.zeros_like(grad), grad], axis=0)
    lse = lse_ref[0]

    def one(block, acc):
        slot = block_slot(block, z, y)
        kv = kv_ref[slot]
        scores = dot(kv, query, 1, 0)
        key = block * ROWS + lax.broadcasted_iota(jnp.int32, (ROWS, 1), 0)
        probs = jnp.where((key >= start) & (key <= rows), jnp.exp(scores - lse), 0.0)
        grad_probs = dot(kv, grad, 1, 0)
        grad_scores = (probs * (grad_probs - rowdot)).astype(jnp.bfloat16)
        gkv_ref[slot] += dot(grad_scores, query, 1, 1) + dot(
            probs.astype(jnp.bfloat16), grad, 1, 1
        )
        return acc + dot(kvt_ref[slot, :HEAD_SIZE], grad_scores, 1, 0)

    acc = lax.fori_loop(
        info[2 + slot_now], last + 1, one, jnp.zeros((HEAD_SIZE, WIDE), jnp.float32)
    )
    acc = acc * HEAD_SIZE**-0.5
    acc = jnp.concatenate([acc[:, h * ROWS : (h + 1) * ROWS] for h in range(HEADS)], axis=0)
    gq_ref[...] = rope(acc, cos_ref[...], -sin_ref[...]).astype(jnp.bfloat16)

    if last_call:

        @pl.when(step == count - 1)
        def _():
            for t, ref in enumerate(g_refs):
                for s in range(RING):
                    ref[s * ROWS : (s + 1) * ROWS, :] = gkv_ref[t * RING + s].astype(jnp.bfloat16)


def input_back_kernel(
    info, gq_ref, k0, k1, k2, k3, w_ref, x0, x1, x2, x3, cos_ref, sin_ref, n_ref, gain_two_ref,
    scale_ref, h0, h1, h2, h3, p0, p1, p2, p3, keep_ref, send_ref, row_ref, gkv_ref,
):
    for out, ref in zip((p0, p1, p2, p3), (h0, h1, h2, h3)):
        out[ROWS:] = ref[...]
    y, x, core = info[1], info[6], info[7]
    total = sum(ref[...].astype(jnp.float32) for ref in (k0, k1, k2, k3)).T
    key = rope(total[:HEAD_SIZE], cos_ref[...], -sin_ref[...])
    gkv_ref[...] = jnp.concatenate([key, total[HEAD_SIZE:]], axis=0).astype(jnp.bfloat16)
    row_ref[:, : 4 * ROWS] = gq_ref[...].T
    row_ref[:, 4 * ROWS :] = gkv_ref[...].T
    gains = []
    for xc in range(CHUNKS):
        columns = slice(xc * CHUNK, (xc + 1) * CHUNK)
        product = dot(row_ref[...], w_ref[:, columns], 1, 0)
        gain = jnp.zeros((1, CHUNK), jnp.float32)
        for s, (ref, inputs) in enumerate(zip((p0, p1, p2, p3), (x0, x1, x2, x3))):
            piece = product[s * ROWS : (s + 1) * ROWS]
            ref[:ROWS, columns] = piece.astype(jnp.bfloat16)
            scale = scale_ref[s * ROWS : (s + 1) * ROWS, :1]
            unit = inputs[:, columns].astype(jnp.float32) * scale
            gain += jnp.sum(piece * unit, axis=0, keepdims=True)
        gains.append(gain)
    gains_two = [gain_two_ref[:, xc * CHUNK : (xc + 1) * CHUNK] for xc in range(CHUNKS)]
    gains = sum(
        dot(jnp.concatenate(rows, axis=0).astype(jnp.bfloat16), gain_spread(which, True), 1, 0)
        for which, rows in enumerate((gains, gains_two))
    )
    kv_all = dot(gkv_ref[...], n_ref[...], 1, 0)
    for xc in range(CHUNKS):
        kv = kv_all[:, xc * CHUNK : (xc + 1) * CHUNK].T
        for home in range(RING):
            halves = [
                jnp.concatenate(
                    [
                        kv[z * 64 + home * 16 : z * 64 + home * 16 + 16]
                        for z in (2 * side, 2 * side + 1)
                    ],
                    axis=0,
                )
                for side in range(2)
            ]
            piece = jnp.broadcast_to(gains[xc : xc + 1, home * 128 : (home + 1) * 128], (16, 128))
            piece = jnp.concatenate(
                [jnp.concatenate(halves, axis=1), jnp.concatenate([piece, piece], axis=1)], axis=0
            ).astype(jnp.bfloat16)
            slots = turned(x, xc // 2), turned(y, home)

            @pl.when(core == xc % 2)
            def _(slots=slots, piece=piece):
                keep_ref[slots[0], slots[1]] = piece

            @pl.when(core != xc % 2)
            def _(slots=slots, piece=piece):
                send_ref[slots[0], slots[1]] = piece


def grad_output_query_kernel(info, o_ref, gq_ref, d0, d1, d2, d3, n_ref, keep_ref, send_ref):
    y, core = info[1], info[7]
    for c, out in ((core, keep_ref), (1 - core, send_ref)):
        columns = place_of(c, CHUNK)
        rows = jnp.concatenate([ref[:, columns] for ref in (d0, d1, d2, d3)], axis=0)
        grad_output = dot(o_ref[...], rows, 1, 0).astype(jnp.bfloat16)
        grad_query = dot(gq_ref[...], n_ref[:, columns], 1, 0).astype(jnp.bfloat16)
        for home in range(RING):
            slot = turned(y, home)
            out[0, slot, :ROWS] = part(grad_output, home, ROWS)
            out[0, slot, ROWS:] = part(grad_query, home, ROWS)


def feed_kernel(
    info, n0, n1, d0, d1, w_hbm, keep_ref, send_ref, h_ref, p0, p1,
    gu_ref, down_ref, n_ref, d_ref, hg_ref, row_ref, slot_ref, sems, slot_sems,
):
    units = gu_ref.shape[2]
    half = units // 2
    first = info[7] == 0

    def fetch(xc, y):
        columns = pl.ds(xc * CHUNK, CHUNK)
        return (
            pltpu.make_async_copy(
                w_hbm.at[xc, y, pl.ds(0, 2)], gu_ref.at[y, :, :, columns], sems.at[0, y, xc]
            ),
            pltpu.make_async_copy(w_hbm.at[xc, y, 2], down_ref.at[y, :, columns], sems.at[1, y, xc]),
        )

    slots = [
        pltpu.make_async_copy(ref, slot_ref.at[i], slot_sems.at[i])
        for i, ref in enumerate((n0, n1, d0, d1))
    ]
    for copy in slots:
        copy.start()
    for xc in range(CHUNKS):
        for copy in fetch(xc, 0):
            copy.start()
    for i, copy in enumerate(slots):
        copy.wait()
        out = (n_ref, d_ref)[i // 2]
        out[:, i % 2 * ROWS : (i % 2 + 1) * ROWS] = slot_ref[i].T
    for xc in range(CHUNKS):
        for copy in fetch(xc, 1):
            copy.start()

    def one(y, _):
        @pl.when(y < RING - 2)
        def _():
            for xc in range(CHUNKS):
                for copy in fetch(xc, y + 2):
                    copy.start()

        for xc in range(CHUNKS):
            for copy in fetch(xc, y):
                copy.wait()
        gate_up = dot(gu_ref[y].reshape(2 * units, MODEL_WIDTH), n_ref[...], 1, 0)
        grad_hidden = dot(down_ref[y], d_ref[...], 1, 0)
        gate, upper = gate_up[:units], gate_up[units:]
        sig = 1.0 / (1.0 + jnp.exp(-gate))
        silu = gate * sig
        grad_gate = grad_hidden * upper * (sig + silu * (1.0 - sig))
        grad_up = grad_hidden * silu
        hidden = silu * upper
        hg_ref[y, 0] = grad_gate.astype(jnp.bfloat16)
        hg_ref[y, 1] = grad_up.astype(jnp.bfloat16)
        h_ref[y] = hidden.astype(jnp.bfloat16)
        for k, value in enumerate((grad_gate, grad_up, hidden)):
            low, high = value[:half], value[half:]
            keep_ref[y, k] = jnp.where(first, low, high).astype(jnp.bfloat16)
            send_ref[y, k] = jnp.where(first, high, low).astype(jnp.bfloat16)
        return 0

    lax.fori_loop(0, RING, one, 0)
    row_ref[...] = hg_ref[...].reshape(RING * 2 * units, 2 * ROWS).T

    def back(i, _):
        columns = place_of(i, 2 * CHUNK)
        weights = gu_ref[:, :, :, columns].reshape(RING * 2 * units, 2 * CHUNK)
        total = dot(row_ref[...], weights, 1, 0).astype(jnp.bfloat16)
        p0[:, columns], p1[:, columns] = total[:ROWS], total[ROWS:]
        return 0

    lax.fori_loop(0, CHUNKS // 2, back, 0)


def half_rows(refs):
    return jnp.concatenate([refs[s][...] for s in HALVES], axis=0)


def feed_grad_kernel(
    keep0, keep1, other0, other1, n0, n1, n2, n3, m0, m1, m2, m3, d0, d1, d2, d3, d_other, g_hbm, gu_ref, down_ref, g_ref, sems
):
    units = keep0.shape[2]
    step = pl.program_id(0)

    @pl.when(step == 0)
    def _():
        for index, ref in enumerate((keep0, keep1, other0, other1)):
            columns = slice(index * 2 * ROWS, (index + 1) * 2 * ROWS)
            gu_ref[:, columns] = ref[:, :2].reshape(RING * 2 * units, 2 * ROWS)
            down_ref[:, columns] = ref[:, 2].reshape(RING * units, 2 * ROWS)

    rows = jnp.concatenate([half_rows((n0, n1, n2, n3)), half_rows((m0, m1, m2, m3))], axis=0)
    grad = dot(gu_ref[...], rows, 1, 0).astype(jnp.bfloat16)
    g_ref[step, :, :2] = grad.reshape(RING, 2, units, 2 * CHUNK)
    rows = jnp.concatenate([half_rows((d0, d1, d2, d3)), d_other[...]], axis=0)
    grad = dot(down_ref[...], rows, 1, 0).astype(jnp.bfloat16)
    g_ref[step, :, 2] = grad.reshape(RING, units, 2 * CHUNK)
    pltpu.make_async_copy(g_ref.at[step], g_hbm.at[step], sems.at[step]).start()

    @pl.when(step == RING - 1)
    def _():
        for x in range(RING):
            pltpu.make_async_copy(g_ref.at[x], g_hbm.at[x], sems.at[x]).wait()


def feed_down_kernel(h0_ref, h1_ref, w_hbm, p0, p1, p2, p3, row_ref, w_ref, sems):
    units = h0_ref.shape[1]
    copies = [
        [
            pltpu.make_async_copy(
                w_hbm.at[xc, y, 2],
                w_ref.at[xc // 2, pl.ds(y * units, units), pl.ds(xc % 2 * CHUNK, CHUNK)],
                sems.at[xc, y],
            )
            for xc in (2 * step, 2 * step + 1)
            for y in range(RING)
        ]
        for step in range(CHUNKS // 2)
    ]
    for group in copies:
        for copy in group:
            copy.start()
    for half, ref in enumerate((h0_ref, h1_ref)):
        row_ref[half * 2 * ROWS : (half + 1) * 2 * ROWS] = (
            ref[...].reshape(RING * units, 2 * ROWS).T
        )
    for step, group in enumerate(copies):
        for copy in group:
            copy.wait()
        total = dot(row_ref[...], w_ref[step], 1, 0).astype(jnp.bfloat16)
        for index, ref in enumerate((p1, p3, p0, p2)):
            ref[:, step * 2 * CHUNK : (step + 1) * 2 * CHUNK] = part(total, index, ROWS)


def residual_back_kernel(g0, g1, g2, g3, h_ref, dy_ref, gain_ref, dh_ref, dh_low_ref, gg_ref):
    grad = sum(ref[...].astype(jnp.float32) for ref in (g0, g1, g2, g3))
    scale = rms_scale(h_ref[...])
    unit = h_ref[...] * scale

    @pl.when(pl.program_id(0) == 0)
    def _():
        gg_ref[...] = jnp.zeros_like(gg_ref)

    gg_ref[...] += jnp.sum(grad * unit, axis=0, keepdims=True)
    out = dy_ref[...].astype(jnp.float32) + norm_back(unit, scale, gain_ref[...], grad)
    dh_ref[...] = out
    dh_low_ref[...] = out.astype(jnp.bfloat16)


def whole(shape):
    return pl.BlockSpec(shape, lambda *_: (0,) * len(shape))


def struct(shape, dtype=jnp.bfloat16):
    return jax.ShapeDtypeStruct(shape, dtype)


def cost(flops, moved, exps=0):
    return pl.CostEstimate(flops=flops, bytes_accessed=moved, transcendentals=exps)


def params(mebibytes):
    return pltpu.CompilerParams(vmem_limit_bytes=mebibytes << 20)


SLOT = (ROWS, MODEL_WIDTH)
SPLIT = ((1, 3), (0, 2))
SPLIT_BACK = ((0, 1, 3), (2,))


def columns_of(slots, rows):
    return pl.BlockSpec((rows, ROWS), lambda s, info: (0, slot_of(slots, s)))


def row_of(slots, width):
    return pl.BlockSpec((1, 1, width), lambda s, info: (slot_of(slots, s), 0, 0))


def hbm(value):
    return pltpu.with_memory_space_constraint(value, pltpu.HBM)


def project_qkv(info, x_slots, pack, k_slots, k_other, cosine, sine):
    return pl.pallas_call(
        qkv_kernel,
        grid_spec=pltpu.PrefetchScalarGridSpec(
            num_scalar_prefetch=1,
            grid=(1,),
            in_specs=[whole(SLOT)] * 4
            + [pl.BlockSpec(memory_space=pltpu.HBM)]
            + [whole((RING, 48, CHUNK))] * 4
            + [whole((RING, RING, 48, CHUNK))]
            + [whole((32, TOKENS))] * 2,
            out_specs=[
                whole((TOKENS, MODEL_WIDTH)),
                whole((512, TOKENS)),
                whole((TOKENS, 128)),
                whole((640, MODEL_WIDTH)),
                whole((2, MODEL_WIDTH)),
                whole((TOKENS, 128)),
            ],
            scratch_shapes=[
                pltpu.VMEM((CHUNKS, CHUNK, 128), jnp.bfloat16),
                pltpu.VMEM((CHUNKS, RING, 16, 128), jnp.float32),
                pltpu.SemaphoreType.DMA((CHUNKS, RING)),
            ],
        ),
        out_shape=[
            struct((TOKENS, MODEL_WIDTH)),
            struct((512, TOKENS)),
            struct((TOKENS, 128)),
            struct((640, MODEL_WIDTH)),
            struct((2, MODEL_WIDTH), jnp.float32),
            struct((TOKENS, 128), jnp.float32),
        ],
        compiler_params=params(32),
        cost_estimate=cost(2 * 640 * TOKENS * MODEL_WIDTH, 9 << 20),
        name="project_qkv",
    )(info, *map(hbm, x_slots), hbm(pack), *k_slots, k_other, cosine, sine)


def attend(slots, info, q_t, kv, starts, pack=None, shared=()):
    count = len(slots)
    walls = [whole((512, MODEL_WIDTH)), whole((BLOCKS, 128, ROWS))]
    shapes = [struct((512, MODEL_WIDTH)), struct((BLOCKS, 128, ROWS))]
    return pl.pallas_call(
        functools.partial(attend_kernel, slots),
        grid_spec=pltpu.PrefetchScalarGridSpec(
            num_scalar_prefetch=1,
            grid=(count,),
            in_specs=[columns_of(slots, 512), whole((BLOCKS, ROWS, 128)), row_of(slots, ROWS)]
            + (walls if shared else [pl.BlockSpec(memory_space=pltpu.HBM)]),
            out_specs=[
                pl.BlockSpec((512, ROWS), lambda s, info: (0, s)),
                pl.BlockSpec((1, 1, WIDE), lambda s, info: (s, 0, 0)),
            ]
            + [whole(SLOT)] * count
            + ([] if shared else walls),
            scratch_shapes=[] if shared else [pltpu.SemaphoreType.DMA((CHUNKS, RING))],
        ),
        out_shape=[struct((512, count * ROWS)), struct((count, 1, WIDE), jnp.float32)]
        + [struct(SLOT)] * count
        + ([] if shared else shapes),
        compiler_params=params(16),
        cost_estimate=cost(
            count * HEADS * TOKENS * 640 * 128 + count * 512 * ROWS * 2 * MODEL_WIDTH,
            6 << 20,
            count * HEADS * ROWS * 640,
        ),
        name="attend",
    )(info, q_t, kv, starts, *(shared or [hbm(pack)]))


def attend_back(
    slots, info, q_t, dh_slots, wall, o_t, lse, kv, kv_t, starts, cosine, sine, before=None
):
    count = len(slots)
    sums = (BLOCKS, ROWS, 128)
    out_specs = [pl.BlockSpec((512, ROWS), lambda s, info: (0, s))]
    out_shape = [struct((512, count * ROWS))]
    scratch_shapes = []
    if before is None:
        out_specs += [whole(sums)]
        out_shape += [struct(sums, jnp.float32)]
    else:
        out_specs += [whole((TOKENS, 128))] * 4
        out_shape += [struct((TOKENS, 128))] * 4
        scratch_shapes += [pltpu.VMEM(sums, jnp.float32)]
    return pl.pallas_call(
        functools.partial(attend_back_kernel, slots),
        grid_spec=pltpu.PrefetchScalarGridSpec(
            num_scalar_prefetch=1,
            grid=(count,),
            in_specs=[columns_of(slots, 512)]
            + [whole(SLOT)] * count
            + [
                whole((512, MODEL_WIDTH)),
                columns_of(slots, 512),
                row_of(slots, WIDE),
                whole((BLOCKS, ROWS, 128)),
                whole((BLOCKS, 128, ROWS)),
                row_of(slots, ROWS),
                columns_of(slots, HEAD_SIZE // 2),
                columns_of(slots, HEAD_SIZE // 2),
            ]
            + ([] if before is None else [whole(sums)]),
            out_specs=out_specs,
            scratch_shapes=scratch_shapes + [pltpu.VMEM((count, *SLOT), jnp.bfloat16)],
        ),
        out_shape=out_shape,
        compiler_params=params(18),
        cost_estimate=cost(
            3 * count * HEADS * ROWS * 640 * 128 * 4 + count * 512 * ROWS * 2 * MODEL_WIDTH,
            8 << 20,
            count * HEADS * ROWS * 640,
        ),
        name="attend_back",
    )(
        info, q_t, *dh_slots, wall, o_t, lse, kv, kv_t, starts, cosine, sine,
        *([] if before is None else [before]),
    )


def input_back(info, gq_t, gkv_slots, w_qkv, x_slots, cosine, sine, normed, gain_two, scales, down):
    pieces = (RING, RING, 48, CHUNK)
    return pl.pallas_call(
        input_back_kernel,
        grid_spec=pltpu.PrefetchScalarGridSpec(
            num_scalar_prefetch=1,
            grid=(1,),
            in_specs=[whole((512, TOKENS))]
            + [whole((TOKENS, 128))] * 4
            + [whole((640, MODEL_WIDTH))]
            + [whole(SLOT)] * 4
            + [whole((32, TOKENS))] * 2
            + [whole((TOKENS, MODEL_WIDTH)), whole((1, MODEL_WIDTH)), whole((TOKENS, 128))]
            + [whole(SLOT)] * 4,
            out_specs=[whole((2 * ROWS, MODEL_WIDTH))] * 4 + [whole(pieces)] * 2,
            scratch_shapes=[
                pltpu.VMEM((TOKENS, 640), jnp.bfloat16),
                pltpu.VMEM((128, TOKENS), jnp.bfloat16),
            ],
        ),
        out_shape=[pltpu.HBM((2 * ROWS, MODEL_WIDTH), jnp.bfloat16)] * 4 + [struct(pieces)] * 2,
        compiler_params=params(32),
        cost_estimate=cost(2 * 768 * TOKENS * MODEL_WIDTH, 15 << 20),
        name="input_back",
    )(
        info, gq_t, *gkv_slots, w_qkv, *map(hbm, x_slots), cosine, sine, normed, gain_two, scales, *down,
    )


def pack_specs(rows):
    spec = pl.BlockSpec((1, RING, rows, CHUNK), lambda s, info: (s, 0, 0, 0))
    return [spec, spec], [struct((RING, RING, rows, CHUNK))] * 2


def pair_columns(rows):
    return pl.BlockSpec((rows, 2 * CHUNK), lambda s, info: (0, (info[6] + RING - s) % RING))


def grad_output_query(info, o_t, gq_t, dh_slots, normed):
    out_specs, out_shape = pack_specs(2 * ROWS)
    return pl.pallas_call(
        grad_output_query_kernel,
        grid_spec=pltpu.PrefetchScalarGridSpec(
            num_scalar_prefetch=1,
            grid=(RING,),
            in_specs=[whole((512, TOKENS))] * 2
            + [pair_columns(ROWS)] * 4
            + [pair_columns(TOKENS)],
            out_specs=out_specs,
        ),
        out_shape=out_shape,
        compiler_params=params(14),
        cost_estimate=cost(4 * 512 * TOKENS * MODEL_WIDTH, 9 << 20),
        name="grad_output_query",
    )(info, o_t, gq_t, *dh_slots, normed)


def feed(info, n_pair, d_pair, weights):
    units = weights.shape[3]
    pair = (2 * ROWS, MODEL_WIDTH)
    split = (RING, 3, units // 2, 2 * ROWS)
    return pl.pallas_call(
        feed_kernel,
        in_specs=[pl.BlockSpec(memory_space=pltpu.SMEM)]
        + [pl.BlockSpec(memory_space=pl.ANY)] * 4
        + [pl.BlockSpec(memory_space=pltpu.HBM)],
        out_specs=[pl.BlockSpec(memory_space=pltpu.VMEM)] * 5,
        out_shape=[struct(split)] * 2 + [struct((RING, units, 2 * ROWS))] + [struct(SLOT)] * 2,
        scratch_shapes=[
            pltpu.VMEM((RING, 2, units, MODEL_WIDTH), jnp.bfloat16),
            pltpu.VMEM((RING, units, MODEL_WIDTH), jnp.bfloat16),
            pltpu.VMEM(pair[::-1], jnp.bfloat16),
            pltpu.VMEM(pair[::-1], jnp.bfloat16),
            pltpu.VMEM((RING, 2, units, 2 * ROWS), jnp.bfloat16),
            pltpu.VMEM((2 * ROWS, RING * 2 * units), jnp.bfloat16),
            pltpu.VMEM((4, *SLOT), jnp.bfloat16),
            pltpu.SemaphoreType.DMA((2, RING, CHUNKS)),
            pltpu.SemaphoreType.DMA((4,)),
        ],
        compiler_params=params(30),
        cost_estimate=cost(5 * RING * units * TOKENS * MODEL_WIDTH, 23 << 20, RING * units * TOKENS // 2),
        name="feed",
    )(info, *map(hbm, n_pair), *map(hbm, d_pair), hbm(weights))


def feed_grad(keeps, others, n_slots, n_other, d_slots, d_other):
    units = keeps[0].shape[2]
    slots = [pl.BlockSpec((ROWS, 2 * CHUNK), lambda i: (0, i))] * 4
    joined = [pl.BlockSpec((TOKENS, 2 * CHUNK), lambda i: (0, i))]
    out = (RING, RING, 3, units, 2 * CHUNK)
    return pl.pallas_call(
        feed_grad_kernel,
        grid=(RING,),
        in_specs=[whole(keeps[0].shape)] * 4 + slots * 3 + joined,
        out_specs=pl.BlockSpec(memory_space=pltpu.HBM),
        out_shape=pltpu.HBM(out, jnp.bfloat16),
        scratch_shapes=[
            pltpu.VMEM((RING * 2 * units, 2 * TOKENS), jnp.bfloat16),
            pltpu.VMEM((RING * units, 2 * TOKENS), jnp.bfloat16),
            pltpu.VMEM(out, jnp.bfloat16),
            pltpu.SemaphoreType.DMA((RING,)),
        ],
        compiler_params=params(30),
        cost_estimate=cost(12 * RING * units * TOKENS * MODEL_WIDTH, 22 << 20),
        name="feed_grad",
    )(*keeps, *others, *map(hbm, n_slots), *n_other, *map(hbm, d_slots), d_other)


def last_kernel(*refs):
    (gn_refs, down_refs), refs = (refs[:RING], refs[RING : 2 * RING]), refs[2 * RING :]
    h_ref, dh_ref, x_ref, gain_ref, result_ref, grad_ref = refs
    down = sum(ref[...].astype(jnp.float32) for ref in down_refs)
    result_ref[...] = (h_ref[...] + down).astype(jnp.bfloat16)
    grad = sum(ref[...].astype(jnp.float32) for ref in gn_refs)
    value = x_ref[...].astype(jnp.float32)
    scale = rms_scale(value)
    out = dh_ref[...] + norm_back(value * scale, scale, gain_ref[...], grad)
    grad_ref[...] = out.astype(jnp.bfloat16)


def last(parts, h1, dh1, inputs, gain):
    half = ROWS // 2
    rows = pl.BlockSpec((half, MODEL_WIDTH), lambda i: (i, 0))
    lower = pl.BlockSpec((half, MODEL_WIDTH), lambda i: (i + 2, 0))
    vector = pl.BlockSpec((1, MODEL_WIDTH), lambda i: (0, 0))
    return pl.pallas_call(
        last_kernel,
        grid=(2,),
        in_specs=[rows] * 4 + [lower] * 4 + [rows] * 3 + [vector],
        out_specs=[rows] * 2,
        out_shape=[struct(SLOT)] * 2,
        compiler_params=params(16),
        cost_estimate=cost(30 * ROWS * MODEL_WIDTH, 8 << 20),
        name="last",
    )(*map(hbm, parts), *map(hbm, parts), hbm(h1), hbm(dh1), hbm(inputs), gain)


def residual_back(grads, h1, out_grad, gain):
    rows = pl.BlockSpec((ROWS // 2, MODEL_WIDTH), lambda i: (i, 0))
    vector = pl.BlockSpec((1, MODEL_WIDTH), lambda i: (0, 0))
    return pl.pallas_call(
        residual_back_kernel,
        grid=(2,),
        in_specs=[rows] * 6 + [vector],
        out_specs=[rows, rows, vector],
        out_shape=[struct(SLOT, jnp.float32), struct(SLOT), struct((1, MODEL_WIDTH), jnp.float32)],
        compiler_params=params(16),
        cost_estimate=cost(30 * ROWS * MODEL_WIDTH, 5 << 20),
        name="residual_back",
    )(*map(hbm, grads), hbm(h1), hbm(out_grad), gain)


def feed_down(hs, weights):
    units = hs[0].shape[1]
    return pl.pallas_call(
        feed_down_kernel,
        in_specs=[pl.BlockSpec(memory_space=pltpu.VMEM)] * 2 + [pl.BlockSpec(memory_space=pltpu.HBM)],
        out_specs=[pl.BlockSpec(memory_space=pltpu.VMEM)] * 4,
        out_shape=[struct(SLOT)] * 4,
        scratch_shapes=[
            pltpu.VMEM((TOKENS, RING * units), jnp.bfloat16),
            pltpu.VMEM((CHUNKS // 2, RING * units, 2 * CHUNK), jnp.bfloat16),
            pltpu.SemaphoreType.DMA((CHUNKS, RING)),
        ],
        compiler_params=params(18),
        cost_estimate=cost(2 * RING * units * TOKENS * MODEL_WIDTH, 9 << 20),
        name="feed_down",
    )(*hs, hbm(weights))


def adamw(weight, first, second, grad, rate, decay):
    first_new = BETA_ONE * first + (1.0 - BETA_ONE) * grad
    second_new = BETA_TWO * second + (1.0 - BETA_TWO) * grad * grad
    fix_one = 1.0 - BETA_ONE**STEP
    fix_two = 1.0 - BETA_TWO**STEP
    update = first_new / fix_one / (jnp.sqrt(second_new / fix_two) + ADAM_EPS)
    return (weight - rate * (update + decay * weight), first_new, second_new)


def adam_feed_kernel(info, own_ref, other_ref, *refs):
    step, core = pl.program_id(0), info[7]
    own = jnp.where(core == 0, own_ref[:, :, :CHUNK], own_ref[:, :, CHUNK:])
    grad = jnp.where(step == core, own, other_ref[...]).astype(jnp.float32)
    for k, (g, rate) in enumerate(((grad[:2], MODEL_WIDTH**-0.5), (grad[2], FF**-0.5))):
        ins, outs = refs[3 * k : 3 * k + 3], refs[6 + 3 * k : 9 + 3 * k]
        values = adamw(*(ref[...] for ref in ins), g, rate, DECAY)
        for ref, value in zip(outs, values):
            ref[...] = value


def adam_feed(info, own, other, gateup, down):
    units = down[0].shape[0]
    half = units // 2
    specs = [pl.BlockSpec((2, half, CHUNK), lambda i, info: (0, i, 0))] * 3
    specs += [pl.BlockSpec((half, CHUNK), lambda i, info: (i, 0))] * 3
    arrays = [*gateup, *down]
    return pl.pallas_call(
        adam_feed_kernel,
        grid_spec=pltpu.PrefetchScalarGridSpec(
            num_scalar_prefetch=1,
            grid=(2,),
            in_specs=[whole(own.shape), whole(other.shape)] + specs,
            out_specs=specs,
        ),
        out_shape=[struct(a.shape, jnp.float32) for a in arrays],
        compiler_params=params(16),
        cost_estimate=cost(30 * 3 * units * CHUNK, 24 * 3 * units * CHUNK),
        name="adam_feed",
    )(info, hbm(own), other, *map(hbm, arrays))


def adam_attention_kernel(*refs):
    parts, refs = refs[:RING], refs[RING:]
    total = sum(ref[: 2 * ROWS].astype(jnp.float32) for ref in parts)
    grads = total[ROWS:].T, total[:ROWS]
    for k, (g, rate) in enumerate(zip(grads, (MODEL_WIDTH**-0.5, (MODEL_WIDTH // 64) ** -0.5))):
        ins, outs = refs[3 * k : 3 * k + 3], refs[6 + 3 * k : 9 + 3 * k]
        values = adamw(*(ref[...] for ref in ins), g, rate, DECAY)
        for ref, value in zip(outs, values):
            ref[...] = value


def adam_attention(parts, query, output):
    arrays = [*query, *output]
    specs = [whole(a.shape) for a in arrays]
    return pl.pallas_call(
        adam_attention_kernel,
        grid=(1,),
        in_specs=[whole(p.shape) for p in parts] + specs,
        out_specs=specs,
        out_shape=[struct(a.shape, jnp.float32) for a in arrays],
        compiler_params=params(16),
        cost_estimate=cost(60 * ROWS * CHUNK, 50 * ROWS * CHUNK),
        name="adam_attention",
    )(*parts, *map(hbm, arrays))


def swap_cores(value):
    return lax.ppermute(value, "core", [(0, 1), (1, 0)])


def scatter_core(keep, other):
    return [
        (keep[s].astype(jnp.float32) + other[s].astype(jnp.float32)).astype(jnp.bfloat16)
        for s in range(RING)
    ]


def sum_x(parts):
    return [
        sum(p[s].astype(jnp.float32) for p in parts).astype(jnp.bfloat16) for s in range(RING)
    ]


def after(values, *others):
    return lax.optimization_barrier((list(values), others))[0]


def local(
    block_input,
    out_grad,
    segments,
    w_query,
    keyvalue_weights,
    w_output,
    w_gateup,
    w_down,
    norm_gains,
    query_first,
    keyval_moment_one,
    output_first,
    gateup_first,
    down_first,
    gains_first,
    query_second,
    keyval_moment_two,
    output_second,
    gateup_second,
    down_second,
    gains_second,
):
    bf16, f32 = jnp.bfloat16, jnp.float32
    x, core, z, y = (lax.axis_index(name) for name in ("x", "core", "z", "y"))
    units = w_down.shape[0]

    kv_rows = keyvalue_weights.astype(bf16).reshape(2, 16, RING, HEAD_SIZE).transpose(2, 1, 0, 3)
    message = jnp.concatenate(
        [
            kv_rows.reshape(RING, 16, 128),
            jnp.broadcast_to(
                jnp.pad(norm_gains.astype(bf16).reshape(1, 1, 32), ((0, 0), (0, 15), (0, 96))),
                (RING, 16, 128),
            ),
        ],
        1,
    )
    small = absolute(scatter_ring_from(relative(message, z), "z"), z)
    kv_piece = jnp.concatenate(
        [small[:2, :16].reshape(32, 128), small[2:, :16].reshape(32, 128)], 1
    )
    gain_piece = jnp.pad(small[:, 16, :32].reshape(1, 128), ((0, 15), (0, 128)))
    kv_piece = jnp.concatenate([kv_piece, gain_piece], 0)

    pack = jnp.concatenate([w_output.astype(bf16), w_query.astype(bf16).T], 0)
    pack = lax.all_gather(pack, SHARE, axis=0, tiled=False)
    x_slots = gather_far_last(block_input, "z")
    (kv_piece,) = after([jnp.stack(gather_ring(kv_piece, "x"))], x_slots[1], x_slots[3])
    k_slots = gather_ring(kv_piece, "y")
    k_other = swap_cores(jnp.stack(after(k_slots, x_slots[2])))
    d_slots = gather_far_last(after([out_grad], *x_slots[1:])[0], "z")
    feed_shard = jnp.concatenate(
        [w_gateup.astype(bf16).transpose(0, 2, 1), w_down.astype(bf16)[None]], 0
    )
    (feed_shard,) = after([feed_shard], pack, d_slots[1], d_slots[3], k_other)
    w_feed = lax.all_gather(feed_shard, SHARE, axis=0, tiled=False)
    w_feed = w_feed.reshape(CHUNKS, RING, 3, units, CHUNK)

    starts = doc_starts(segments[0])
    by_block = lax.dynamic_index_in_dim(starts.reshape(RING, RING, ROWS), y, 1, keepdims=False)
    row_starts = jnp.stack(relative(by_block, z))
    places = (z + RING - jnp.arange(RING, dtype=jnp.int32)) % RING
    begins = places * (RING * ROWS) + y * ROWS
    positions = (begins[:, None] + jnp.arange(ROWS, dtype=jnp.int32) - row_starts).reshape(-1)
    half = HEAD_SIZE // 2
    freqs = 10000.0 ** (-jnp.arange(half, dtype=f32) * 2.0 / HEAD_SIZE)
    angles = freqs[:, None] * positions.astype(f32)[None, :]
    cosine, sine = jnp.cos(angles), jnp.sin(angles)
    info = jnp.concatenate(
        [
            jnp.stack([z, y]).astype(jnp.int32),
            row_starts[:, 0] // ROWS,
            jnp.stack([x, core]).astype(jnp.int32),
        ]
    )
    row_starts = row_starts[:, None, :]

    normed, q_t, kv_own, w_qkv, gains, scales = project_qkv(
        info, x_slots, pack, k_slots, k_other, cosine, sine
    )
    kv = jnp.stack(gather_ring(kv_own, "y")).reshape(BLOCKS, ROWS, 2 * HEAD_SIZE)
    d_all = jnp.concatenate([d_slots[s] for s in HALVES], 0)
    q_t, d_all = after([q_t, d_all])
    d_other = swap_cores(d_all)
    near_o, near_lse, o_1, o_3, *shared = attend(SPLIT[0], info, q_t, kv, row_starts, pack)
    wo, kv_t = shared
    (q_late,) = after([q_t], o_1, d_slots[2])
    far_o, far_lse, o_0, o_2 = attend(SPLIT[1], info, q_late, kv, row_starts, shared=shared)
    o_t = jnp.concatenate(
        [far_o[:, :ROWS], near_o[:, :ROWS], far_o[:, ROWS:], near_o[:, ROWS:]], 1
    )
    lse = jnp.stack([far_lse[0], near_lse[0], far_lse[1], near_lse[1]])
    o_1, o_3 = after([o_1, o_3], d_slots[2])
    o_slots = scatter_far_last(o_0, o_1, o_3, o_2, "z")
    o_sum = sum(p.astype(f32) for p in o_slots)
    h1 = block_input.astype(f32) + o_sum

    scale_two = rms_scale(h1)
    unit_two = h1 * scale_two
    (normed_two,) = after([(unit_two * gains[1]).astype(bf16)], d_other)
    n_slots = gather_far_last(normed_two, "z")
    keep0, send0, h0, gn2_1, gn2_3 = feed(
        info, [n_slots[s] for s in HALVES[:2]], [d_slots[s] for s in HALVES[:2]], w_feed
    )
    n_other = [swap_cores(value) for value in n_slots]
    keep1, send1, h1_half, gn2_0, gn2_2 = feed(
        info, after([n_slots[s] for s in HALVES[2:]], keep0), [d_slots[s] for s in HALVES[2:]], w_feed
    )
    gn2_slots = scatter_ring([gn2_0, gn2_1, gn2_2, gn2_3], "z")
    other0 = swap_cores(send0)
    (send1,) = after([send1], *n_other, other0, gn2_slots[1], gn2_slots[3])
    others = other0, swap_cores(send1)
    grad_feed = feed_grad((keep0, keep1), others, n_slots, n_other, d_slots, d_other)
    *gn2_slots, grad_feed = after([*gn2_slots, grad_feed])
    dh1, dh1_low, grad_gain_two = residual_back(gn2_slots, h1, out_grad, gains[1:])
    own_feed = lax.psum_scatter(
        grad_feed.reshape(16, 3, units // 2, 2 * CHUNK), ("x", "y"), scatter_dimension=0, tiled=False
    )

    down_slots = feed_down(after([h0, h1_half], *gn2_slots), w_feed)
    dh_slots = gather_far_last(dh1_low, "z", *down_slots)
    near, far = SPLIT_BACK
    arguments = wo, o_t, lse, kv, kv_t, row_starts, cosine, sine
    gq_near, sums = attend_back(near, info, q_t, [dh_slots[s] for s in near], *arguments)
    (dh_far,) = after([dh_slots[2]], sums)
    gq_far, *gkv_slots = attend_back(far, info, q_t, [dh_far], *arguments, before=sums)
    gq_t = jnp.concatenate([gq_near[:, : 2 * ROWS], gq_far, gq_near[:, 2 * ROWS :]], 1)
    gkv_slots = scatter_ring(gkv_slots, "y")
    (gq_late,) = after([gq_t], gkv_slots[1], gkv_slots[3])
    keep, send = grad_output_query(info, o_t, gq_late, dh_slots, normed)
    (send,) = after([send], gkv_slots[2])
    gkv_slots = after(gkv_slots, send)
    *gn1_slots, keep_kv, send_kv = input_back(
        info, gq_t, gkv_slots, w_qkv, x_slots, cosine, sine, normed, grad_gain_two, scales, down_slots
    )
    gn1_0, gn1_1, gn1_2, gn1_3 = gn1_slots
    gn1_slots = scatter_far_last(gn1_0, gn1_1, gn1_3, gn1_2, "z")
    parts = zip(scatter_core(keep, swap_cores(send)), scatter_core(keep_kv, swap_cores(send_kv)))
    parts = scatter_ring([jnp.concatenate(p, 1) for p in parts], "x")

    parts_y = scatter_ring(sum_x(parts), "y")

    parts_y = after(parts_y, gn1_slots[2])
    own_pack = sum(p[2 * ROWS :].astype(f32) for p in parts_y)

    kv_piece = own_pack[:32]
    kv_piece = jnp.concatenate([kv_piece[:, :128], kv_piece[:, 128:]], 0).reshape(RING, 16, 128)
    gain_piece = own_pack[32, :128].reshape(RING, 1, 32)
    message = jnp.concatenate([kv_piece, jnp.pad(gain_piece, ((0, 0), (0, 15), (0, 96)))], 1)
    small = scatter_ring_from(relative(message, z), "z")

    result, grad_input = last(after(gn1_slots, *parts_y[1:]), h1, dh1, block_input, gains[:1])
    (own_feed,) = after([own_feed], small[1], grad_input)
    other_send = jnp.where(core == 0, own_feed[..., CHUNK:], own_feed[..., :CHUNK])
    other = swap_cores(other_send)
    attention = adam_attention(
        after(parts_y, other_send),
        (w_query, query_first, query_second),
        (w_output, output_first, output_second),
    )
    q, o = attention[:3], attention[3:]
    turn = (0, 2, 1)
    feed_arrays = adam_feed(
        info,
        own_feed,
        other,
        [a.transpose(turn) for a in (w_gateup, gateup_first, gateup_second)],
        (w_down, down_first, down_second),
    )
    gu = [a.transpose(turn) for a in feed_arrays[:3]]
    down = feed_arrays[3:]
    small[2:] = after(small[2:], *feed_arrays)
    small = absolute(small, z)
    own_kv = small[:, :16].reshape(RING, 16, 2, HEAD_SIZE).transpose(2, 1, 0, 3)
    own_kv = own_kv.reshape(2, 16, RING * HEAD_SIZE)
    own_gains = jnp.sum(small[:, 16, :32], 0).reshape(2, 16)

    rate = MODEL_WIDTH ** (-0.5)
    kvs = adamw(keyvalue_weights, keyval_moment_one, keyval_moment_two, own_kv, rate, DECAY)
    gain = adamw(norm_gains, gains_first, gains_second, own_gains, GAIN_RATE, 0.0)
    updates = (q, kvs, o, gu, down, gain)
    return (result, grad_input, *(u[i] for i in range(3) for u in updates))


def scatter_ring_from(slots, axis):
    own, after, far, before = scatter_ring(slots, axis)
    return [own, before, far, after]


def solution(mesh):
    view = Mesh(mesh.devices.reshape(4, 2, 4, 4), ("x", "core", "z", "y"))
    dp, tensor = ("x", "core"), ("z", "y")
    both = dp + tensor
    tokens = P(both, None)
    weights = (
        P(dp, tensor),
        P(None, both, None),
        P(tensor, dp),
        P(None, dp, tensor),
        P(tensor, dp),
        P(None, both),
    )
    return jax.shard_map(
        local,
        mesh=view,
        in_specs=(tokens, tokens, P(dp, None), *weights * 3),
        out_specs=(tokens, tokens, *weights * 3),
        check_vma=False,
    )
```
